32 devices in a mesh: dp: 8 (over z, x), fsdp: 4 (over y, core).
Axes of the slice: x: 2, y: 2, z: 4, core: 2. Of those that a mesh axis runs over, the one named last changes fastest.
Arguments:
- layer_input: bfloat16 [32, 4096, 512], P(('dp', 'fsdp')), may hold values from -6 to 6
- doc_lengths: int32 [32, 8], P(('dp', 'fsdp')), may hold values from 1 to 2048, 4096 in all within a row
- out_cotangent: bfloat16 [32, 4096, 512], P(('dp', 'fsdp')), may hold values from -6 to 6
- proj_master: float32 [512, 2048], P(('dp', 'fsdp')), as said below
- proj_moment1: float32 [512, 2048], P(('dp', 'fsdp')), may hold values from -48 to 48
- proj_moment2: float32 [512, 2048], P(('dp', 'fsdp')), may hold values from 157.2864 to 1572.864
- up_master: float32 [512, 2048], P(('dp', 'fsdp')), may hold values from -0.25 to 0.25
- up_moment1: float32 [512, 2048], P(('dp', 'fsdp')), may hold values from -64 to 64
- up_moment2: float32 [512, 2048], P(('dp', 'fsdp')), may hold values from 353.8944 to 3538.944
- down_master: float32 [2048, 512], P(('dp', 'fsdp')), may hold values from -0.125 to 0.125
- down_moment1: float32 [2048, 512], P(('dp', 'fsdp')), may hold values from -128 to 128
- down_moment2: float32 [2048, 512], P(('dp', 'fsdp')), may hold values from 1441.792 to 14417.92
- sort_master: float32 [512, 128], P(('dp', 'fsdp')), may hold values from -2 to 2
- sort_moment1: float32 [512, 128], P(('dp', 'fsdp')), may hold values from -24 to 24
- sort_moment2: float32 [512, 128], P(('dp', 'fsdp')), may hold values from 39.3216 to 393.216
- norm_master: float32 [4, 512], P(None, ('dp', 'fsdp')), as said below
- norm_moment1: float32 [4, 512], P(None, ('dp', 'fsdp')), may hold values from -256 to 256
- norm_moment2: float32 [4, 512], P(None, ('dp', 'fsdp')), may hold values from 3932.16 to 39321.6
Outputs:
- layer_output: bfloat16 [32, 4096, 512], P(('dp', 'fsdp'))
- input_grad: float32 [32, 4096, 512], P(('dp', 'fsdp'))
- proj_new: float32 [512, 2048], P(('dp', 'fsdp'))
- proj_first: float32 [512, 2048], P(('dp', 'fsdp'))
- proj_second: float32 [512, 2048], P(('dp', 'fsdp'))
- up_new: float32 [512, 2048], P(('dp', 'fsdp'))
- up_first: float32 [512, 2048], P(('dp', 'fsdp'))
- up_second: float32 [512, 2048], P(('dp', 'fsdp'))
- down_new: float32 [2048, 512], P(('dp', 'fsdp'))
- down_first: float32 [2048, 512], P(('dp', 'fsdp'))
- down_second: float32 [2048, 512], P(('dp', 'fsdp'))
- sort_new: float32 [512, 128], P(('dp', 'fsdp'))
- sort_first: float32 [512, 128], P(('dp', 'fsdp'))
- sort_second: float32 [512, 128], P(('dp', 'fsdp'))
- norm_new: float32 [4, 512], P(None, ('dp', 'fsdp'))
- norm_first: float32 [4, 512], P(None, ('dp', 'fsdp'))
- norm_second: float32 [4, 512], P(None, ('dp', 'fsdp'))
The draws below stay inside these ranges and needn't reach their ends.
Inputs may be any that keep to these rules, and one draw needn't show every extreme that they name: `doc_lengths`: each row's 8 documents fill its 4096 tokens; in every row the longest has exactly 4096 // 2 tokens. `proj_master`: the last 512 columns, the output projection, are about four times as large as the others. `norm_master`: rows 0 and 2 are gains near one, rows 1 and 3 biases.
All inputs are finite; a program needn't handle non-finite values.
Results may differ from the reference program's by a relative error of at most 0.012.
Values may be sent and summed in bfloat16 or wider, within the bound.
A program may use at most 384 MiB of HBM per device.

```python
import math
import jax
import jax.numpy as jnp
import numpy as np
from jax import lax

D = 512
H = 8
HD = 64
FF = 2048
BLOCK = 32
SINK_ITERS = 8
STEP = 10
SEQ = 4096
DOCS = 8
ROWS = 32
TOKENS = 131072
NB = 128


def draw_proj_master(key, part):
    key = jax.random.fold_in(key, 11)
    base = jnp.clip(jax.random.normal(key, (D, 4 * D), jnp.float32), -5.0, 5.0) * D ** (-0.5)
    column = jnp.arange(4 * D)[None, :]
    return jnp.where(column >= 3 * D, 4.0 * base, base).astype(jnp.float32)


def draw_norm_master(key, part):
    key = jax.random.fold_in(key, 23)
    noise = jnp.clip(jax.random.normal(key, (4, D), jnp.float32), -3.0, 3.0)
    row_index = jnp.arange(4)[:, None]
    gains = 1.0 + 0.15 * noise
    biases = 0.3 * noise
    return jnp.where(row_index % 2 == 0, gains, biases).astype(jnp.float32)


def block_scale(own_key, shape, cuts, smallest, largest):
    def one(dim, parts):
        steps = jax.random.uniform(jax.random.fold_in(jax.random.fold_in(own_key, 6), dim), (parts,), jnp.float32, smallest / len(cuts), largest / len(cuts))
        return jnp.repeat(jnp.exp(steps), shape[dim] // parts).reshape((-1,) + (1,) * (len(shape) - dim - 1))

    factor_of = one(*cuts[0])
    for cut in cuts[1:]:
        factor_of = factor_of * one(*cut)
    return factor_of


def length_profile(count, total, most, lean):
    loads = [(1 << 20) // math.isqrt(grade ** lean) + 1 for grade in range(2, count + 1)]
    rest, holding = total - most - (count - 1), [1] * (count - 1)
    while rest > 0:
        movable = [i for i in range(count - 1) if holding[i] < most]
        mass, left = sum([loads[i] for i in movable]), rest
        for i in movable:
            extra = min(most - holding[i], max(1, left * loads[i] // mass), rest)
            holding[i] = holding[i] + extra
            rest = rest - extra
    return np.array([most] + holding)


def ragged_sizes(rng, number_of, total, most, lean):
    if number_of == 2:
        one = jax.random.randint(rng, (), max(1, total - most), min(most, total - 1) + 1)
        return jnp.stack([one, total - one])
    tallies = jnp.asarray(length_profile(number_of, total, most, lean), jnp.int32)
    pairs = (number_of - 1) // 2
    source_of, taker = tallies[1:1 + 2 * pairs:2], tallies[2:2 + 2 * pairs:2]
    margin = jnp.minimum(source_of - 1, most - taker)
    moved = jax.random.randint(jax.random.fold_in(rng, 1), (pairs,), 0, 1 << 20) % (margin + 1)
    tallies = tallies.at[1:1 + 2 * pairs:2].set(source_of - moved).at[2:2 + 2 * pairs:2].set(taker + moved)
    return tallies[jax.random.permutation(jax.random.fold_in(rng, 2), number_of)]


def normal_values(own_key, dims, deviation, most, cuts=(), held_as=jnp.bfloat16):
    level = block_scale(own_key, dims, cuts, -0.22, 0.18) if cuts else 1.0
    result = jax.random.normal(own_key, dims, jnp.float32) * deviation * level
    return jnp.minimum(jnp.maximum(result, -most), most).astype(held_as)


def setup_inputs(seed: int = 0) -> dict:
    seeds = jax.random.split(jax.random.key(seed), 19)
    layer_input = normal_values(seeds[0], (ROWS, SEQ, D), 1.0, 6.0, ((0, 32),))
    doc_lengths = jax.vmap(lambda own: ragged_sizes(own, DOCS, SEQ, SEQ // 2, 2))(jax.random.split(seeds[1], ROWS)).reshape((ROWS, DOCS)).astype(jnp.int32)
    out_cotangent = normal_values(seeds[2], (ROWS, SEQ, D), 1.0, 6.0, ((0, 32),))
    proj_master = draw_proj_master(jax.random.fold_in(seeds[18], 71), 0)
    proj_moment1 = normal_values(seeds[4], (D, 4 * D), (0.022 * TOKENS ** 0.5), 48.0, ((0, 32),), jnp.float32)
    proj_moment2 = jnp.clip(jnp.exp(math.log(1572.864) - 2.3025851 * jax.random.uniform(seeds[5], (D, 4 * D), jnp.float32) ** block_scale(seeds[5], (D, 4 * D), ((0, 32),), -0.2, 0.2)), 157.2864, 1572.864)
    up_master = normal_values(seeds[6], (D, FF), D ** -0.5, 0.25, ((0, 32),), jnp.float32)
    up_moment1 = normal_values(seeds[7], (D, FF), (0.033 * TOKENS ** 0.5), 64.0, ((0, 32),), jnp.float32)
    up_moment2 = jnp.clip(jnp.exp(math.log(3538.944) - 2.3025851 * jax.random.uniform(seeds[8], (D, FF), jnp.float32) ** block_scale(seeds[8], (D, FF), ((0, 32),), -0.2, 0.2)), 353.8944, 3538.944)
    down_master = normal_values(seeds[9], (FF, D), FF ** -0.5, 0.125, ((0, 32),), jnp.float32)
    down_moment1 = normal_values(seeds[10], (FF, D), (0.066 * TOKENS ** 0.5), 128.0, ((0, 32),), jnp.float32)
    down_moment2 = jnp.clip(jnp.exp(math.log(14417.92) - 2.3025851 * jax.random.uniform(seeds[11], (FF, D), jnp.float32) ** block_scale(seeds[11], (FF, D), ((0, 32),), -0.2, 0.2)), 1441.792, 14417.92)
    sort_master = normal_values(seeds[12], (D, NB), (D // 64) ** -0.5, 2.0, ((0, 32),), jnp.float32)
    sort_moment1 = normal_values(seeds[13], (D, NB), (0.011 * TOKENS ** 0.5), 24.0, ((0, 32),), jnp.float32)
    sort_moment2 = jnp.clip(jnp.exp(math.log(393.216) - 2.3025851 * jax.random.uniform(seeds[14], (D, NB), jnp.float32) ** block_scale(seeds[14], (D, NB), ((0, 32),), -0.2, 0.2)), 39.3216, 393.216)
    norm_master = draw_norm_master(jax.random.fold_in(seeds[18], 71), 0)
    norm_moment1 = normal_values(seeds[16], (4, D), (0.11 * TOKENS ** 0.5), 256.0, ((1, 32),), jnp.float32)
    norm_moment2 = jnp.clip(jnp.exp(math.log(39321.6) - 2.3025852 * jax.random.uniform(seeds[17], (4, D), jnp.float32) ** block_scale(seeds[17], (4, D), ((1, 32),), -0.2, 0.2)), 3932.16, 39321.6)
    return dict(layer_input=layer_input, doc_lengths=doc_lengths, out_cotangent=out_cotangent, proj_master=proj_master, proj_moment1=proj_moment1, proj_moment2=proj_moment2, up_master=up_master, up_moment1=up_moment1, up_moment2=up_moment2, down_master=down_master, down_moment1=down_moment1, down_moment2=down_moment2, sort_master=sort_master, sort_moment1=sort_moment1, sort_moment2=sort_moment2, norm_master=norm_master, norm_moment1=norm_moment1, norm_moment2=norm_moment2)


@jax.custom_vjp
def low(v):
    return lax.optimization_barrier(v.astype(jnp.bfloat16)).astype(jnp.float32)

@jax.custom_vjp
def low_back(v):
    return v

def low_keep(v):
    return (low(v), None)

def low_pass(kept, grad):
    return (grad,)

def back_keep(v):
    return (v, None)

def back_low(kept, grad):
    return (low(grad),)
low.defvjp(low_keep, low_pass)
low_back.defvjp(back_keep, back_low)
mask_penalty = 6.0
score_floor = -1000000000.0
norm_eps = 1e-05
beta_first = 0.9
beta_second = 0.95
adam_eps = 1e-08
weight_decay = 0.1
rate_matrix = 0.1
rate_other = 0.5
exact = lax.Precision.HIGHEST

def project(left, right):
    return jnp.einsum('...k,kn->...n', left, right, precision=exact)

def segment_ids(lengths, seq_len):
    ends = jnp.cumsum(lengths, axis=-1).astype(jnp.int32)
    places = jnp.arange(seq_len, dtype=jnp.int32)
    return lax.optimization_barrier(jnp.sum((places[None, :, None] >= ends[:, None, :]).astype(jnp.int32), axis=-1)).astype(jnp.int32)

def layer_norm(values, gain, shift):
    centre = values - lax.optimization_barrier(jnp.mean(values, axis=-1, keepdims=True))
    spread = lax.optimization_barrier(jnp.mean(centre * centre, axis=-1, keepdims=True))
    return centre * lax.rsqrt(spread + norm_eps) * gain + shift

def attention_part(inputs, segments, proj, sort_weight, norms):
    rows, length, width = inputs.shape
    blocks = length // BLOCK
    normed = low(layer_norm(inputs, norms[0], norms[1]))
    projected = low(low_back(project(normed, proj[:, :3 * width])))
    heads = projected.reshape(rows, blocks, BLOCK, 3, H, HD)
    queries = heads[:, :, :, 0]
    keys_all = heads[:, :, :, 1]
    values_all = heads[:, :, :, 2]
    block_means = low(lax.optimization_barrier(jnp.mean(normed.reshape(rows, blocks, BLOCK, width), axis=2)))
    score_logits = low_back(project(block_means, sort_weight))
    firsts = segments[:, ::BLOCK]
    split_blocks = (firsts[:, :, None] != firsts[:, None, :]).astype(jnp.float32)
    score_logits = score_logits - mask_penalty * split_blocks
    for sweep in range(SINK_ITERS):
        score_logits = score_logits - jax.nn.logsumexp(score_logits, axis=2, keepdims=True)
        score_logits = score_logits - jax.nn.logsumexp(score_logits, axis=1, keepdims=True)
    block_permutation = low(jnp.exp(score_logits))
    sorted_keys = low(low_back(jnp.einsum('rij,rjthe->rithe', block_permutation, keys_all, precision=exact)))
    sorted_values = low(low_back(jnp.einsum('rij,rjthe->rithe', block_permutation, values_all, precision=exact)))
    scale = HD ** (-0.5)
    local_scores = jnp.einsum('rnthe,rnshe->rnhts', queries, keys_all, precision=exact) * scale
    block_segs = segments.reshape(rows, blocks, BLOCK)
    same_doc = block_segs[:, :, :, None] == block_segs[:, :, None, :]
    local_scores = jnp.where(same_doc[:, :, None], local_scores, score_floor)
    far_scores = jnp.einsum('rnthe,rnshe->rnhts', queries, sorted_keys, precision=exact) * scale
    scores = low_back(jnp.concatenate([local_scores, far_scores], axis=-1))
    highest = lax.optimization_barrier(jnp.max(scores, axis=-1, keepdims=True))
    exps = jnp.exp(scores - highest)
    probs = low(exps / lax.optimization_barrier(jnp.sum(exps, axis=-1, keepdims=True)))
    context = jnp.einsum('rnhts,rnshe->rnthe', probs[..., :BLOCK], values_all, precision=exact)
    context = context + jnp.einsum('rnhts,rnshe->rnthe', probs[..., BLOCK:], sorted_values, precision=exact)
    context = low(low_back(context.reshape(rows, length, width)))
    return inputs + low_back(project(context, proj[:, 3 * width:]))

def ffn_part(hidden, up_weight, down_weight, norms):
    normed_two = low(layer_norm(hidden, norms[2], norms[3]))
    pre_act = low_back(project(normed_two, up_weight))
    activated = low(jax.nn.gelu(pre_act, approximate=True))
    return hidden + low_back(project(activated, down_weight))

def adamw(master, first, second, grad, rate, decay):
    first_new = beta_first * first + (1.0 - beta_first) * grad
    second_new = beta_second * second + (1.0 - beta_second) * grad * grad
    first_hat = first_new / (1.0 - beta_first ** STEP)
    second_hat = second_new / (1.0 - beta_second ** STEP)
    master_new = master - rate * (first_hat / (jnp.sqrt(second_hat) + adam_eps) + decay * master)
    return (master_new, first_new, second_new)

def reference(layer_input, doc_lengths, out_cotangent, proj_master, proj_moment1, proj_moment2, up_master, up_moment1, up_moment2, down_master, down_moment1, down_moment2, sort_master, sort_moment1, sort_moment2, norm_master, norm_moment1, norm_moment2):
    masters = (proj_master, up_master, down_master, sort_master, norm_master)
    weights = tuple((master.astype(jnp.bfloat16).astype(jnp.float32) for master in masters))
    group = math.gcd(ROWS, max(1, 4096 // SEQ))
    count = ROWS // group
    inputs = layer_input.reshape(count, group, SEQ, D)
    lengths = doc_lengths.reshape(count, group, DOCS)
    cotangent = out_cotangent.reshape(count, group, SEQ, D)

    def one_group(totals, pieces):
        piece_in, piece_len, piece_cot = pieces
        segments = segment_ids(piece_len, SEQ)

        def whole(inputs_f, proj, up_weight, down_weight, sort_weight, norms):
            hidden = attention_part(inputs_f, segments, proj, sort_weight, norms)
            return ffn_part(hidden, up_weight, down_weight, norms)
        output, pullback = jax.vjp(whole, piece_in.astype(jnp.float32), *weights)
        grads = pullback(piece_cot.astype(jnp.float32))
        totals = tuple((total + grad for total, grad in zip(totals, grads[1:])))
        return (totals, (output.astype(jnp.bfloat16), grads[0]))
    zeros = tuple((jnp.zeros_like(weight) for weight in weights))
    totals, (outputs, input_grads) = lax.scan(one_group, zeros, (inputs, lengths, cotangent))
    proj_new, proj_first, proj_second = adamw(proj_master, proj_moment1, proj_moment2, totals[0], rate_matrix, weight_decay)
    up_new, up_first, up_second = adamw(up_master, up_moment1, up_moment2, totals[1], rate_matrix, weight_decay)
    down_new, down_first, down_second = adamw(down_master, down_moment1, down_moment2, totals[2], rate_matrix, weight_decay)
    sort_new, sort_first, sort_second = adamw(sort_master, sort_moment1, sort_moment2, totals[3], rate_other, weight_decay)
    norm_new, norm_first, norm_second = adamw(norm_master, norm_moment1, norm_moment2, totals[4], rate_other, 0.0)
    return (outputs.reshape(ROWS, SEQ, D), input_grads.reshape(ROWS, SEQ, D), proj_new, proj_first, proj_second, up_new, up_first, up_second, down_new, down_first, down_second, sort_new, sort_first, sort_second, norm_new, norm_first, norm_second)
```

```python
import functools
import jax
import jax.numpy as jnp
from jax import lax
from jax.experimental import pallas as pl
from jax.experimental.pallas import tpu as pltpu
from jax.sharding import PartitionSpec as P

HD = 64
BLOCK = 32
SINK_ITERS = 8
STEP = 10
TILE = 512
LANES = 128

mask_penalty = 6.0
score_floor = -1000000000.0
norm_eps = 1e-05
beta_first = 0.9
beta_second = 0.95
adam_eps = 1e-08
weight_decay = 0.1
rate_matrix = 0.1
rate_other = 0.5

bf16 = jnp.bfloat16
f32 = jnp.float32
VMEM_LIMIT = 62 * 2**20


def dot(left, right):
    return lax.dot_general(left, right, (((1,), (0,)), ((), ())), preferred_element_type=f32)


def dot_nt(left, right):
    return lax.dot_general(left, right, (((1,), (1,)), ((), ())), preferred_element_type=f32)


def dot_tn(left, right):
    return lax.dot_general(left, right, (((0,), (0,)), ((), ())), preferred_element_type=f32)


def doc_ends(lengths_ref):
    total = lengths_ref[0, 0]
    ends = [total]
    for k in range(1, lengths_ref.shape[1]):
        total = total + lengths_ref[0, k]
        ends.append(total)
    return ends


def segments_of(places, ends):
    count = jnp.zeros(places.shape, jnp.int32)
    for end in ends:
        count = count + (places >= end).astype(jnp.int32)
    return count


def center_scale(values):
    centre = values - jnp.mean(values, axis=-1, keepdims=True)
    spread = jnp.mean(centre * centre, axis=-1, keepdims=True)
    inverse = lax.rsqrt(spread + norm_eps)
    return centre * inverse, inverse


def log_sum_exp(logits, axis):
    top = jnp.max(logits, axis=axis, keepdims=True)
    return top + jnp.log(jnp.sum(jnp.exp(logits - top), axis=axis, keepdims=True))


def front_kernel(
    lengths_ref, norms_ref, x_ref, proj_ref, sort_ref,
    normed_hbm, qkv_hbm, skv_hbm, tkv_hbm, means_ref, states_ref,
    normed_s, stage, qkv_buf, low_buf, flip_buf, copy_sem, qkv_sem, low_sem, flip_sem,
):
    seq, width = x_ref.shape
    tiles = seq // TILE
    blocks = seq // BLOCK
    per_tile = TILE // BLOCK
    chunks = 2 * width // LANES
    ends = doc_ends(lengths_ref)
    gain = norms_ref[0:1, :].astype(f32)
    shift = norms_ref[1:2, :].astype(f32)

    def norm_step(k, carry):
        rows = pl.ds(pl.multiple_of(k * TILE, TILE), TILE)
        xhat, unused = center_scale(x_ref[rows, :].astype(f32))
        normed = (xhat * gain + shift).astype(bf16)
        normed_s[rows, :] = normed
        sums = jnp.sum(normed.astype(f32).reshape(per_tile, BLOCK, width), axis=1)
        means_ref[pl.ds(pl.multiple_of(k * per_tile, per_tile), per_tile), :] = (
            sums * (1.0 / BLOCK)
        ).astype(bf16)
        return carry

    lax.fori_loop(0, tiles, norm_step, 0)
    normed_copy = pltpu.make_async_copy(normed_s, normed_hbm, copy_sem)
    normed_copy.start()

    logits = dot(means_ref[...], sort_ref[...])
    first_i = segments_of(lax.broadcasted_iota(jnp.int32, (blocks, blocks), 0) * BLOCK, ends)
    first_j = segments_of(lax.broadcasted_iota(jnp.int32, (blocks, blocks), 1) * BLOCK, ends)
    logits = jnp.where(first_i != first_j, logits - mask_penalty, logits)

    def qkv_copy(k, slot):
        rows = pl.ds(pl.multiple_of(k * TILE, TILE), TILE)
        return pltpu.make_async_copy(qkv_buf.at[slot], qkv_hbm.at[rows, :], qkv_sem.at[slot])

    def project_step(k, logits):
        rows = pl.ds(pl.multiple_of(k * TILE, TILE), TILE)
        slot = lax.rem(k, 2)

        @pl.when(k >= 2)
        def _():
            qkv_copy(k - 2, slot).wait()

        logits = logits - log_sum_exp(logits, 1)
        states_ref[2 * k] = jnp.exp(logits)
        logits = logits - log_sum_exp(logits, 0)
        states_ref[2 * k + 1] = jnp.exp(logits)
        normed = normed_s[rows, :]
        qkv_buf[slot, :, :width] = dot(normed, proj_ref[:, :width]).astype(bf16)
        for half in range(2):
            columns = slice((1 + half) * width, (2 + half) * width)
            product = dot(normed, proj_ref[:, columns]).astype(bf16)
            qkv_buf[slot, :, columns] = product
            wide = product.astype(f32)
            for c in range(width // LANES):
                stage[half * (width // LANES) + c, rows, :] = wide[:, c * LANES : (c + 1) * LANES]
        qkv_copy(k, slot).start()
        return logits

    assert tiles == SINK_ITERS
    lax.fori_loop(0, tiles, project_step, logits)
    permute = states_ref[2 * SINK_ITERS - 1].astype(bf16)

    def flip_copy(t, slot):
        return pltpu.make_async_copy(flip_buf.at[slot], tkv_hbm.at[t], flip_sem.at[slot])

    def sort_step(i, carry):
        group = flip_buf.shape[0]

        @pl.when(i >= 1)
        def _():
            for u in range(group):
                flip_copy((i - 1) * group + u, u).wait()

        loaded = []
        for u in range(group):
            t = i * group + u
            loaded.append(
                jnp.concatenate(
                    [stage[c, pl.ds(t, blocks, stride=BLOCK), :] for c in range(chunks)], axis=1
                ).astype(bf16)
            )
        for u in range(group):
            t = i * group + u
            flip_buf[u] = loaded[u].T
            flip_copy(t, u).start()
            moved = dot(permute, loaded[u])
            for c in range(chunks):
                stage[c, pl.ds(t, blocks, stride=BLOCK), :] = moved[:, c * LANES : (c + 1) * LANES]
        return carry

    group = flip_buf.shape[0]
    lax.fori_loop(0, BLOCK // group, sort_step, 0)

    def low_copy(k, slot):
        rows = pl.ds(pl.multiple_of(k * TILE, TILE), TILE)
        return pltpu.make_async_copy(low_buf.at[slot], skv_hbm.at[rows, :], low_sem.at[slot])

    def low_step(k, carry):
        rows = pl.ds(pl.multiple_of(k * TILE, TILE), TILE)
        slot = lax.rem(k, 2)

        @pl.when(k >= 2)
        def _():
            low_copy(k - 2, slot).wait()

        for c in range(chunks):
            low_buf[slot, :, c * LANES : (c + 1) * LANES] = stage[c, rows, :].astype(bf16)
        low_copy(k, slot).start()
        return carry

    lax.fori_loop(0, tiles, low_step, 0)
    for u in range(group):
        flip_copy(BLOCK - group + u, u).wait()
    for k in (tiles - 2, tiles - 1):
        qkv_copy(k, k % 2).wait()
        low_copy(k, k % 2).wait()
    normed_copy.wait()


def front(lengths, norms, x, proj, sort):
    seq, width = x.shape
    blocks = seq // BLOCK
    hbm = pl.BlockSpec(memory_space=pl.ANY)
    vmem = pl.BlockSpec(memory_space=pltpu.VMEM)
    return pl.pallas_call(
        front_kernel,
        out_shape=(
            jax.ShapeDtypeStruct((seq, width), bf16),
            jax.ShapeDtypeStruct((seq, 3 * width), bf16),
            jax.ShapeDtypeStruct((seq, 2 * width), bf16),
            jax.ShapeDtypeStruct((BLOCK, 2 * width, blocks), bf16),
            jax.ShapeDtypeStruct((blocks, width), bf16),
            jax.ShapeDtypeStruct((2 * SINK_ITERS, blocks, blocks), f32),
        ),
        in_specs=[pl.BlockSpec(memory_space=pltpu.SMEM), vmem, vmem, vmem, vmem],
        out_specs=[hbm, hbm, hbm, hbm, vmem, vmem],
        scratch_shapes=[
            pltpu.VMEM((seq, width), bf16),
            pltpu.VMEM((2 * width // LANES, seq, LANES), f32),
            pltpu.VMEM((2, TILE, 3 * width), bf16),
            pltpu.VMEM((2, TILE, 2 * width), bf16),
            pltpu.VMEM((2, 2 * width, blocks), bf16),
            pltpu.SemaphoreType.DMA,
            pltpu.SemaphoreType.DMA((2,)),
            pltpu.SemaphoreType.DMA((2,)),
            pltpu.SemaphoreType.DMA((2,)),
        ],
        compiler_params=pltpu.CompilerParams(vmem_limit_bytes=VMEM_LIMIT),
        name="front",
    )(lengths, norms, x, proj, sort)


def layer_norm_back(grad, gain, xhat, inverse):
    scaled = grad * gain
    mean_one = jnp.mean(scaled, axis=-1, keepdims=True)
    mean_two = jnp.mean(scaled * xhat, axis=-1, keepdims=True)
    return (scaled - mean_one - xhat * mean_two) * inverse


def middle_kernel(
    lengths_ref, norms_ref, x_ref, cot_ref, qkv_ref, skv_ref, out_proj_ref, up_ref, down_ref,
    y_ref, hidden_grad_ref, gq_ref, gkv_ref, gskv_ref, gup_ref, gdown_ref, gout_ref, gnorm_ref,
    gup, gdown, gout, probs_s, context_s, gcontext_s,
):
    step = pl.program_id(0)
    tile, width = x_ref.shape
    hidden_units = up_ref.shape[1]
    pairs = tile // (2 * BLOCK)
    head_pairs = width // LANES
    scale = HD ** (-0.5)
    ends = doc_ends(lengths_ref)

    @pl.when(step == 0)
    def _():
        gup[...] = jnp.zeros_like(gup)
        gdown[...] = jnp.zeros_like(gdown)
        gout[...] = jnp.zeros_like(gout)
        gnorm_ref[...] = jnp.zeros_like(gnorm_ref)

    lane = lax.broadcasted_iota(jnp.int32, (1, LANES), 1)
    low_head = lane < HD
    low_block = lax.rem(lane, 2 * BLOCK) < BLOCK
    zero = jnp.zeros((), bf16)

    def two_heads(part):
        return jnp.concatenate(
            [jnp.where(low_head, part, zero), jnp.where(low_head, zero, part)], axis=0
        )

    def two_blocks(part):
        return jnp.concatenate(
            [jnp.where(low_block, part, zero), jnp.where(low_block, zero, part)], axis=0
        )

    def stack_keys(own, far):
        return jnp.concatenate(
            [own[:BLOCK], far[:BLOCK], own[BLOCK:], far[BLOCK:]], axis=0
        )

    def pick_block(full):
        return jnp.where(low_block, full[: 2 * BLOCK], full[2 * BLOCK :])

    def pick_head(full):
        return jnp.where(low_head, full[: 2 * BLOCK], full[2 * BLOCK :])

    def attend(p, carry):
        rows = pl.ds(pl.multiple_of(p * 2 * BLOCK, 2 * BLOCK), 2 * BLOCK)
        base = step * tile + p * 2 * BLOCK
        query_seg = segments_of(base + lax.rem(lane, 2 * BLOCK), ends)
        key_place = (
            base
            + jnp.where(low_block, 0, BLOCK)
            + lax.broadcasted_iota(jnp.int32, (BLOCK, LANES), 0)
        )
        same = segments_of(key_place, ends) == query_seg
        for hp in range(head_pairs):
            cols = slice(hp * LANES, (hp + 1) * LANES)
            key_cols = slice(width + hp * LANES, width + (hp + 1) * LANES)
            value_cols = slice(2 * width + hp * LANES, 2 * width + (hp + 1) * LANES)
            queries = two_heads(qkv_ref[rows, cols])
            keys = stack_keys(qkv_ref[rows, key_cols], skv_ref[rows, cols])
            values = stack_keys(qkv_ref[rows, value_cols], skv_ref[rows, key_cols])
            scores = pick_block(dot(keys, queries.T)) * scale
            scores = jnp.concatenate(
                [jnp.where(same, scores[:BLOCK], score_floor), scores[BLOCK:]], axis=0
            )
            exps = jnp.exp(scores - jnp.max(scores, axis=0, keepdims=True))
            probs = (exps / jnp.sum(exps, axis=0, keepdims=True)).astype(bf16)
            probs_s[p * head_pairs + hp] = probs
            context_s[rows, cols] = pick_head(dot_tn(two_blocks(probs), values)).astype(bf16)
        return carry

    lax.fori_loop(0, pairs, attend, 0)

    inputs = x_ref[...].astype(f32)
    context = context_s[...]
    hidden = inputs + dot(context, out_proj_ref[...])
    xhat_two, inverse_two = center_scale(hidden)
    gain_two = norms_ref[2:3, :].astype(f32)
    normed_two = (xhat_two * gain_two + norms_ref[3:4, :].astype(f32)).astype(bf16)
    normed_two_t = normed_two.T
    cot = cot_ref[...]
    total_out = hidden
    grad_normed_two = None
    root = 0.7978845608028654
    for c in range(hidden_units // TILE):
        cols = slice(c * TILE, (c + 1) * TILE)
        pre = dot(normed_two, up_ref[:, cols])
        grad_act = dot_nt(cot, down_ref[cols, :])
        square = pre * pre
        half_tanh = 0.5 + 0.5 * jnp.tanh(pre * (root + (root * 0.044715) * square))
        act = pre * half_tanh
        slope = half_tanh + act * (1.0 - half_tanh) * (
            2.0 * root + (6.0 * root * 0.044715) * square
        )
        act = act.astype(bf16)
        grad_pre = (grad_act * slope).astype(bf16)
        total_out = total_out + dot(act, down_ref[cols, :])
        back = dot_nt(grad_pre, up_ref[:, cols])
        grad_normed_two = back if grad_normed_two is None else grad_normed_two + back
        gup[:, cols] += dot(normed_two_t, grad_pre)
        gdown[cols, :] += dot_tn(act, cot)
    y_ref[...] = total_out.astype(bf16)
    gnorm_ref[0:1, :] += jnp.sum(grad_normed_two * xhat_two, axis=0, keepdims=True)
    gnorm_ref[1:2, :] += jnp.sum(grad_normed_two, axis=0, keepdims=True)
    hidden_grad = cot.astype(f32) + layer_norm_back(
        grad_normed_two, gain_two, xhat_two, inverse_two
    )
    hidden_grad_ref[...] = hidden_grad
    grad_attn = hidden_grad.astype(bf16)
    gout[...] += dot_tn(context, grad_attn)
    gcontext_s[...] = dot_nt(grad_attn, out_proj_ref[...]).astype(bf16)

    def attend_back(p, carry):
        rows = pl.ds(pl.multiple_of(p * 2 * BLOCK, 2 * BLOCK), 2 * BLOCK)
        for hp in range(head_pairs):
            cols = slice(hp * LANES, (hp + 1) * LANES)
            key_cols = slice(width + hp * LANES, width + (hp + 1) * LANES)
            value_cols = slice(2 * width + hp * LANES, 2 * width + (hp + 1) * LANES)
            queries = two_heads(qkv_ref[rows, cols])
            keys = stack_keys(qkv_ref[rows, key_cols], skv_ref[rows, cols])
            values = stack_keys(qkv_ref[rows, value_cols], skv_ref[rows, key_cols])
            gcontext = two_heads(gcontext_s[rows, cols])
            probs = probs_s[p * head_pairs + hp]
            wide = probs.astype(f32)
            grad_probs = pick_block(dot(values, gcontext.T))
            weighted = wide * grad_probs
            grad_scores = weighted - wide * jnp.sum(weighted, axis=0, keepdims=True)
            grad_scores = two_blocks((grad_scores * scale).astype(bf16))
            gq_ref[rows, cols] = pick_head(dot_tn(grad_scores, keys)).astype(bf16)
            gkeys = dot(grad_scores, queries).astype(bf16)
            gvalues = dot(two_blocks(probs), gcontext).astype(bf16)
            for grads, where in ((gkeys, cols), (gvalues, key_cols)):
                gkv_ref[rows, where] = jnp.concatenate(
                    [grads[:BLOCK], grads[2 * BLOCK : 3 * BLOCK]], axis=0
                )
                gskv_ref[rows, where] = jnp.concatenate(
                    [grads[BLOCK : 2 * BLOCK], grads[3 * BLOCK :]], axis=0
                )
        return carry

    lax.fori_loop(0, pairs, attend_back, 0)

    @pl.when(step == pl.num_programs(0) - 1)
    def _():
        gup_ref[...] = gup[...].astype(bf16)
        gdown_ref[...] = gdown[...].astype(bf16)
        gout_ref[...] = gout[...].astype(bf16)


def middle(lengths, norms, x, cot, qkv, skv, proj, up, down):
    seq, width = x.shape
    hidden_units = up.shape[1]
    tiles = seq // TILE

    def rows(columns):
        return pl.BlockSpec((TILE, columns), lambda i: (i, 0))

    def fixed(shape, index=(0, 0)):
        return pl.BlockSpec(shape, lambda i: index, pipeline_mode=pl.Buffered(1))

    return pl.pallas_call(
        middle_kernel,
        grid=(tiles,),
        out_shape=(
            jax.ShapeDtypeStruct((seq, width), bf16),
            jax.ShapeDtypeStruct((seq, width), f32),
            jax.ShapeDtypeStruct((seq, width), bf16),
            jax.ShapeDtypeStruct((seq, 2 * width), bf16),
            jax.ShapeDtypeStruct((seq, 2 * width), bf16),
            jax.ShapeDtypeStruct((width, hidden_units), bf16),
            jax.ShapeDtypeStruct((hidden_units, width), bf16),
            jax.ShapeDtypeStruct((width, width), bf16),
            jax.ShapeDtypeStruct((2, width), f32),
        ),
        in_specs=[
            pl.BlockSpec(memory_space=pltpu.SMEM),
            fixed(norms.shape),
            rows(width),
            rows(width),
            rows(3 * width),
            rows(2 * width),
            fixed((width, width), (0, 3)),
            fixed(up.shape),
            fixed(down.shape),
        ],
        out_specs=[
            rows(width),
            rows(width),
            rows(width),
            rows(2 * width),
            rows(2 * width),
            fixed((width, hidden_units)),
            fixed((hidden_units, width)),
            fixed((width, width)),
            fixed((2, width)),
        ],
        scratch_shapes=[
            pltpu.VMEM((width, hidden_units), f32),
            pltpu.VMEM((hidden_units, width), f32),
            pltpu.VMEM((width, width), f32),
            pltpu.VMEM((TILE // (2 * BLOCK) * (width // LANES), 2 * BLOCK, LANES), bf16),
            pltpu.VMEM((TILE, width), bf16),
            pltpu.VMEM((TILE, width), bf16),
        ],
        compiler_params=pltpu.CompilerParams(vmem_limit_bytes=VMEM_LIMIT),
        name="middle",
    )(lengths, norms, x, cot, qkv, skv, proj, up, down)


def back_kernel(
    norms_ref, gskv_hbm, tkv_hbm, states_ref, means_ref, proj_ref, sort_ref,
    x_hbm, normed_hbm, hidden_grad_hbm, gq_hbm, gkv_hbm,
    gx_hbm, gproj_ref, gsort_ref, gnorm_ref,
    stage, low_buf, flip_buf, gproj, gperm, gmeans, low_sem, flip_sem,
):
    seq, width = x_hbm.shape
    tiles = seq // TILE
    blocks = seq // BLOCK
    chunks = 2 * width // LANES
    per_tile = TILE // BLOCK

    def low_copy(k, slot):
        rows = pl.ds(pl.multiple_of(k * TILE, TILE), TILE)
        return pltpu.make_async_copy(gskv_hbm.at[rows, :], low_buf.at[slot], low_sem.at[slot])

    group = flip_buf.shape[0] // 2

    def flip_copy(t, slot):
        return pltpu.make_async_copy(tkv_hbm.at[t], flip_buf.at[slot], flip_sem.at[slot])

    low_copy(0, 0).start()
    low_copy(1, 1).start()
    for u in range(group):
        flip_copy(u, u).start()

    def load_step(k, carry):
        rows = pl.ds(pl.multiple_of(k * TILE, TILE), TILE)
        slot = lax.rem(k, 2)
        low_copy(k, slot).wait()
        for c in range(chunks):
            stage[c, rows, :] = low_buf[slot, :, c * LANES : (c + 1) * LANES].astype(f32)

        @pl.when(k + 2 < tiles)
        def _():
            low_copy(k + 2, slot).start()

        return carry

    lax.fori_loop(0, tiles, load_step, 0)

    final = states_ref[2 * SINK_ITERS - 1]
    permute_t = final.astype(bf16).T
    gperm[...] = jnp.zeros_like(gperm)

    def sort_step(i, carry):
        side = lax.rem(i, 2) * group

        @pl.when(i + 1 < BLOCK // group)
        def _():
            for u in range(group):
                flip_copy((i + 1) * group + u, group - side + u).start()

        for u in range(group):
            flip_copy(i * group + u, side + u).wait()
        loaded = []
        for u in range(group):
            t = i * group + u
            loaded.append(
                jnp.concatenate(
                    [stage[c, pl.ds(t, blocks, stride=BLOCK), :] for c in range(chunks)], axis=1
                ).astype(bf16)
            )
        total = gperm[...]
        for u in range(group):
            t = i * group + u
            total = total + dot(loaded[u], flip_buf[side + u])
            moved = dot(permute_t, loaded[u])
            for c in range(chunks):
                stage[c, pl.ds(t, blocks, stride=BLOCK), :] = moved[:, c * LANES : (c + 1) * LANES]
        gperm[...] = total
        return carry

    lax.fori_loop(0, BLOCK // group, sort_step, 0)

    grad = gperm[...] * final
    for sweep in reversed(range(SINK_ITERS)):
        grad = grad - states_ref[2 * sweep + 1] * jnp.sum(grad, axis=0, keepdims=True)
        grad = grad - states_ref[2 * sweep] * jnp.sum(grad, axis=1, keepdims=True)
    grad = grad.astype(bf16)
    gsort_ref[...] = dot_tn(means_ref[...], grad).astype(gsort_ref.dtype)
    gmeans[...] = dot_nt(grad, sort_ref[...]) * (1.0 / BLOCK)
    gproj[...] = jnp.zeros_like(gproj)
    gnorm_ref[...] = jnp.zeros_like(gnorm_ref)
    gain = norms_ref[0:1, :].astype(f32)

    def tile_step(x_ref, normed_ref, hidden_grad_ref, gq_ref, gkv_ref, gx_ref):
        k = pl.program_id(0)
        rows = pl.ds(pl.multiple_of(k * TILE, TILE), TILE)
        far = jnp.concatenate([stage[c, rows, :] for c in range(chunks)], axis=1)
        gkv = (gkv_ref[...].astype(f32) + far).astype(bf16)
        gq = gq_ref[...]
        normed = normed_ref[...]
        gproj[:, :width] += dot_tn(normed, gq)
        gproj[:, width:] += dot_tn(normed, gkv)
        grad_normed = dot_nt(gq, proj_ref[:, :width]) + dot_nt(gkv, proj_ref[:, width : 3 * width])
        means = gmeans[pl.ds(pl.multiple_of(k * per_tile, per_tile), per_tile), :]
        grad_normed = grad_normed + jnp.broadcast_to(
            means[:, None, :], (per_tile, BLOCK, width)
        ).reshape(TILE, width)
        xhat, inverse = center_scale(x_ref[...].astype(f32))
        gnorm_ref[0:1, :] += jnp.sum(grad_normed * xhat, axis=0, keepdims=True)
        gnorm_ref[1:2, :] += jnp.sum(grad_normed, axis=0, keepdims=True)
        gx_ref[...] = hidden_grad_ref[...] + layer_norm_back(grad_normed, gain, xhat, inverse)

    def rows_of(columns):
        return pl.BlockSpec((TILE, columns), lambda i: (i, 0))

    pltpu.emit_pipeline(
        tile_step,
        grid=(tiles,),
        in_specs=[rows_of(width)] * 4 + [rows_of(2 * width)],
        out_specs=[rows_of(width)],
    )(x_hbm, normed_hbm, hidden_grad_hbm, gq_hbm, gkv_hbm, gx_hbm)
    gproj_ref[...] = gproj[...].astype(gproj_ref.dtype)


def back(norms, gskv, tkv, states, means, proj, sort, x, normed, hidden_grad, gq, gkv):
    seq, width = x.shape
    blocks = seq // BLOCK
    hbm = pl.BlockSpec(memory_space=pl.ANY)
    vmem = pl.BlockSpec(memory_space=pltpu.VMEM)
    return pl.pallas_call(
        back_kernel,
        out_shape=(
            jax.ShapeDtypeStruct((seq, width), f32),
            jax.ShapeDtypeStruct((width, 3 * width), bf16),
            jax.ShapeDtypeStruct((width, blocks), bf16),
            jax.ShapeDtypeStruct((2, width), f32),
        ),
        in_specs=[vmem, hbm, hbm, vmem, vmem, vmem, vmem, hbm, hbm, hbm, hbm, hbm],
        out_specs=[hbm, vmem, vmem, vmem],
        scratch_shapes=[
            pltpu.VMEM((2 * width // LANES, seq, LANES), f32),
            pltpu.VMEM((2, TILE, 2 * width), bf16),
            pltpu.VMEM((4, 2 * width, blocks), bf16),
            pltpu.VMEM((width, 3 * width), f32),
            pltpu.VMEM((blocks, blocks), f32),
            pltpu.VMEM((blocks, width), f32),
            pltpu.SemaphoreType.DMA((2,)),
            pltpu.SemaphoreType.DMA((4,)),
        ],
        compiler_params=pltpu.CompilerParams(vmem_limit_bytes=VMEM_LIMIT),
        name="back",
    )(norms, gskv, tkv, states, means, proj, sort, x, normed, hidden_grad, gq, gkv)


MESH_ID = pl.DeviceIdType.MESH
AXES = ("dp", "fsdp")
SPLIT = (4, 2, 2, 2)
COPIES = 8


def coordinates():
    dp, fsdp = lax.axis_index("dp"), lax.axis_index("fsdp")
    return dp // 2, dp % 2, fsdp // 2, fsdp % 2


def device_of(z, x, y, c):
    return (z * 2 + x, y * 2 + c)


def z_others(z):
    return (z + 1 - 2 * (z % 2), (z + 2) % 4, 3 - z)


def neighbours():
    z, x, y, c = coordinates()
    others = [device_of(one, x, y, c) for one in z_others(z)]
    return others + [
        device_of(z, 1 - x, y, c), device_of(z, x, 1 - y, c), device_of(z, x, y, 1 - c)
    ]


def meet_neighbours():
    barrier = pltpu.get_barrier_semaphore()
    peers = neighbours()
    for peer in peers:
        pl.semaphore_signal(barrier, inc=1, device_id=peer, device_id_type=MESH_ID)
    pl.semaphore_wait(barrier, len(peers))


def halves(shape):
    if shape[-1] > LANES:
        middle_column = shape[-1] // 2
        return (
            (slice(None), pl.ds(0, middle_column)),
            (slice(None), pl.ds(middle_column, middle_column)),
        )
    middle_row = shape[-2] // 2
    return (
        (pl.ds(0, middle_row), slice(None)),
        (pl.ds(middle_row, middle_row), slice(None)),
    )


def remote(source, target, sems, index, device):
    send, recv = sems
    return pltpu.make_async_remote_copy(
        src_ref=source, dst_ref=target, send_sem=send.at[index], recv_sem=recv.at[index],
        device_id=device, device_id_type=MESH_ID,
    )


def gather_stages(full, sems, base):
    z, x, y, c = coordinates()
    first, second = halves(full.shape)
    every = slice(None)

    def same(index, place, device):
        part = full.at[place]
        return remote(part, part, sems, base + index, device)

    def stage_z():
        return [
            same(k, (z, x, y, c), device_of(one, x, y, c)) for k, one in enumerate(z_others(z))
        ]

    def stage_one():
        return [
            same(3, (every, x, y, c) + first, device_of(z, 1 - x, y, c)),
            same(4, (every, x, y, c) + second, device_of(z, x, 1 - y, c)),
        ]

    def stage_two():
        return [
            same(5, (every, every, y, c) + first, device_of(z, x, 1 - y, c)),
            same(6, (every, x, every, c) + second, device_of(z, 1 - x, y, c)),
        ]

    def stage_core():
        return [same(7, (every, every, every, c), device_of(z, x, y, 1 - c))]

    return [stage_z, stage_one, stage_two, stage_core]


def start_all(copies):
    for copy in copies:
        copy.start()


def wait_all(copies):
    for copy in copies:
        copy.wait()


def one_hot(shape, row_of, column_of):
    rows = lax.broadcasted_iota(jnp.int32, shape, 0)
    columns = lax.broadcasted_iota(jnp.int32, shape, 1)
    return row_of(rows, columns) == column_of(rows, columns)


def norm_place():
    z, x, y, c = coordinates()
    device = (z * 2 + x) * 4 + y * 2 + c
    return device // 8, device % 8


def gather_kernel(proj_ref, up_ref, down_ref, sort_ref, norm_ref, proj, up, down, small, send, recv):
    z, x, y, c = coordinates()
    mine = (z, x, y, c)
    proj[mine] = proj_ref[...].astype(bf16)
    up[mine] = up_ref[...].astype(bf16)
    down[mine] = down_ref[...].astype(bf16)
    quarter, eighth = norm_place()
    own = norm_ref.shape[1]
    spread = one_hot((own, LANES), lambda r, l: r + eighth * own, lambda r, l: l)
    lanes = dot(norm_ref[...].astype(bf16), spread.astype(bf16)).astype(bf16)
    lift = one_hot((16, 4), lambda r, l: r, lambda r, l: l * 4 + quarter)
    tile = dot(lift.astype(bf16), lanes).astype(bf16)
    small[mine] = jnp.concatenate([sort_ref[...].astype(bf16), tile], axis=0)
    meet_neighbours()
    fulls = (proj, up, down, small)
    plans = [gather_stages(full, (send, recv), COPIES * b) for b, full in enumerate(fulls)]
    for step in range(4):
        copies = [copy for plan in plans for copy in plan[step]()]
        start_all(copies)
        wait_all(copies)


def gather(proj, up, down, sort, norm):
    shapes = (proj.shape, up.shape, down.shape, (32, LANES))
    vmem = pl.BlockSpec(memory_space=pltpu.VMEM)
    proj, up, down, small = pl.pallas_call(
        gather_kernel,
        out_shape=tuple(jax.ShapeDtypeStruct(SPLIT + shape, bf16) for shape in shapes),
        in_specs=[vmem] * 5,
        out_specs=[vmem] * 4,
        scratch_shapes=[pltpu.SemaphoreType.DMA((4 * COPIES,))] * 2,
        compiler_params=pltpu.CompilerParams(
            collective_id=0, has_side_effects=True, vmem_limit_bytes=VMEM_LIMIT
        ),
        name="gather",
    )(proj, up, down, sort, norm)
    small = small.reshape(32, 32, LANES)
    sort = small[:, :16].reshape(-1, LANES)
    norms = jnp.sum(small[:, 16:].astype(f32), axis=0).astype(bf16).reshape(4, -1)

    def flat(array):
        return array.reshape(-1, array.shape[-1])

    return flat(proj), flat(up), flat(down), sort, norms


def add_low(*parts):
    total = parts[0].astype(f32)
    for part in parts[1:]:
        total = total + part.astype(f32)
    return total


class Reduce:
    def __init__(self, part, total, got_c, sum_c, got_a, got_b, sum_a, sum_b, got_z, sems, base):
        self.part, self.total, self.got_c, self.sum_c = part, total, got_c, sum_c
        self.got_a, self.got_b, self.sum_a, self.sum_b = got_a, got_b, sum_a, sum_b
        self.got_z, self.sems, self.base = got_z, sems, base
        self.first, self.second = halves(part.shape)

    def copies(self, step):
        z, x, y, c = coordinates()
        every = slice(None)
        to_x, to_y = device_of(z, 1 - x, y, c), device_of(z, x, 1 - y, c)

        def one(source, target, index, device):
            return remote(source, target, self.sems, self.base + index, device)

        if step == 0:
            away = self.part.at[every, every, every, 1 - c]
            return [one(away, self.got_c, 0, device_of(z, x, y, 1 - c))]
        if step == 1:
            away_a = self.sum_c.at[(every, every, 1 - y) + self.first]
            away_b = self.sum_c.at[(every, 1 - x, every) + self.second]
            return [one(away_a, self.got_a, 1, to_y), one(away_b, self.got_b, 2, to_x)]
        if step == 2:
            away_a, away_b = self.sum_a.at[every, 1 - x], self.sum_b.at[every, 1 - y]
            return [
                one(away_a, self.got_c.at[(every, 0, 0) + self.first], 3, to_x),
                one(away_b, self.got_c.at[(every, 0, 0) + self.second], 4, to_y),
            ]
        return [
            one(self.sum_c.at[other, 0, 0], self.got_z.at[k], 5 + k, device_of(other, x, y, c))
            for k, other in enumerate(z_others(z))
        ]

    def add(self, step):
        z, x, y, c = coordinates()
        if step == 3:
            self.total[...] = add_low(self.sum_c[z, 0, 0], *[self.got_z[k] for k in range(3)])
            return

        def line(i, carry):
            if step == 0:
                for j in range(2):
                    for k in range(2):
                        self.sum_c[i, j, k] = add_low(
                            self.part[i, j, k, c], self.got_c[i, j, k]
                        ).astype(bf16)
            elif step == 1:
                for j in range(2):
                    self.sum_a[i, j] = add_low(
                        self.sum_c[(i, j, y) + self.first], self.got_a[i, j]
                    ).astype(bf16)
                    self.sum_b[i, j] = add_low(
                        self.sum_c[(i, x, j) + self.second], self.got_b[i, j]
                    ).astype(bf16)
            else:
                self.sum_c[(i, 0, 0) + self.first] = add_low(
                    self.sum_a[i, x], self.got_c[(i, 0, 0) + self.first]
                ).astype(bf16)
                self.sum_c[(i, 0, 0) + self.second] = add_low(
                    self.sum_b[i, y], self.got_c[(i, 0, 0) + self.second]
                ).astype(bf16)
            return carry

        lax.fori_loop(0, 4, line, 0)


def reduce_scratch(rows, columns):
    half = (rows, columns // 2) if columns > LANES else (rows // 2, columns)
    shapes = (
        (4, 2, 2, rows, columns), (4, 2, 2, rows, columns), (4, 2) + half, (4, 2) + half,
        (4, 2) + half, (4, 2) + half, (3, rows, columns),
    )
    return [pltpu.VMEM(shape, bf16) for shape in shapes]


def norm_rows(grads):
    rows = []
    for grad in grads:
        for i in range(grad.shape[0]):
            for q in range(grad.shape[1] // LANES):
                rows.append(grad[i : i + 1, q * LANES : (q + 1) * LANES])
    return jnp.concatenate(rows, axis=0)


def reduce_kernel(
    gqkv_ref, gout_ref, gup_ref, gdown_ref, gsort_ref, gone_ref, gtwo_ref,
    qkv_sum, out_sum, up_sum, down_sum, sort_sum, norm_sum,
    small, small_sum, send, recv, *scratch,
):
    tile = norm_rows((gone_ref[...], gtwo_ref[...])).astype(bf16)
    for i in range(4):
        for j in range(2):
            for k in range(2):
                for m in range(2):
                    small[i, j, k, m, :16] = gsort_ref[i, j, k, m]
                    small[i, j, k, m, 16:] = tile
    meet_neighbours()
    parts = (gqkv_ref, gout_ref, gup_ref, gdown_ref, small)
    totals = (qkv_sum, out_sum, up_sum, down_sum, small_sum)
    plans = [
        Reduce(part, total, *scratch[7 * b : 7 * b + 7], (send, recv), COPIES * b)
        for b, (part, total) in enumerate(zip(parts, totals))
    ]
    for step in range(4):
        copies = [plan.copies(step) for plan in plans]
        for one in copies:
            start_all(one)
        for one, plan in zip(copies, plans):
            wait_all(one)
            plan.add(step)
    sort_sum[...] = small_sum[:16, :]
    quarter, eighth = norm_place()
    own = norm_sum.shape[1]
    drop = one_hot((4, 16), lambda r, l: r * 4 + quarter, lambda r, l: l).astype(f32)
    pick = one_hot((LANES, own), lambda r, l: r, lambda r, l: l + eighth * own).astype(f32)

    def exact(left, right):
        return lax.dot_general(
            left, right, (((1,), (0,)), ((), ())),
            precision=lax.Precision.HIGHEST, preferred_element_type=f32,
        )

    norm_sum[...] = exact(exact(drop, small_sum[16:, :]), pick)


def reduce(gqkv, gout, gup, gdown, gsort, gone, gtwo):
    devices = 32

    def split(grad):
        return grad.reshape(SPLIT + (grad.shape[0] // devices, grad.shape[1]))

    parts = tuple(split(grad) for grad in (gqkv, gout, gup, gdown, gsort))
    shapes = [part.shape[-2:] for part in parts]
    vmem = pl.BlockSpec(memory_space=pltpu.VMEM)
    small = (32, LANES)
    scratch = [pltpu.VMEM(SPLIT + small, bf16), pltpu.VMEM(small, f32)]
    scratch += [pltpu.SemaphoreType.DMA((5 * COPIES,))] * 2
    for shape in shapes[:4] + [small]:
        scratch += reduce_scratch(*shape)
    qkv, out, up, down, sort, norm = pl.pallas_call(
        reduce_kernel,
        out_shape=tuple(
            jax.ShapeDtypeStruct(shape, f32) for shape in shapes + [(4, gone.shape[1] // devices)]
        ),
        in_specs=[vmem] * 7,
        out_specs=[vmem] * 6,
        scratch_shapes=scratch,
        compiler_params=pltpu.CompilerParams(
            collective_id=1, has_side_effects=True, vmem_limit_bytes=VMEM_LIMIT
        ),
        name="reduce",
    )(*parts, gone, gtwo)
    return jnp.concatenate([qkv, out], axis=1), up, down, sort, norm


def adamw(master, first, second, grad, rate, decay):
    first_new = beta_first * first + (1.0 - beta_first) * grad
    second_new = beta_second * second + (1.0 - beta_second) * grad * grad
    first_hat = first_new / (1.0 - beta_first**STEP)
    second_hat = second_new / (1.0 - beta_second**STEP)
    master_new = master - rate * (first_hat / (jnp.sqrt(second_hat) + adam_eps) + decay * master)
    return (master_new, first_new, second_new)


RATES = (
    (rate_matrix, weight_decay), (rate_matrix, weight_decay), (rate_matrix, weight_decay),
    (rate_other, weight_decay), (rate_other, 0.0),
)


def update_kernel(*refs):
    sums, states, results = refs[:5], refs[5:20], refs[20:]
    for b, (rate, decay) in enumerate(RATES):
        state = [ref[...] for ref in states[3 * b : 3 * b + 3]]
        for ref, value in zip(
            results[3 * b : 3 * b + 3], adamw(*state, sums[b][...], rate, decay)
        ):
            ref[...] = value


def update(sums, states):
    vmem = pl.BlockSpec(memory_space=pltpu.VMEM)
    return pl.pallas_call(
        update_kernel,
        out_shape=tuple(jax.ShapeDtypeStruct(state.shape, f32) for state in states),
        in_specs=[vmem] * 20,
        out_specs=[vmem] * 15,
        compiler_params=pltpu.CompilerParams(vmem_limit_bytes=VMEM_LIMIT),
        name="update",
    )(*sums, *states)


def gather_plain(proj, up, down, sort, norm):
    def gathered(shard, axis):
        return lax.all_gather(shard.astype(bf16), AXES, axis=axis, tiled=True)

    return (*(gathered(shard, 0) for shard in (proj, up, down, sort)), gathered(norm, 1))


def reduce_plain(gqkv, gout, gup, gdown, gsort, gone, gtwo):
    def summed(grad, axis):
        return lax.psum_scatter(
            grad.astype(f32), AXES, scatter_dimension=axis, tiled=True
        )

    gproj = jnp.concatenate([gqkv, gout], axis=1)
    gnorm = jnp.concatenate([gone, gtwo], axis=0)
    return (*(summed(grad, 0) for grad in (gproj, gup, gdown, gsort)), summed(gnorm, 1))


def body(
    near, layer_input, doc_lengths, out_cotangent, *states,
):
    x = layer_input[0]
    cot = out_cotangent[0]
    proj, up, down, sort, norms = (gather if near else gather_plain)(*states[::3])
    normed, qkv, skv, tkv, means, kept = front(doc_lengths, norms, x, proj, sort)
    y, hidden_grad, gq, gkv, gskv, gup, gdown, gout, gnorm_two = middle(
        doc_lengths, norms, x, cot, qkv, skv, proj, up, down
    )
    gx, gqkv, gsort, gnorm_one = back(
        norms, gskv, tkv, kept, means, proj, sort, x, normed, hidden_grad, gq, gkv
    )
    sums = (reduce if near else reduce_plain)(gqkv, gout, gup, gdown, gsort, gnorm_one, gnorm_two)
    return (y[None], gx[None], *update(sums, states))


def solution(mesh):
    rows3, rows2, columns = P(AXES, None, None), P(AXES, None), P(None, AXES)
    near = (mesh.shape["dp"], mesh.shape["fsdp"]) == (8, 4)
    return jax.shard_map(
        functools.partial(body, near),
        mesh=mesh,
        in_specs=(rows3, rows2, rows3) + (rows2,) * 12 + (columns,) * 3,
        out_specs=(rows3, rows3) + (rows2,) * 12 + (columns,) * 3,
        check_vma=False,
    )
```

```python
import functools
import jax
import jax.numpy as jnp
from jax import lax
from jax.experimental import pallas as pl
from jax.experimental.pallas import tpu as pltpu
from jax.sharding import PartitionSpec as P

HD = 64
BLOCK = 32
SINK_ITERS = 8
STEP = 10
TILE = 512
LANES = 128

mask_penalty = 6.0
score_floor = -1000000000.0
norm_eps = 1e-05
beta_first = 0.9
beta_second = 0.95
adam_eps = 1e-08
weight_decay = 0.1
rate_matrix = 0.1
rate_other = 0.5

bf16 = jnp.bfloat16
f32 = jnp.float32
VMEM_LIMIT = 62 * 2**20


def dot(left, right):
    return lax.dot_general(left, right, (((1,), (0,)), ((), ())), preferred_element_type=f32)


def dot_nt(left, right):
    return lax.dot_general(left, right, (((1,), (1,)), ((), ())), preferred_element_type=f32)


def dot_tn(left, right):
    return lax.dot_general(left, right, (((0,), (0,)), ((), ())), preferred_element_type=f32)


def doc_ends(lengths_ref):
    total = lengths_ref[0, 0]
    ends = [total]
    for k in range(1, lengths_ref.shape[1]):
        total = total + lengths_ref[0, k]
        ends.append(total)
    return ends


def segments_of(places, ends):
    count = jnp.zeros(places.shape, jnp.int32)
    for end in ends:
        count = count + (places >= end).astype(jnp.int32)
    return count


def center_scale(values):
    centre = values - jnp.mean(values, axis=-1, keepdims=True)
    spread = jnp.mean(centre * centre, axis=-1, keepdims=True)
    inverse = lax.rsqrt(spread + norm_eps)
    return centre * inverse, inverse


def log_sum_exp(logits, axis):
    top = jnp.max(logits, axis=axis, keepdims=True)
    return top + jnp.log(jnp.sum(jnp.exp(logits - top), axis=axis, keepdims=True))


GROUP = 8 * BLOCK


def regroup_matrix(inverse):
    rows = lax.broadcasted_iota(jnp.int32, (GROUP, GROUP), 1 if inverse else 0)
    columns = lax.broadcasted_iota(jnp.int32, (GROUP, GROUP), 0 if inverse else 1)
    hit = (rows // 8 == columns % BLOCK) & (rows % 8 == columns // BLOCK)
    return hit.astype(f32).astype(bf16)


def spread_tokens(stage, matrix, k, part):
    columns = part.shape[1]
    for g in range(part.shape[0] // GROUP):
        place = pl.multiple_of((k * (part.shape[0] // GROUP) + g) * 8, 8)
        moved = dot(matrix, part[g * GROUP : (g + 1) * GROUP])
        stage[:, pl.ds(place, 8), :] = moved.reshape(BLOCK, 8, columns)


def collect_tokens(stage, matrix, k, rows):
    parts = []
    for g in range(rows // GROUP):
        place = pl.multiple_of((k * (rows // GROUP) + g) * 8, 8)
        part = stage[:, pl.ds(place, 8), :].reshape(GROUP, stage.shape[2]).astype(bf16)
        parts.append(dot(matrix, part))
    return jnp.concatenate(parts, axis=0)


def front_kernel(
    lengths_ref, norms_ref, x_ref, proj_ref, sort_ref,
    normed_hbm, qkv_hbm, skv_hbm, tkv_hbm, means_ref, states_ref,
    normed_s, stage, matrix, qkv_buf, low_buf, flip_buf, copy_sem, qkv_sem, low_sem, flip_sem,
):
    seq, width = x_ref.shape
    tiles = seq // TILE
    blocks = seq // BLOCK
    per_tile = TILE // BLOCK
    chunks = 2 * width // LANES
    ends = doc_ends(lengths_ref)
    gain = norms_ref[0:1, :].astype(f32)
    shift = norms_ref[1:2, :].astype(f32)

    def norm_step(k, carry):
        rows = pl.ds(pl.multiple_of(k * TILE, TILE), TILE)
        xhat, unused = center_scale(x_ref[rows, :].astype(f32))
        normed = (xhat * gain + shift).astype(bf16)
        normed_s[rows, :] = normed
        sums = jnp.sum(normed.astype(f32).reshape(per_tile, BLOCK, width), axis=1)
        means_ref[pl.ds(pl.multiple_of(k * per_tile, per_tile), per_tile), :] = (
            sums * (1.0 / BLOCK)
        ).astype(bf16)
        return carry

    lax.fori_loop(0, tiles, norm_step, 0)
    normed_copy = pltpu.make_async_copy(normed_s, normed_hbm, copy_sem)
    normed_copy.start()

    logits = dot(means_ref[...], sort_ref[...])
    first_i = segments_of(lax.broadcasted_iota(jnp.int32, (blocks, blocks), 0) * BLOCK, ends)
    first_j = segments_of(lax.broadcasted_iota(jnp.int32, (blocks, blocks), 1) * BLOCK, ends)
    logits = jnp.where(first_i != first_j, logits - mask_penalty, logits)

    def qkv_copy(k, slot):
        rows = pl.ds(pl.multiple_of(k * TILE, TILE), TILE)
        return pltpu.make_async_copy(qkv_buf.at[slot], qkv_hbm.at[rows, :], qkv_sem.at[slot])

    def project_step(k, logits):
        rows = pl.ds(pl.multiple_of(k * TILE, TILE), TILE)
        slot = lax.rem(k, 2)

        @pl.when(k >= 2)
        def _():
            qkv_copy(k - 2, slot).wait()

        logits = logits - log_sum_exp(logits, 1)
        states_ref[2 * k] = jnp.exp(logits)
        logits = logits - log_sum_exp(logits, 0)
        states_ref[2 * k + 1] = jnp.exp(logits)
        normed = normed_s[rows, :]
        qkv_buf[slot, :, :width] = dot(normed, proj_ref[:, :width]).astype(bf16)
        product = dot(normed, proj_ref[:, width : 3 * width]).astype(bf16)
        qkv_buf[slot, :, width:] = product
        spread_tokens(stage, matrix[...], k, product)
        qkv_copy(k, slot).start()
        return logits

    assert tiles == SINK_ITERS
    matrix[...] = regroup_matrix(False)
    lax.fori_loop(0, tiles, project_step, logits)
    permute = states_ref[2 * SINK_ITERS - 1].astype(bf16)

    def flip_copy(t, slot):
        return pltpu.make_async_copy(flip_buf.at[slot], tkv_hbm.at[t], flip_sem.at[slot])

    def sort_step(i, carry):
        group = flip_buf.shape[0]

        @pl.when(i >= 1)
        def _():
            for u in range(group):
                flip_copy((i - 1) * group + u, u).wait()

        loaded = []
        for u in range(group):
            t = i * group + u
            loaded.append(stage[t].astype(bf16))
        for u in range(group):
            t = i * group + u
            flip_buf[u] = loaded[u].astype(f32).T.astype(bf16)
            flip_copy(t, u).start()
            stage[t] = dot(permute, loaded[u])
        return carry

    group = flip_buf.shape[0]
    lax.fori_loop(0, BLOCK // group, sort_step, 0)

    def low_copy(k, slot):
        rows = pl.ds(pl.multiple_of(k * TILE, TILE), TILE)
        return pltpu.make_async_copy(low_buf.at[slot], skv_hbm.at[rows, :], low_sem.at[slot])

    def low_step(k, carry):
        rows = pl.ds(pl.multiple_of(k * TILE, TILE), TILE)
        slot = lax.rem(k, 2)

        @pl.when(k >= 2)
        def _():
            low_copy(k - 2, slot).wait()

        low_buf[slot] = collect_tokens(stage, matrix[...], k, TILE).astype(bf16)
        low_copy(k, slot).start()
        return carry

    matrix[...] = regroup_matrix(True)
    lax.fori_loop(0, tiles, low_step, 0)
    for u in range(group):
        flip_copy(BLOCK - group + u, u).wait()
    for k in (tiles - 2, tiles - 1):
        qkv_copy(k, k % 2).wait()
        low_copy(k, k % 2).wait()
    normed_copy.wait()


def front(lengths, norms, x, proj, sort):
    seq, width = x.shape
    blocks = seq // BLOCK
    hbm = pl.BlockSpec(memory_space=pl.ANY)
    vmem = pl.BlockSpec(memory_space=pltpu.VMEM)
    return pl.pallas_call(
        front_kernel,
        out_shape=(
            jax.ShapeDtypeStruct((seq, width), bf16),
            jax.ShapeDtypeStruct((seq, 3 * width), bf16),
            jax.ShapeDtypeStruct((seq, 2 * width), bf16),
            jax.ShapeDtypeStruct((BLOCK, 2 * width, blocks), bf16),
            jax.ShapeDtypeStruct((blocks, width), bf16),
            jax.ShapeDtypeStruct((2 * SINK_ITERS, blocks, blocks), f32),
        ),
        in_specs=[pl.BlockSpec(memory_space=pltpu.SMEM), vmem, vmem, vmem, vmem],
        out_specs=[hbm, hbm, hbm, hbm, vmem, vmem],
        scratch_shapes=[
            pltpu.VMEM((seq, width), bf16),
            pltpu.VMEM((BLOCK, blocks, 2 * width), f32),
            pltpu.VMEM((GROUP, GROUP), bf16),
            pltpu.VMEM((2, TILE, 3 * width), bf16),
            pltpu.VMEM((2, TILE, 2 * width), bf16),
            pltpu.VMEM((4, 2 * width, blocks), bf16),
            pltpu.SemaphoreType.DMA,
            pltpu.SemaphoreType.DMA((2,)),
            pltpu.SemaphoreType.DMA((2,)),
            pltpu.SemaphoreType.DMA((8,)),
        ],
        compiler_params=pltpu.CompilerParams(vmem_limit_bytes=VMEM_LIMIT),
        name="front",
    )(lengths, norms, x, proj, sort)


def layer_norm_back(grad, gain, xhat, inverse):
    scaled = grad * gain
    mean_one = jnp.mean(scaled, axis=-1, keepdims=True)
    mean_two = jnp.mean(scaled * xhat, axis=-1, keepdims=True)
    return (scaled - mean_one - xhat * mean_two) * inverse


def middle_kernel(
    lengths_ref, norms_ref, x_ref, cot_ref, qkv_ref, skv_ref, out_proj_ref, up_ref, down_ref,
    y_ref, hidden_grad_ref, gq_ref, gkv_ref, gskv_ref, gup_ref, gdown_ref, gout_ref, gnorm_ref,
    gup, gdown, gout, probs_s, context_s, gcontext_s, gq_s, gkv_s, gskv_s, grads_s,
):
    step = pl.program_id(0)
    tile, width = x_ref.shape
    hidden_units = up_ref.shape[1]
    pairs = tile // (2 * BLOCK)
    head_pairs = width // LANES
    scale = HD ** (-0.5)
    ends = doc_ends(lengths_ref)

    @pl.when(step == 0)
    def _():
        gup[...] = jnp.zeros_like(gup)
        gdown[...] = jnp.zeros_like(gdown)
        gout[...] = jnp.zeros_like(gout)
        gnorm_ref[...] = jnp.zeros_like(gnorm_ref)

    lane = lax.broadcasted_iota(jnp.int32, (1, LANES), 1)
    low_head = lane < HD
    low_block = lax.rem(lane, 2 * BLOCK) < BLOCK
    head_one = low_head.astype(f32).astype(bf16)
    head_two = (1.0 - low_head.astype(f32)).astype(bf16)
    block_one = low_block.astype(f32).astype(bf16)
    block_two = (1.0 - low_block.astype(f32)).astype(bf16)

    def two_heads(part):
        return jnp.concatenate(
            [part * head_one, part * head_two], axis=0
        )

    def two_blocks(part):
        return jnp.concatenate(
            [part * block_one, part * block_two], axis=0
        )

    def stack_keys(own, far):
        return jnp.concatenate(
            [own[:BLOCK], far[:BLOCK], own[BLOCK:], far[BLOCK:]], axis=0
        )

    def pick_block(full):
        return jnp.where(low_block, full[: 2 * BLOCK], full[2 * BLOCK :])

    def pick_head(full):
        return jnp.where(low_head, full[: 2 * BLOCK], full[2 * BLOCK :])

    def attend(p, carry):
        rows = pl.ds(pl.multiple_of(p * 2 * BLOCK, 2 * BLOCK), 2 * BLOCK)
        base = step * tile + p * 2 * BLOCK
        query_seg = segments_of(base + lax.rem(lane, 2 * BLOCK), ends)
        key_place = (
            base
            + jnp.where(low_block, 0, BLOCK)
            + lax.broadcasted_iota(jnp.int32, (BLOCK, LANES), 0)
        )
        same = segments_of(key_place, ends) == query_seg
        for hp in range(head_pairs):
            cols = slice(hp * LANES, (hp + 1) * LANES)
            key_cols = slice(width + hp * LANES, width + (hp + 1) * LANES)
            value_cols = slice(2 * width + hp * LANES, 2 * width + (hp + 1) * LANES)
            queries = two_heads(qkv_ref[rows, cols])
            keys = stack_keys(qkv_ref[rows, key_cols], skv_ref[rows, cols])
            values = stack_keys(qkv_ref[rows, value_cols], skv_ref[rows, key_cols])
            scores = pick_block(dot(keys, queries.astype(f32).T.astype(bf16))) * scale
            scores = jnp.concatenate(
                [jnp.where(same, scores[:BLOCK], score_floor), scores[BLOCK:]], axis=0
            )
            exps = jnp.exp(scores - jnp.max(scores, axis=0, keepdims=True))
            probs = (exps / jnp.sum(exps, axis=0, keepdims=True)).astype(bf16)
            probs_s[p * head_pairs + hp] = probs
            context_s[rows, cols] = pick_head(dot_tn(two_blocks(probs), values)).astype(bf16)
        return carry

    lax.fori_loop(0, pairs, attend, 0, unroll=8)

    inputs = x_ref[...].astype(f32)
    context = context_s[...]
    hidden = inputs + dot(context, out_proj_ref[...])
    xhat_two, inverse_two = center_scale(hidden)
    gain_two = norms_ref[2:3, :].astype(f32)
    normed_two = (xhat_two * gain_two + norms_ref[3:4, :].astype(f32)).astype(bf16)
    normed_two_t = normed_two.T
    cot = cot_ref[...]
    total_out = hidden
    grad_normed_two = None
    root = 0.7978845608028654
    for c in range(hidden_units // TILE):
        cols = slice(c * TILE, (c + 1) * TILE)
        pre = dot(normed_two, up_ref[:, cols])
        grad_act = dot_nt(cot, down_ref[cols, :])
        square = pre * pre
        half_tanh = 0.5 + 0.5 * jnp.tanh(pre * (root + (root * 0.044715) * square))
        act = pre * half_tanh
        slope = half_tanh + act * (1.0 - half_tanh) * (
            2.0 * root + (6.0 * root * 0.044715) * square
        )
        act = act.astype(bf16)
        grad_pre = (grad_act * slope).astype(bf16)
        total_out = total_out + dot(act, down_ref[cols, :])
        back = dot_nt(grad_pre, up_ref[:, cols])
        grad_normed_two = back if grad_normed_two is None else grad_normed_two + back
        gup[:, cols] += dot(normed_two_t, grad_pre)
        gdown[cols, :] += dot_tn(act, cot)
    y_ref[...] = total_out.astype(bf16)
    gnorm_ref[0:1, :] += jnp.sum(grad_normed_two * xhat_two, axis=0, keepdims=True)
    gnorm_ref[1:2, :] += jnp.sum(grad_normed_two, axis=0, keepdims=True)
    hidden_grad = cot.astype(f32) + layer_norm_back(
        grad_normed_two, gain_two, xhat_two, inverse_two
    )
    hidden_grad_ref[...] = hidden_grad
    grad_attn = hidden_grad.astype(bf16)
    gout[...] += dot_tn(context, grad_attn)
    gcontext_s[...] = dot_nt(grad_attn, out_proj_ref[...]).astype(bf16)

    def attend_back(p, carry):
        rows = pl.ds(pl.multiple_of(p * 2 * BLOCK, 2 * BLOCK), 2 * BLOCK)
        for hp in range(head_pairs):
            cols = slice(hp * LANES, (hp + 1) * LANES)
            key_cols = slice(width + hp * LANES, width + (hp + 1) * LANES)
            value_cols = slice(2 * width + hp * LANES, 2 * width + (hp + 1) * LANES)
            values = stack_keys(qkv_ref[rows, value_cols], skv_ref[rows, key_cols])
            gcontext = two_heads(gcontext_s[rows, cols])
            wide = probs_s[p * head_pairs + hp].astype(f32)
            grad_probs = pick_block(dot(values, gcontext.astype(f32).T.astype(bf16)))
            weighted = wide * grad_probs
            grad_scores = weighted - wide * jnp.sum(weighted, axis=0, keepdims=True)
            grad_scores = (grad_scores * scale).astype(bf16)
            grads_s[p * head_pairs + hp] = grad_scores
        return carry

    lax.fori_loop(0, pairs, attend_back, 0, unroll=8)

    def attend_last(p, carry):
        rows = pl.ds(pl.multiple_of(p * 2 * BLOCK, 2 * BLOCK), 2 * BLOCK)
        for hp in range(head_pairs):
            cols = slice(hp * LANES, (hp + 1) * LANES)
            key_cols = slice(width + hp * LANES, width + (hp + 1) * LANES)
            value_cols = slice(2 * width + hp * LANES, 2 * width + (hp + 1) * LANES)
            keys = stack_keys(qkv_ref[rows, key_cols], skv_ref[rows, cols])
            gq_s[rows, cols] = pick_head(dot_tn(two_blocks(grads_s[p * head_pairs + hp]), keys)).astype(bf16)
            gkeys = dot(two_blocks(grads_s[p * head_pairs + hp]), two_heads(qkv_ref[rows, cols])).astype(bf16)
            gvalues = dot(two_blocks(probs_s[p * head_pairs + hp]), two_heads(gcontext_s[rows, cols])).astype(bf16)
            for grads, where in ((gkeys, cols), (gvalues, key_cols)):
                gkv_s[rows, where] = jnp.concatenate(
                    [grads[:BLOCK], grads[2 * BLOCK : 3 * BLOCK]], axis=0
                )
                gskv_s[rows, where] = jnp.concatenate(
                    [grads[BLOCK : 2 * BLOCK], grads[3 * BLOCK :]], axis=0
                )
        return carry

    lax.fori_loop(0, pairs, attend_last, 0, unroll=8)
    gq_ref[...] = gq_s[...]
    gkv_ref[...] = gkv_s[...]
    gskv_ref[...] = gskv_s[...]

    @pl.when(step == pl.num_programs(0) - 1)
    def _():
        gup_ref[...] = gup[...].astype(bf16)
        gdown_ref[...] = gdown[...].astype(bf16)
        gout_ref[...] = gout[...].astype(bf16)


def middle(lengths, norms, x, cot, qkv, skv, proj, up, down):
    seq, width = x.shape
    hidden_units = up.shape[1]
    tiles = seq // TILE

    def rows(columns):
        return pl.BlockSpec((TILE, columns), lambda i: (i, 0))

    def fixed(shape, index=(0, 0)):
        return pl.BlockSpec(shape, lambda i: index, pipeline_mode=pl.Buffered(1))

    return pl.pallas_call(
        middle_kernel,
        grid=(tiles,),
        out_shape=(
            jax.ShapeDtypeStruct((seq, width), bf16),
            jax.ShapeDtypeStruct((seq, width), f32),
            jax.ShapeDtypeStruct((seq, width), bf16),
            jax.ShapeDtypeStruct((seq, 2 * width), bf16),
            jax.ShapeDtypeStruct((seq, 2 * width), bf16),
            jax.ShapeDtypeStruct((width, hidden_units), bf16),
            jax.ShapeDtypeStruct((hidden_units, width), bf16),
            jax.ShapeDtypeStruct((width, width), bf16),
            jax.ShapeDtypeStruct((2, width), f32),
        ),
        in_specs=[
            pl.BlockSpec(memory_space=pltpu.SMEM),
            fixed(norms.shape),
            rows(width),
            rows(width),
            rows(3 * width),
            rows(2 * width),
            fixed((width, width), (0, 3)),
            fixed(up.shape),
            fixed(down.shape),
        ],
        out_specs=[
            rows(width),
            rows(width),
            rows(width),
            rows(2 * width),
            rows(2 * width),
            fixed((width, hidden_units)),
            fixed((hidden_units, width)),
            fixed((width, width)),
            fixed((2, width)),
        ],
        scratch_shapes=[
            pltpu.VMEM((width, hidden_units), f32),
            pltpu.VMEM((hidden_units, width), f32),
            pltpu.VMEM((width, width), f32),
            pltpu.VMEM((TILE // (2 * BLOCK) * (width // LANES), 2 * BLOCK, LANES), bf16),
            pltpu.VMEM((TILE, width), bf16),
            pltpu.VMEM((TILE, width), bf16),pltpu.VMEM((TILE, width), bf16),pltpu.VMEM((TILE, 2*width), bf16),pltpu.VMEM((TILE, 2*width), bf16),
            pltpu.VMEM((TILE // (2 * BLOCK) * (width // LANES), 2 * BLOCK, LANES), bf16),
        ],
        compiler_params=pltpu.CompilerParams(vmem_limit_bytes=VMEM_LIMIT),
        name="middle",
    )(lengths, norms, x, cot, qkv, skv, proj, up, down)


def back_kernel(
    norms_ref, gskv_hbm, tkv_hbm, states_ref, means_ref, proj_ref, sort_ref,
    x_hbm, normed_hbm, hidden_grad_hbm, gq_hbm, gkv_hbm,
    gx_hbm, gproj_ref, gsort_ref, gnorm_ref,
    stage, matrix, low_buf, flip_buf, gproj, gperm, gmeans, low_sem, flip_sem,
):
    seq, width = x_hbm.shape
    tiles = seq // TILE
    blocks = seq // BLOCK
    chunks = 2 * width // LANES
    per_tile = TILE // BLOCK

    def low_copy(k, slot):
        rows = pl.ds(pl.multiple_of(k * TILE, TILE), TILE)
        return pltpu.make_async_copy(gskv_hbm.at[rows, :], low_buf.at[slot], low_sem.at[slot])

    group = flip_buf.shape[0] // 2

    def flip_copy(t, slot):
        return pltpu.make_async_copy(tkv_hbm.at[t], flip_buf.at[slot], flip_sem.at[slot])

    low_copy(0, 0).start()
    low_copy(1, 1).start()
    for u in range(group):
        flip_copy(u, u).start()

    def load_step(k, carry):
        rows = pl.ds(pl.multiple_of(k * TILE, TILE), TILE)
        slot = lax.rem(k, 2)
        low_copy(k, slot).wait()
        spread_tokens(stage, matrix[...], k, low_buf[slot])

        @pl.when(k + 2 < tiles)
        def _():
            low_copy(k + 2, slot).start()

        return carry

    matrix[...] = regroup_matrix(False)
    lax.fori_loop(0, tiles, load_step, 0)
    matrix[...] = regroup_matrix(True)

    final = states_ref[2 * SINK_ITERS - 1]
    permute_t = final.T.astype(bf16)
    gperm[...] = jnp.zeros_like(gperm)

    def sort_step(i, carry):
        side = lax.rem(i, 2) * group

        @pl.when(i + 1 < BLOCK // group)
        def _():
            for u in range(group):
                flip_copy((i + 1) * group + u, group - side + u).start()

        for u in range(group):
            flip_copy(i * group + u, side + u).wait()
        loaded = []
        for u in range(group):
            t = i * group + u
            loaded.append(stage[t].astype(bf16))
        total = gperm[...]
        for u in range(group):
            t = i * group + u
            total = total + dot(loaded[u], flip_buf[side + u])
            stage[t] = dot(permute_t, loaded[u])
        gperm[...] = total
        return carry

    lax.fori_loop(0, BLOCK // group, sort_step, 0)

    grad = gperm[...] * final
    for sweep in reversed(range(SINK_ITERS)):
        grad = grad - states_ref[2 * sweep + 1] * jnp.sum(grad, axis=0, keepdims=True)
        grad = grad - states_ref[2 * sweep] * jnp.sum(grad, axis=1, keepdims=True)
    grad = grad.astype(bf16)
    gsort_ref[...] = dot_tn(means_ref[...], grad).astype(gsort_ref.dtype)
    gmeans[...] = dot_nt(grad, sort_ref[...]) * (1.0 / BLOCK)
    gproj[...] = jnp.zeros_like(gproj)
    gnorm_ref[...] = jnp.zeros_like(gnorm_ref)
    gain = norms_ref[0:1, :].astype(f32)

    def tile_step(x_ref, normed_ref, hidden_grad_ref, gq_ref, gkv_ref, gx_ref):
        k = pl.program_id(0)
        rows = pl.ds(pl.multiple_of(k * TILE, TILE), TILE)
        far = collect_tokens(stage, matrix[...], k, TILE)
        gkv = (gkv_ref[...].astype(f32) + far).astype(bf16)
        gq = gq_ref[...]
        normed = normed_ref[...]
        gproj[:, :width] += dot_tn(normed, gq)
        gproj[:, width:] += dot_tn(normed, gkv)
        grad_normed = dot_nt(gq, proj_ref[:, :width]) + dot_nt(gkv, proj_ref[:, width : 3 * width])
        means = gmeans[pl.ds(pl.multiple_of(k * per_tile, per_tile), per_tile), :]
        grad_normed = grad_normed + jnp.broadcast_to(
            means[:, None, :], (per_tile, BLOCK, width)
        ).reshape(TILE, width)
        xhat, inverse = center_scale(x_ref[...].astype(f32))
        gnorm_ref[0:1, :] += jnp.sum(grad_normed * xhat, axis=0, keepdims=True)
        gnorm_ref[1:2, :] += jnp.sum(grad_normed, axis=0, keepdims=True)
        gx_ref[...] = hidden_grad_ref[...] + layer_norm_back(grad_normed, gain, xhat, inverse)

    def rows_of(columns):
        return pl.BlockSpec((TILE, columns), lambda i: (i, 0))

    pltpu.emit_pipeline(
        tile_step,
        grid=(tiles,),
        in_specs=[rows_of(width)] * 4 + [rows_of(2 * width)],
        out_specs=[rows_of(width)],
    )(x_hbm, normed_hbm, hidden_grad_hbm, gq_hbm, gkv_hbm, gx_hbm)
    gproj_ref[...] = gproj[...].astype(gproj_ref.dtype)


def back(norms, gskv, tkv, states, means, proj, sort, x, normed, hidden_grad, gq, gkv):
    seq, width = x.shape
    blocks = seq // BLOCK
    hbm = pl.BlockSpec(memory_space=pl.ANY)
    vmem = pl.BlockSpec(memory_space=pltpu.VMEM)
    return pl.pallas_call(
        back_kernel,
        out_shape=(
            jax.ShapeDtypeStruct((seq, width), f32),
            jax.ShapeDtypeStruct((width, 3 * width), bf16),
            jax.ShapeDtypeStruct((width, blocks), bf16),
            jax.ShapeDtypeStruct((2, width), f32),
        ),
        in_specs=[vmem, hbm, hbm, vmem, vmem, vmem, vmem, hbm, hbm, hbm, hbm, hbm],
        out_specs=[hbm, vmem, vmem, vmem],
        scratch_shapes=[
            pltpu.VMEM((BLOCK, blocks, 2 * width), f32),
            pltpu.VMEM((GROUP, GROUP), bf16),
            pltpu.VMEM((2, TILE, 2 * width), bf16),
            pltpu.VMEM((8, 2 * width, blocks), bf16),
            pltpu.VMEM((width, 3 * width), f32),
            pltpu.VMEM((blocks, blocks), f32),
            pltpu.VMEM((blocks, width), f32),
            pltpu.SemaphoreType.DMA((2,)),
            pltpu.SemaphoreType.DMA((8,)),
        ],
        compiler_params=pltpu.CompilerParams(vmem_limit_bytes=VMEM_LIMIT),
        name="back",
    )(norms, gskv, tkv, states, means, proj, sort, x, normed, hidden_grad, gq, gkv)


MESH_ID = pl.DeviceIdType.MESH
AXES = ("dp", "fsdp")
SPLIT = (4, 2, 2, 2)
COPIES = 8


def coordinates():
    dp, fsdp = lax.axis_index("dp"), lax.axis_index("fsdp")
    return dp // 2, dp % 2, fsdp // 2, fsdp % 2


def device_of(z, x, y, c):
    return (z * 2 + x, y * 2 + c)


def z_others(z):
    return (z + 1 - 2 * (z % 2), (z + 2) % 4, 3 - z)


def neighbours():
    z, x, y, c = coordinates()
    others = [device_of(one, x, y, c) for one in z_others(z)]
    return others + [
        device_of(z, 1 - x, y, c), device_of(z, x, 1 - y, c), device_of(z, x, y, 1 - c)
    ]


def meet_neighbours():
    barrier = pltpu.get_barrier_semaphore()
    peers = neighbours()
    for peer in peers:
        pl.semaphore_signal(barrier, inc=1, device_id=peer, device_id_type=MESH_ID)
    pl.semaphore_wait(barrier, len(peers))


def halves(shape):
    if shape[-1] > LANES:
        middle_column = shape[-1] // 2
        return (
            (slice(None), pl.ds(0, middle_column)),
            (slice(None), pl.ds(middle_column, middle_column)),
        )
    middle_row = shape[-2] // 2
    return (
        (pl.ds(0, middle_row), slice(None)),
        (pl.ds(middle_row, middle_row), slice(None)),
    )


def remote(source, target, sems, index, device):
    send, recv = sems
    return pltpu.make_async_remote_copy(
        src_ref=source, dst_ref=target, send_sem=send.at[index], recv_sem=recv.at[index],
        device_id=device, device_id_type=MESH_ID,
    )


def gather_stages(full, sems, base):
    z, x, y, c = coordinates()
    first, second = halves(full.shape)
    every = slice(None)

    def same(index, place, device):
        part = full.at[place]
        return remote(part, part, sems, base + index, device)

    def stage_z():
        return [
            same(k, (z, x, y, c), device_of(one, x, y, c)) for k, one in enumerate(z_others(z))
        ]

    def stage_one():
        return [
            same(3, (every, x, y, c) + first, device_of(z, 1 - x, y, c)),
            same(4, (every, x, y, c) + second, device_of(z, x, 1 - y, c)),
        ]

    def stage_two():
        return [
            same(5, (every, every, y, c) + first, device_of(z, x, 1 - y, c)),
            same(6, (every, x, every, c) + second, device_of(z, 1 - x, y, c)),
        ]

    def stage_core():
        return [same(7, (every, every, every, c), device_of(z, x, y, 1 - c))]

    return [stage_z, stage_one, stage_two, stage_core]


def start_all(copies):
    for copy in copies:
        copy.start()


def wait_all(copies):
    for copy in copies:
        copy.wait()


def one_hot(shape, row_of, column_of):
    rows = lax.broadcasted_iota(jnp.int32, shape, 0)
    columns = lax.broadcasted_iota(jnp.int32, shape, 1)
    return row_of(rows, columns) == column_of(rows, columns)


def norm_place():
    z, x, y, c = coordinates()
    device = (z * 2 + x) * 4 + y * 2 + c
    return device // 8, device % 8


def gather_kernel(proj_ref, up_ref, down_ref, sort_ref, norm_ref, proj, up, down, small, send, recv):
    z, x, y, c = coordinates()
    mine = (z, x, y, c)
    proj[mine] = proj_ref[...].astype(bf16)
    up[mine] = up_ref[...].astype(bf16)
    down[mine] = down_ref[...].astype(bf16)
    quarter, eighth = norm_place()
    own = norm_ref.shape[1]
    spread = one_hot((own, LANES), lambda r, l: r + eighth * own, lambda r, l: l)
    lanes = dot(norm_ref[...].astype(bf16), spread.astype(bf16)).astype(bf16)
    lift = one_hot((16, 4), lambda r, l: r, lambda r, l: l * 4 + quarter)
    tile = dot(lift.astype(bf16), lanes).astype(bf16)
    small[mine] = jnp.concatenate([sort_ref[...].astype(bf16), tile], axis=0)
    meet_neighbours()
    fulls = (proj, up, down, small)
    plans = [gather_stages(full, (send, recv), COPIES * b) for b, full in enumerate(fulls)]
    for step in range(4):
        copies = [copy for plan in plans for copy in plan[step]()]
        start_all(copies)
        wait_all(copies)


def gather(proj, up, down, sort, norm):
    shapes = (proj.shape, up.shape, down.shape, (32, LANES))
    vmem = pl.BlockSpec(memory_space=pltpu.VMEM)
    proj, up, down, small = pl.pallas_call(
        gather_kernel,
        out_shape=tuple(jax.ShapeDtypeStruct(SPLIT + shape, bf16) for shape in shapes),
        in_specs=[vmem] * 5,
        out_specs=[vmem] * 4,
        scratch_shapes=[pltpu.SemaphoreType.DMA((4 * COPIES,))] * 2,
        compiler_params=pltpu.CompilerParams(
            collective_id=0, has_side_effects=True, vmem_limit_bytes=VMEM_LIMIT
        ),
        name="gather",
    )(proj, up, down, sort, norm)
    small = small.reshape(32, 32, LANES)
    sort = small[:, :16].reshape(-1, LANES)
    norms = jnp.sum(small[:, 16:].astype(f32), axis=0).astype(bf16).reshape(4, -1)

    def flat(array):
        return array.reshape(-1, array.shape[-1])

    return flat(proj), flat(up), flat(down), sort, norms


def add_low(*parts):
    total = parts[0].astype(f32)
    for part in parts[1:]:
        total = total + part.astype(f32)
    return total


class Reduce:
    def __init__(self, part, total, got_c, sum_c, got_a, got_b, sum_a, sum_b, got_z, sems, base):
        self.part, self.total, self.got_c, self.sum_c = part, total, got_c, sum_c
        self.got_a, self.got_b, self.sum_a, self.sum_b = got_a, got_b, sum_a, sum_b
        self.got_z, self.sems, self.base = got_z, sems, base
        self.first, self.second = halves(part.shape)

    def copies(self, step):
        z, x, y, c = coordinates()
        every = slice(None)
        to_x, to_y = device_of(z, 1 - x, y, c), device_of(z, x, 1 - y, c)

        def one(source, target, index, device):
            return remote(source, target, self.sems, self.base + index, device)

        if step == 0:
            away = self.part.at[every, every, every, 1 - c]
            return [one(away, self.got_c, 0, device_of(z, x, y, 1 - c))]
        if step == 1:
            away_a = self.sum_c.at[(every, every, 1 - y) + self.first]
            away_b = self.sum_c.at[(every, 1 - x, every) + self.second]
            return [one(away_a, self.got_a, 1, to_y), one(away_b, self.got_b, 2, to_x)]
        if step == 2:
            away_a, away_b = self.sum_a.at[every, 1 - x], self.sum_b.at[every, 1 - y]
            return [
                one(away_a, self.got_c.at[(every, 0, 0) + self.first], 3, to_x),
                one(away_b, self.got_c.at[(every, 0, 0) + self.second], 4, to_y),
            ]
        return [
            one(self.sum_c.at[other, 0, 0], self.got_z.at[k], 5 + k, device_of(other, x, y, c))
            for k, other in enumerate(z_others(z))
        ]

    def add(self, step):
        z, x, y, c = coordinates()
        if step == 3:
            self.total[...] = add_low(self.sum_c[z, 0, 0], *[self.got_z[k] for k in range(3)])
            return

        def line(i, carry):
            if step == 0:
                for j in range(2):
                    for k in range(2):
                        self.sum_c[i, j, k] = add_low(
                            self.part[i, j, k, c], self.got_c[i, j, k]
                        ).astype(bf16)
            elif step == 1:
                for j in range(2):
                    self.sum_a[i, j] = add_low(
                        self.sum_c[(i, j, y) + self.first], self.got_a[i, j]
                    ).astype(bf16)
                    self.sum_b[i, j] = add_low(
                        self.sum_c[(i, x, j) + self.second], self.got_b[i, j]
                    ).astype(bf16)
            else:
                self.sum_c[(i, 0, 0) + self.first] = add_low(
                    self.sum_a[i, x], self.got_c[(i, 0, 0) + self.first]
                ).astype(bf16)
                self.sum_c[(i, 0, 0) + self.second] = add_low(
                    self.sum_b[i, y], self.got_c[(i, 0, 0) + self.second]
                ).astype(bf16)
            return carry

        lax.fori_loop(0, 4, line, 0)


def reduce_scratch(rows, columns):
    half = (rows, columns // 2) if columns > LANES else (rows // 2, columns)
    shapes = (
        (4, 2, 2, rows, columns), (4, 2, 2, rows, columns), (4, 2) + half, (4, 2) + half,
        (4, 2) + half, (4, 2) + half, (3, rows, columns),
    )
    return [pltpu.VMEM(shape, bf16) for shape in shapes]


def norm_rows(grads):
    rows = []
    for grad in grads:
        for i in range(grad.shape[0]):
            for q in range(grad.shape[1] // LANES):
                rows.append(grad[i : i + 1, q * LANES : (q + 1) * LANES])
    return jnp.concatenate(rows, axis=0)


def reduce_kernel(
    gqkv_ref, gout_ref, gup_ref, gdown_ref, gsort_ref, gone_ref, gtwo_ref,
    qkv_sum, out_sum, up_sum, down_sum, sort_sum, norm_sum,
    small, small_sum, send, recv, *scratch,
):
    tile = norm_rows((gone_ref[...], gtwo_ref[...])).astype(bf16)
    for i in range(4):
        for j in range(2):
            for k in range(2):
                for m in range(2):
                    small[i, j, k, m, :16] = gsort_ref[i, j, k, m]
                    small[i, j, k, m, 16:] = tile
    meet_neighbours()
    parts = (gqkv_ref, gout_ref, gup_ref, gdown_ref, small)
    totals = (qkv_sum, out_sum, up_sum, down_sum, small_sum)
    plans = [
        Reduce(part, total, *scratch[7 * b : 7 * b + 7], (send, recv), COPIES * b)
        for b, (part, total) in enumerate(zip(parts, totals))
    ]
    for step in range(4):
        copies = [plan.copies(step) for plan in plans]
        for one in copies:
            start_all(one)
        for one, plan in zip(copies, plans):
            wait_all(one)
            plan.add(step)
    sort_sum[...] = small_sum[:16, :]
    quarter, eighth = norm_place()
    own = norm_sum.shape[1]
    drop = one_hot((4, 16), lambda r, l: r * 4 + quarter, lambda r, l: l).astype(f32)
    pick = one_hot((LANES, own), lambda r, l: r, lambda r, l: l + eighth * own).astype(f32)

    def exact(left, right):
        return lax.dot_general(
            left, right, (((1,), (0,)), ((), ())),
            precision=lax.Precision.HIGHEST, preferred_element_type=f32,
        )

    norm_sum[...] = exact(exact(drop, small_sum[16:, :]), pick)


def reduce(gqkv, gout, gup, gdown, gsort, gone, gtwo):
    devices = 32

    def split(grad):
        return grad.reshape(SPLIT + (grad.shape[0] // devices, grad.shape[1]))

    parts = tuple(split(grad) for grad in (gqkv, gout, gup, gdown, gsort))
    shapes = [part.shape[-2:] for part in parts]
    vmem = pl.BlockSpec(memory_space=pltpu.VMEM)
    small = (32, LANES)
    scratch = [pltpu.VMEM(SPLIT + small, bf16), pltpu.VMEM(small, f32)]
    scratch += [pltpu.SemaphoreType.DMA((5 * COPIES,))] * 2
    for shape in shapes[:4] + [small]:
        scratch += reduce_scratch(*shape)
    qkv, out, up, down, sort, norm = pl.pallas_call(
        reduce_kernel,
        out_shape=tuple(
            jax.ShapeDtypeStruct(shape, f32) for shape in shapes + [(4, gone.shape[1] // devices)]
        ),
        in_specs=[vmem] * 7,
        out_specs=[vmem] * 6,
        scratch_shapes=scratch,
        compiler_params=pltpu.CompilerParams(
            collective_id=1, has_side_effects=True, vmem_limit_bytes=VMEM_LIMIT
        ),
        name="reduce",
    )(*parts, gone, gtwo)
    return jnp.concatenate([qkv, out], axis=1), up, down, sort, norm


def adamw(master, first, second, grad, rate, decay):
    first_new = beta_first * first + (1.0 - beta_first) * grad
    second_new = beta_second * second + (1.0 - beta_second) * grad * grad
    first_hat = first_new / (1.0 - beta_first**STEP)
    second_hat = second_new / (1.0 - beta_second**STEP)
    master_new = master - rate * (first_hat / (jnp.sqrt(second_hat) + adam_eps) + decay * master)
    return (master_new, first_new, second_new)


RATES = (
    (rate_matrix, weight_decay), (rate_matrix, weight_decay), (rate_matrix, weight_decay),
    (rate_other, weight_decay), (rate_other, 0.0),
)


def update_kernel(*refs):
    sums, states, results = refs[:5], refs[5:20], refs[20:]
    for b, (rate, decay) in enumerate(RATES):
        state = [ref[...] for ref in states[3 * b : 3 * b + 3]]
        for ref, value in zip(
            results[3 * b : 3 * b + 3], adamw(*state, sums[b][...], rate, decay)
        ):
            ref[...] = value


def update(sums, states):
    vmem = pl.BlockSpec(memory_space=pltpu.VMEM)
    return pl.pallas_call(
        update_kernel,
        out_shape=tuple(jax.ShapeDtypeStruct(state.shape, f32) for state in states),
        in_specs=[vmem] * 20,
        out_specs=[vmem] * 15,
        compiler_params=pltpu.CompilerParams(vmem_limit_bytes=VMEM_LIMIT),
        name="update",
    )(*sums, *states)


def gather_plain(proj, up, down, sort, norm):
    def gathered(shard, axis):
        return lax.all_gather(shard.astype(bf16), AXES, axis=axis, tiled=True)

    return (*(gathered(shard, 0) for shard in (proj, up, down, sort)), gathered(norm, 1))


def reduce_plain(gqkv, gout, gup, gdown, gsort, gone, gtwo):
    def summed(grad, axis):
        return lax.psum_scatter(
            grad.astype(f32), AXES, scatter_dimension=axis, tiled=True
        )

    gproj = jnp.concatenate([gqkv, gout], axis=1)
    gnorm = jnp.concatenate([gone, gtwo], axis=0)
    return (*(summed(grad, 0) for grad in (gproj, gup, gdown, gsort)), summed(gnorm, 1))


def body(
    near, layer_input, doc_lengths, out_cotangent, *states,
):
    x = layer_input[0]
    cot = out_cotangent[0]
    proj, up, down, sort, norms = (gather if near else gather_plain)(*states[::3])
    normed, qkv, skv, tkv, means, kept = front(doc_lengths, norms, x, proj, sort)
    y, hidden_grad, gq, gkv, gskv, gup, gdown, gout, gnorm_two = middle(
        doc_lengths, norms, x, cot, qkv, skv, proj, up, down
    )
    gx, gqkv, gsort, gnorm_one = back(
        norms, gskv, tkv, kept, means, proj, sort, x, normed, hidden_grad, gq, gkv
    )
    sums = (reduce if near else reduce_plain)(gqkv, gout, gup, gdown, gsort, gnorm_one, gnorm_two)
    return (y[None], gx[None], *update(sums, states))


def solution(mesh):
    rows3, rows2, columns = P(AXES, None, None), P(AXES, None), P(None, AXES)
    near = (mesh.shape["dp"], mesh.shape["fsdp"]) == (8, 4)
    return jax.shard_map(
        functools.partial(body, near),
        mesh=mesh,
        in_specs=(rows3, rows2, rows3) + (rows2,) * 12 + (columns,) * 3,
        out_specs=(rows3, rows3) + (rows2,) * 12 + (columns,) * 3,
        check_vma=False,
    )
```

```python
import functools
import jax
import jax.numpy as jnp
from jax import lax
from jax.experimental import pallas as pl
from jax.experimental.pallas import tpu as pltpu
from jax.sharding import PartitionSpec as P

HD = 64
BLOCK = 32
SINK_ITERS = 8
STEP = 10
TILE = 512
LANES = 128

mask_penalty = 6.0
score_floor = -1000000000.0
norm_eps = 1e-05
beta_first = 0.9
beta_second = 0.95
adam_eps = 1e-08
weight_decay = 0.1
rate_matrix = 0.1
rate_other = 0.5

bf16 = jnp.bfloat16
f32 = jnp.float32
VMEM_LIMIT = 62 * 2**20


def dot(left, right):
    return lax.dot_general(left, right, (((1,), (0,)), ((), ())), preferred_element_type=f32)


def dot_nt(left, right):
    return lax.dot_general(left, right, (((1,), (1,)), ((), ())), preferred_element_type=f32)


def dot_tn(left, right):
    return lax.dot_general(left, right, (((0,), (0,)), ((), ())), preferred_element_type=f32)


def doc_ends(lengths_ref):
    total = lengths_ref[0, 0]
    ends = [total]
    for k in range(1, lengths_ref.shape[1]):
        total = total + lengths_ref[0, k]
        ends.append(total)
    return ends


def segments_of(places, ends):
    count = jnp.zeros(places.shape, jnp.int32)
    for end in ends:
        count = count + (places >= end).astype(jnp.int32)
    return count


def center_scale(values):
    centre = values - jnp.mean(values, axis=-1, keepdims=True)
    spread = jnp.mean(centre * centre, axis=-1, keepdims=True)
    inverse = lax.rsqrt(spread + norm_eps)
    return centre * inverse, inverse


def log_sum_exp(logits, axis):
    top = jnp.max(logits, axis=axis, keepdims=True)
    return top + jnp.log(jnp.sum(jnp.exp(logits - top), axis=axis, keepdims=True))


MESH_ID = pl.DeviceIdType.MESH
AXES = ("dp", "fsdp")
SPLIT = (4, 2, 2, 2)
COPIES = 8


def coordinates():
    dp, fsdp = lax.axis_index("dp"), lax.axis_index("fsdp")
    return dp // 2, dp % 2, fsdp // 2, fsdp % 2


def device_of(z, x, y, c):
    return (z * 2 + x, y * 2 + c)


def z_others(z):
    return (z + 1 - 2 * (z % 2), (z + 2) % 4, 3 - z)


def neighbours():
    z, x, y, c = coordinates()
    others = [device_of(one, x, y, c) for one in z_others(z)]
    return others + [
        device_of(z, 1 - x, y, c), device_of(z, x, 1 - y, c), device_of(z, x, y, 1 - c)
    ]


def meet_neighbours():
    barrier = pltpu.get_barrier_semaphore()
    peers = neighbours()
    for peer in peers:
        pl.semaphore_signal(barrier, inc=1, device_id=peer, device_id_type=MESH_ID)
    pl.semaphore_wait(barrier, len(peers))


def halves(shape):
    if shape[-1] > LANES:
        middle_column = shape[-1] // 2
        return (
            (slice(None), pl.ds(0, middle_column)),
            (slice(None), pl.ds(middle_column, middle_column)),
        )
    middle_row = shape[-2] // 2
    return (
        (pl.ds(0, middle_row), slice(None)),
        (pl.ds(middle_row, middle_row), slice(None)),
    )


def remote(source, target, sems, index, device):
    send, recv = sems
    return pltpu.make_async_remote_copy(
        src_ref=source, dst_ref=target, send_sem=send.at[index], recv_sem=recv.at[index],
        device_id=device, device_id_type=MESH_ID,
    )


def gather_stages(full, sems, base):
    z, x, y, c = coordinates()
    first, second = halves(full.shape)
    every = slice(None)

    def same(index, place, device):
        part = full.at[place]
        return remote(part, part, sems, base + index, device)

    def stage_z():
        return [
            same(k, (z, x, y, c), device_of(one, x, y, c)) for k, one in enumerate(z_others(z))
        ]

    def stage_one():
        return [
            same(3, (every, x, y, c) + first, device_of(z, 1 - x, y, c)),
            same(4, (every, x, y, c) + second, device_of(z, x, 1 - y, c)),
        ]

    def stage_two():
        return [
            same(5, (every, every, y, c) + first, device_of(z, x, 1 - y, c)),
            same(6, (every, x, every, c) + second, device_of(z, 1 - x, y, c)),
        ]

    def stage_core():
        return [same(7, (every, every, every, c), device_of(z, x, y, 1 - c))]

    return [stage_z, stage_one, stage_two, stage_core]


def start_all(copies):
    for copy in copies:
        copy.start()


def wait_all(copies):
    for copy in copies:
        copy.wait()


def one_hot(shape, row_of, column_of):
    rows = lax.broadcasted_iota(jnp.int32, shape, 0)
    columns = lax.broadcasted_iota(jnp.int32, shape, 1)
    return row_of(rows, columns) == column_of(rows, columns)


def norm_place():
    z, x, y, c = coordinates()
    device = (z * 2 + x) * 4 + y * 2 + c
    return device // 8, device % 8


GROUP = 8 * BLOCK


def regroup_matrix(inverse):
    rows = lax.broadcasted_iota(jnp.int32, (GROUP, GROUP), 1 if inverse else 0)
    columns = lax.broadcasted_iota(jnp.int32, (GROUP, GROUP), 0 if inverse else 1)
    hit = (rows // 8 == columns % BLOCK) & (rows % 8 == columns // BLOCK)
    return hit.astype(f32).astype(bf16)


def spread_tokens(stage, matrix, k, part):
    columns = part.shape[1]
    for g in range(part.shape[0] // GROUP):
        place = pl.multiple_of((k * (part.shape[0] // GROUP) + g) * 8, 8)
        moved = dot(matrix, part[g * GROUP : (g + 1) * GROUP])
        stage[:, pl.ds(place, 8), :] = moved.reshape(BLOCK, 8, columns)


def collect_tokens(stage, matrix, k, rows):
    parts = []
    for g in range(rows // GROUP):
        place = pl.multiple_of((k * (rows // GROUP) + g) * 8, 8)
        part = stage[:, pl.ds(place, 8), :].reshape(GROUP, stage.shape[2]).astype(bf16)
        parts.append(dot(matrix, part))
    return jnp.concatenate(parts, axis=0)


class Quiet:
    def __getattr__(self, name):
        return lambda *unused: None


class GatherSteps:
    def __init__(self, proj, up, down, small, sems):
        fulls = (proj, up, down, small)
        self.proj, self.up, self.down, self.small = [
            gather_stages(full, sems, COPIES * b) for b, full in enumerate(fulls)
        ]

    def start(self, plan, step):
        start_all(plan[step]())

    def turn(self, plan, step):
        wait_all(plan[step]())
        if step < 3:
            start_all(plan[step + 1]())

    def begin(self):
        self.start(self.small, 0)
        self.start(self.proj, 0)
        for step in range(4):
            self.turn(self.small, step)
        self.turn(self.proj, 0)

    def half_normed(self):
        self.turn(self.proj, 1)
        self.start(self.up, 0)

    def all_normed(self):
        self.turn(self.proj, 2)

    def before_project(self):
        self.turn(self.proj, 3)
        self.turn(self.up, 0)
        self.start(self.down, 0)

    def project(self, k):
        self.when(k, 2, self.up, 1)
        self.when(k, 5, self.up, 2)
        self.when(k, 6, self.down, 0)

    def sort(self, i):
        self.when(i, 2, self.down, 1)

    def low(self, k):
        self.when(k, 0, self.up, 3)
        self.when(k, 2, self.down, 2)

    def end(self):
        self.turn(self.down, 3)

    def when(self, k, place, plan, step):
        pl.when(k == place)(functools.partial(self.turn, plan, step))


def front_near_kernel(
    lengths_ref, x_ref, proj_own, up_own, down_own, sort_own, norm_own,
    proj, up, down, sort_ref, norms_ref, *rest,
):
    rest, (small, send, recv) = rest[:-3], rest[-3:]
    mine = coordinates()
    proj[mine] = proj_own[...].astype(bf16)
    up[mine] = up_own[...].astype(bf16)
    down[mine] = down_own[...].astype(bf16)
    quarter, eighth = norm_place()
    own = norm_own.shape[1]
    spread = one_hot((own, LANES), lambda r, l: r + eighth * own, lambda r, l: l)
    lanes = dot(norm_own[...].astype(bf16), spread.astype(f32).astype(bf16)).astype(bf16)
    lift = one_hot((16, 4), lambda r, l: r, lambda r, l: l * 4 + quarter)
    tile = dot(lift.astype(f32).astype(bf16), lanes).astype(bf16)
    small[mine] = jnp.concatenate([sort_own[...].astype(bf16), tile], axis=0)
    meet_neighbours()
    steps = GatherSteps(proj, up, down, small, (send, recv))
    steps.begin()
    pieces = small[...].reshape(-1, 32, LANES)
    sort_ref[...] = pieces[:, :16].reshape(sort_ref.shape)
    tile = jnp.sum(pieces[:, 16:].astype(f32), axis=0)
    norms_ref[...] = jnp.concatenate(
        [
            jnp.concatenate([tile[4 * i + q : 4 * i + q + 1] for q in range(4)], axis=1)
            for i in range(4)
        ],
        axis=0,
    )

    def columns_of(columns):
        return proj[:, :, :, :, :, columns].reshape(x_ref.shape[1], -1)

    front_steps(steps, columns_of, lengths_ref, norms_ref, x_ref, sort_ref, *rest)


def front_plain_kernel(lengths_ref, norms_ref, x_ref, proj_ref, sort_ref, *rest):
    front_steps(
        Quiet(), lambda columns: proj_ref[:, columns], lengths_ref, norms_ref, x_ref, sort_ref, *rest
    )


def front_steps(
    steps, proj_columns, lengths_ref, norms_ref, x_ref, sort_ref,
    normed_hbm, qkv_hbm, skv_hbm, tkv_hbm, means_ref, states_ref,
    normed_s, stage, matrix, qkv_buf, low_buf, flip_buf, copy_sem, qkv_sem, low_sem, flip_sem,
):
    seq, width = x_ref.shape
    tiles = seq // TILE
    blocks = seq // BLOCK
    per_tile = TILE // BLOCK
    chunks = 2 * width // LANES
    ends = doc_ends(lengths_ref)
    gain = norms_ref[0:1, :].astype(f32)
    shift = norms_ref[1:2, :].astype(f32)

    def norm_step(k, carry):
        rows = pl.ds(pl.multiple_of(k * TILE, TILE), TILE)
        xhat, unused = center_scale(x_ref[rows, :].astype(f32))
        normed = (xhat * gain + shift).astype(bf16)
        normed_s[rows, :] = normed
        sums = jnp.sum(normed.astype(f32).reshape(per_tile, BLOCK, width), axis=1)
        means_ref[pl.ds(pl.multiple_of(k * per_tile, per_tile), per_tile), :] = (
            sums * (1.0 / BLOCK)
        ).astype(bf16)
        return carry

    lax.fori_loop(0, tiles // 2, norm_step, 0)
    steps.half_normed()
    lax.fori_loop(tiles // 2, tiles, norm_step, 0)
    steps.all_normed()
    normed_copy = pltpu.make_async_copy(normed_s, normed_hbm, copy_sem)
    normed_copy.start()

    logits = dot(means_ref[...], sort_ref[...])
    first_i = segments_of(lax.broadcasted_iota(jnp.int32, (blocks, blocks), 0) * BLOCK, ends)
    first_j = segments_of(lax.broadcasted_iota(jnp.int32, (blocks, blocks), 1) * BLOCK, ends)
    logits = jnp.where(first_i != first_j, logits - mask_penalty, logits)

    def qkv_copy(k, slot):
        rows = pl.ds(pl.multiple_of(k * TILE, TILE), TILE)
        return pltpu.make_async_copy(qkv_buf.at[slot], qkv_hbm.at[rows, :], qkv_sem.at[slot])

    def project_step(k, logits):
        rows = pl.ds(pl.multiple_of(k * TILE, TILE), TILE)
        slot = lax.rem(k, 2)

        @pl.when(k >= 2)
        def _():
            qkv_copy(k - 2, slot).wait()

        steps.project(k)
        logits = logits - log_sum_exp(logits, 1)
        states_ref[2 * k] = jnp.exp(logits)
        logits = logits - log_sum_exp(logits, 0)
        states_ref[2 * k + 1] = jnp.exp(logits)
        normed = normed_s[rows, :]
        qkv_buf[slot, :, :width] = dot(normed, proj_columns(slice(0, width))).astype(bf16)
        product = dot(normed, proj_columns(slice(width, 3 * width))).astype(bf16)
        qkv_buf[slot, :, width:] = product
        spread_tokens(stage, matrix[...], k, product)
        qkv_copy(k, slot).start()
        return logits

    assert tiles == SINK_ITERS
    steps.before_project()
    matrix[...] = regroup_matrix(False)
    lax.fori_loop(0, tiles, project_step, logits)
    permute = states_ref[2 * SINK_ITERS - 1].astype(bf16)

    def flip_copy(t, slot):
        return pltpu.make_async_copy(flip_buf.at[slot], tkv_hbm.at[t], flip_sem.at[slot])

    def sort_step(i, carry):
        group = flip_buf.shape[0]
        steps.sort(i)

        @pl.when(i >= 1)
        def _():
            for u in range(group):
                flip_copy((i - 1) * group + u, u).wait()

        loaded = []
        for u in range(group):
            t = i * group + u
            loaded.append(stage[t].astype(bf16))
        for u in range(group):
            t = i * group + u
            flip_buf[u] = loaded[u].astype(f32).T.astype(bf16)
            flip_copy(t, u).start()
            stage[t] = dot(permute, loaded[u])
        return carry

    group = flip_buf.shape[0]
    lax.fori_loop(0, BLOCK // group, sort_step, 0)

    def low_copy(k, slot):
        rows = pl.ds(pl.multiple_of(k * TILE, TILE), TILE)
        return pltpu.make_async_copy(low_buf.at[slot], skv_hbm.at[rows, :], low_sem.at[slot])

    def low_step(k, carry):
        rows = pl.ds(pl.multiple_of(k * TILE, TILE), TILE)
        slot = lax.rem(k, 2)

        @pl.when(k >= 2)
        def _():
            low_copy(k - 2, slot).wait()

        steps.low(k)
        low_buf[slot] = collect_tokens(stage, matrix[...], k, TILE).astype(bf16)
        low_copy(k, slot).start()
        return carry

    matrix[...] = regroup_matrix(True)
    lax.fori_loop(0, tiles, low_step, 0)
    for u in range(group):
        flip_copy(BLOCK - group + u, u).wait()
    for k in (tiles - 2, tiles - 1):
        qkv_copy(k, k % 2).wait()
        low_copy(k, k % 2).wait()
    normed_copy.wait()
    steps.end()


def front_shapes(seq, width):
    blocks = seq // BLOCK
    hbm = pl.BlockSpec(memory_space=pl.ANY)
    vmem = pl.BlockSpec(memory_space=pltpu.VMEM)
    shapes = (
        jax.ShapeDtypeStruct((seq, width), bf16),
        jax.ShapeDtypeStruct((seq, 3 * width), bf16),
        jax.ShapeDtypeStruct((seq, 2 * width), bf16),
        jax.ShapeDtypeStruct((BLOCK, 2 * width, blocks), bf16),
        jax.ShapeDtypeStruct((blocks, width), bf16),
        jax.ShapeDtypeStruct((2 * SINK_ITERS, blocks, blocks), f32),
    )
    scratch = [
            pltpu.VMEM((seq, width), bf16),
            pltpu.VMEM((BLOCK, blocks, 2 * width), f32),
            pltpu.VMEM((GROUP, GROUP), bf16),
            pltpu.VMEM((2, TILE, 3 * width), bf16),
            pltpu.VMEM((2, TILE, 2 * width), bf16),
            pltpu.VMEM((4, 2 * width, blocks), bf16),
            pltpu.SemaphoreType.DMA,
            pltpu.SemaphoreType.DMA((2,)),
            pltpu.SemaphoreType.DMA((2,)),
            pltpu.SemaphoreType.DMA((8,)),
    ]
    return shapes, [hbm, hbm, hbm, hbm, vmem, vmem], scratch


def front_plain(lengths, x, *shards):
    proj, up, down, sort, norms = gather_plain(*shards)
    shapes, specs, scratch = front_shapes(*x.shape)
    vmem = pl.BlockSpec(memory_space=pltpu.VMEM)
    results = pl.pallas_call(
        front_plain_kernel,
        out_shape=shapes,
        in_specs=[pl.BlockSpec(memory_space=pltpu.SMEM), vmem, vmem, vmem, vmem],
        out_specs=specs,
        scratch_shapes=scratch,
        compiler_params=pltpu.CompilerParams(vmem_limit_bytes=VMEM_LIMIT),
        name="front",
    )(lengths, norms, x, proj, sort)
    return (proj, up, down, sort, norms, *results)


def front_near(lengths, x, proj, up, down, sort, norm):
    seq, width = x.shape
    shapes, specs, scratch = front_shapes(seq, width)
    vmem = pl.BlockSpec(memory_space=pltpu.VMEM)
    fulls = [jax.ShapeDtypeStruct(SPLIT + own.shape, bf16) for own in (proj, up, down)]
    fulls += [jax.ShapeDtypeStruct((32 * sort.shape[0], LANES), bf16)]
    fulls += [jax.ShapeDtypeStruct((4, width), f32)]
    scratch = scratch + [pltpu.VMEM(SPLIT + (32, LANES), bf16)]
    scratch += [pltpu.SemaphoreType.DMA((4 * COPIES,))] * 2
    results = pl.pallas_call(
        front_near_kernel,
        out_shape=tuple(fulls) + shapes,
        in_specs=[pl.BlockSpec(memory_space=pltpu.SMEM)] + [vmem] * 6,
        out_specs=[vmem] * 5 + specs,
        scratch_shapes=scratch,
        compiler_params=pltpu.CompilerParams(
            collective_id=0, has_side_effects=True, vmem_limit_bytes=VMEM_LIMIT
        ),
        name="front",
    )(lengths, x, proj, up, down, sort, norm)
    return tuple(full.reshape(-1, full.shape[-1]) for full in results[:3]) + tuple(results[3:])


def layer_norm_back(grad, gain, xhat, inverse):
    scaled = grad * gain
    mean_one = jnp.mean(scaled, axis=-1, keepdims=True)
    mean_two = jnp.mean(scaled * xhat, axis=-1, keepdims=True)
    return (scaled - mean_one - xhat * mean_two) * inverse


def middle_kernel(
    lengths_ref, norms_ref, x_ref, cot_ref, qkv_ref, skv_ref, out_proj_ref, up_ref, down_ref,
    y_ref, hidden_grad_ref, gq_ref, gkv_ref, gskv_ref, gup_ref, gdown_ref, gout_ref, gnorm_ref,
    gup, gdown, gout, probs_s, context_s, gcontext_s, gq_s, gkv_s, gskv_s, grads_s,
):
    step = pl.program_id(0)
    tile, width = x_ref.shape
    hidden_units = up_ref.shape[1]
    pairs = tile // (2 * BLOCK)
    head_pairs = width // LANES
    scale = HD ** (-0.5)
    ends = doc_ends(lengths_ref)

    @pl.when(step == 0)
    def _():
        gup[...] = jnp.zeros_like(gup)
        gdown[...] = jnp.zeros_like(gdown)
        gout[...] = jnp.zeros_like(gout)
        gnorm_ref[...] = jnp.zeros_like(gnorm_ref)

    lane = lax.broadcasted_iota(jnp.int32, (1, LANES), 1)
    low_head = lane < HD
    low_block = lax.rem(lane, 2 * BLOCK) < BLOCK
    head_one = low_head.astype(f32).astype(bf16)
    head_two = (1.0 - low_head.astype(f32)).astype(bf16)
    block_one = low_block.astype(f32).astype(bf16)
    block_two = (1.0 - low_block.astype(f32)).astype(bf16)

    def two_heads(part):
        return jnp.concatenate(
            [part * head_one, part * head_two], axis=0
        )

    def two_blocks(part):
        return jnp.concatenate(
            [part * block_one, part * block_two], axis=0
        )

    def stack_keys(own, far):
        return jnp.concatenate(
            [own[:BLOCK], far[:BLOCK], own[BLOCK:], far[BLOCK:]], axis=0
        )

    def pick_block(full):
        return jnp.where(low_block, full[: 2 * BLOCK], full[2 * BLOCK :])

    def pick_head(full):
        return jnp.where(low_head, full[: 2 * BLOCK], full[2 * BLOCK :])

    def attend(p, carry):
        rows = pl.ds(pl.multiple_of(p * 2 * BLOCK, 2 * BLOCK), 2 * BLOCK)
        base = step * tile + p * 2 * BLOCK
        query_seg = segments_of(base + lax.rem(lane, 2 * BLOCK), ends)
        key_place = (
            base
            + jnp.where(low_block, 0, BLOCK)
            + lax.broadcasted_iota(jnp.int32, (BLOCK, LANES), 0)
        )
        same = segments_of(key_place, ends) == query_seg
        for hp in range(head_pairs):
            cols = slice(hp * LANES, (hp + 1) * LANES)
            key_cols = slice(width + hp * LANES, width + (hp + 1) * LANES)
            value_cols = slice(2 * width + hp * LANES, 2 * width + (hp + 1) * LANES)
            queries = two_heads(qkv_ref[rows, cols])
            keys = stack_keys(qkv_ref[rows, key_cols], skv_ref[rows, cols])
            values = stack_keys(qkv_ref[rows, value_cols], skv_ref[rows, key_cols])
            scores = pick_block(dot(keys, queries.astype(f32).T.astype(bf16))) * scale
            scores = jnp.concatenate(
                [jnp.where(same, scores[:BLOCK], score_floor), scores[BLOCK:]], axis=0
            )
            exps = jnp.exp(scores - jnp.max(scores, axis=0, keepdims=True))
            probs = (exps / jnp.sum(exps, axis=0, keepdims=True)).astype(bf16)
            probs_s[p * head_pairs + hp] = probs
            context_s[rows, cols] = pick_head(dot_tn(two_blocks(probs), values)).astype(bf16)
        return carry

    lax.fori_loop(0, pairs, attend, 0, unroll=8)

    inputs = x_ref[...].astype(f32)
    context = context_s[...]
    hidden = inputs + dot(context, out_proj_ref[...])
    xhat_two, inverse_two = center_scale(hidden)
    gain_two = norms_ref[2:3, :].astype(f32)
    normed_two = (xhat_two * gain_two + norms_ref[3:4, :].astype(f32)).astype(bf16)
    normed_two_t = normed_two.T
    cot = cot_ref[...]
    total_out = hidden
    grad_normed_two = None
    root = 0.7978845608028654
    for c in range(hidden_units // TILE):
        cols = slice(c * TILE, (c + 1) * TILE)
        pre = dot(normed_two, up_ref[:, cols])
        grad_act = dot_nt(cot, down_ref[cols, :])
        square = pre * pre
        half_tanh = 0.5 + 0.5 * jnp.tanh(pre * (root + (root * 0.044715) * square))
        act = pre * half_tanh
        slope = half_tanh + act * (1.0 - half_tanh) * (
            2.0 * root + (6.0 * root * 0.044715) * square
        )
        act = act.astype(bf16)
        grad_pre = (grad_act * slope).astype(bf16)
        total_out = total_out + dot(act, down_ref[cols, :])
        back = dot_nt(grad_pre, up_ref[:, cols])
        grad_normed_two = back if grad_normed_two is None else grad_normed_two + back
        gup[:, cols] += dot(normed_two_t, grad_pre)
        gdown[cols, :] += dot_tn(act, cot)
    y_ref[...] = total_out.astype(bf16)
    gnorm_ref[0:1, :] += jnp.sum(grad_normed_two * xhat_two, axis=0, keepdims=True)
    gnorm_ref[1:2, :] += jnp.sum(grad_normed_two, axis=0, keepdims=True)
    hidden_grad = cot.astype(f32) + layer_norm_back(
        grad_normed_two, gain_two, xhat_two, inverse_two
    )
    hidden_grad_ref[...] = hidden_grad
    grad_attn = hidden_grad.astype(bf16)
    gout[...] += dot_tn(context, grad_attn)
    gcontext_s[...] = dot_nt(grad_attn, out_proj_ref[...]).astype(bf16)

    def attend_back(p, carry):
        rows = pl.ds(pl.multiple_of(p * 2 * BLOCK, 2 * BLOCK), 2 * BLOCK)
        for hp in range(head_pairs):
            cols = slice(hp * LANES, (hp + 1) * LANES)
            key_cols = slice(width + hp * LANES, width + (hp + 1) * LANES)
            value_cols = slice(2 * width + hp * LANES, 2 * width + (hp + 1) * LANES)
            values = stack_keys(qkv_ref[rows, value_cols], skv_ref[rows, key_cols])
            gcontext = two_heads(gcontext_s[rows, cols])
            wide = probs_s[p * head_pairs + hp].astype(f32)
            grad_probs = pick_block(dot(values, gcontext.astype(f32).T.astype(bf16)))
            weighted = wide * grad_probs
            grad_scores = weighted - wide * jnp.sum(weighted, axis=0, keepdims=True)
            grad_scores = (grad_scores * scale).astype(bf16)
            grads_s[p * head_pairs + hp] = grad_scores
        return carry

    lax.fori_loop(0, pairs, attend_back, 0, unroll=8)

    def attend_last(p, carry):
        rows = pl.ds(pl.multiple_of(p * 2 * BLOCK, 2 * BLOCK), 2 * BLOCK)
        for hp in range(head_pairs):
            cols = slice(hp * LANES, (hp + 1) * LANES)
            key_cols = slice(width + hp * LANES, width + (hp + 1) * LANES)
            value_cols = slice(2 * width + hp * LANES, 2 * width + (hp + 1) * LANES)
            keys = stack_keys(qkv_ref[rows, key_cols], skv_ref[rows, cols])
            gq_s[rows, cols] = pick_head(dot_tn(two_blocks(grads_s[p * head_pairs + hp]), keys)).astype(bf16)
            gkeys = dot(two_blocks(grads_s[p * head_pairs + hp]), two_heads(qkv_ref[rows, cols])).astype(bf16)
            gvalues = dot(two_blocks(probs_s[p * head_pairs + hp]), two_heads(gcontext_s[rows, cols])).astype(bf16)
            for grads, where in ((gkeys, cols), (gvalues, key_cols)):
                gkv_s[rows, where] = jnp.concatenate(
                    [grads[:BLOCK], grads[2 * BLOCK : 3 * BLOCK]], axis=0
                )
                gskv_s[rows, where] = jnp.concatenate(
                    [grads[BLOCK : 2 * BLOCK], grads[3 * BLOCK :]], axis=0
                )
        return carry

    lax.fori_loop(0, pairs, attend_last, 0, unroll=8)
    gq_ref[...] = gq_s[...]
    gkv_ref[...] = gkv_s[...]
    gskv_ref[...] = gskv_s[...]

    @pl.when(step == pl.num_programs(0) - 1)
    def _():
        gup_ref[...] = gup[...].astype(bf16)
        gdown_ref[...] = gdown[...].astype(bf16)
        gout_ref[...] = gout[...].astype(bf16)


def middle(lengths, norms, x, cot, qkv, skv, proj, up, down):
    seq, width = x.shape
    hidden_units = up.shape[1]
    tiles = seq // TILE

    def rows(columns):
        return pl.BlockSpec((TILE, columns), lambda i: (i, 0))

    def fixed(shape, index=(0, 0)):
        return pl.BlockSpec(shape, lambda i: index, pipeline_mode=pl.Buffered(1))

    return pl.pallas_call(
        middle_kernel,
        grid=(tiles,),
        out_shape=(
            jax.ShapeDtypeStruct((seq, width), bf16),
            jax.ShapeDtypeStruct((seq, width), f32),
            jax.ShapeDtypeStruct((seq, width), bf16),
            jax.ShapeDtypeStruct((seq, 2 * width), bf16),
            jax.ShapeDtypeStruct((seq, 2 * width), bf16),
            jax.ShapeDtypeStruct((width, hidden_units), bf16),
            jax.ShapeDtypeStruct((hidden_units, width), bf16),
            jax.ShapeDtypeStruct((width, width), bf16),
            jax.ShapeDtypeStruct((2, width), f32),
        ),
        in_specs=[
            pl.BlockSpec(memory_space=pltpu.SMEM),
            fixed(norms.shape),
            rows(width),
            rows(width),
            rows(3 * width),
            rows(2 * width),
            fixed((width, width), (0, 3)),
            fixed(up.shape),
            fixed(down.shape),
        ],
        out_specs=[
            rows(width),
            rows(width),
            rows(width),
            rows(2 * width),
            rows(2 * width),
            fixed((width, hidden_units)),
            fixed((hidden_units, width)),
            fixed((width, width)),
            fixed((2, width)),
        ],
        scratch_shapes=[
            pltpu.VMEM((width, hidden_units), f32),
            pltpu.VMEM((hidden_units, width), f32),
            pltpu.VMEM((width, width), f32),
            pltpu.VMEM((TILE // (2 * BLOCK) * (width // LANES), 2 * BLOCK, LANES), bf16),
            pltpu.VMEM((TILE, width), bf16),
            pltpu.VMEM((TILE, width), bf16),pltpu.VMEM((TILE, width), bf16),pltpu.VMEM((TILE, 2*width), bf16),pltpu.VMEM((TILE, 2*width), bf16),
            pltpu.VMEM((TILE // (2 * BLOCK) * (width // LANES), 2 * BLOCK, LANES), bf16),
        ],
        compiler_params=pltpu.CompilerParams(vmem_limit_bytes=VMEM_LIMIT),
        name="middle",
    )(lengths, norms, x, cot, qkv, skv, proj, up, down)


def add_low(*parts):
    total = parts[0].astype(f32)
    for part in parts[1:]:
        total = total + part.astype(f32)
    return total


class Reduce:
    def __init__(self, part, total, columns, got_c, got_a, got_b, got_two, got_z, sems, base):
        self.part, self.total, self.columns = part, total, columns
        self.got_c, self.got_a, self.got_b = got_c, got_a, got_b
        self.got_two, self.got_z, self.sems, self.base = got_two, got_z, sems, base
        self.first, self.second = halves(part.shape)

    def copies(self, step):
        z, x, y, c = coordinates()
        every = slice(None)
        to_x, to_y = device_of(z, 1 - x, y, c), device_of(z, x, 1 - y, c)

        def one(source, target, index, device):
            return remote(source, target, self.sems, self.base + index, device)

        if step == 0:
            away = self.part.at[every, every, every, 1 - c]
            return [one(away, self.got_c, 0, device_of(z, x, y, 1 - c))]
        if step == 1:
            away_a = self.got_c.at[(every, every, 1 - y) + self.first]
            away_b = self.got_c.at[(every, 1 - x, every) + self.second]
            return [one(away_a, self.got_a, 1, to_y), one(away_b, self.got_b, 2, to_x)]
        if step == 2:
            away_a, away_b = self.got_a.at[every, 1 - x], self.got_b.at[every, 1 - y]
            return [
                one(away_a, self.got_two.at[(every,) + self.first], 3, to_x),
                one(away_b, self.got_two.at[(every,) + self.second], 4, to_y),
            ]
        return [
            one(self.got_two.at[other], self.got_z.at[k], 5 + k, device_of(other, x, y, c))
            for k, other in enumerate(z_others(z))
        ]

    def start(self, step):
        start_all(self.copies(step))

    def turn(self, step):
        wait_all(self.copies(step))
        self.add(step)
        if step < 3:
            self.start(step + 1)

    def add(self, step):
        z, x, y, c = coordinates()
        if step == 3:
            self.total[:, self.columns] = add_low(
                self.got_two[z], *[self.got_z[k] for k in range(3)]
            )
            return

        def line(i, carry):
            if step == 0:
                for j in range(2):
                    for k in range(2):
                        self.got_c[i, j, k] = add_low(
                            self.part[i, j, k, c], self.got_c[i, j, k]
                        ).astype(bf16)
            elif step == 1:
                for j in range(2):
                    self.got_a[i, j] = add_low(
                        self.got_c[(i, j, y) + self.first], self.got_a[i, j]
                    ).astype(bf16)
                    self.got_b[i, j] = add_low(
                        self.got_c[(i, x, j) + self.second], self.got_b[i, j]
                    ).astype(bf16)
            else:
                self.got_two[(i,) + self.first] = add_low(
                    self.got_a[i, x], self.got_two[(i,) + self.first]
                ).astype(bf16)
                self.got_two[(i,) + self.second] = add_low(
                    self.got_b[i, y], self.got_two[(i,) + self.second]
                ).astype(bf16)
            return carry

        lax.fori_loop(0, 4, line, 0)


def reduce_scratch(rows, columns):
    half = (rows, columns // 2) if columns > LANES else (rows // 2, columns)
    shapes = (
        (4, 2, 2, rows, columns), (4, 2) + half, (4, 2) + half, (4, rows, columns),
        (3, rows, columns),
    )
    return [pltpu.VMEM(shape, bf16) for shape in shapes]


class ReduceSteps:
    def __init__(self, qkv, out, up, down, small):
        self.qkv, self.out, self.up, self.down, self.small = qkv, out, up, down, small

    def begin(self):
        self.up.start(0)
        self.down.start(0)
        self.out.start(0)

    def loaded(self):
        self.up.turn(0)

    def sort(self, i):
        self.when(i, 5, self.up, 1)
        self.when(i, 6, self.down, 0)

    def swept(self):
        self.up.turn(2)

    def first(self, k):
        self.when(k, 1, self.down, 1)
        self.when(k, 2, self.out, 0)
        self.when(k, 4, self.down, 2)
        self.when(k, 6, self.up, 3)
        self.when(k, 7, self.out, 1)

    def between(self):
        self.qkv.start(0)
        self.out.turn(2)

    def second(self, k):
        self.when(k, 1, self.down, 3)
        self.when(k, 2, self.qkv, 0)
        self.when(k, 3, self.out, 3)
        self.when(k, 6, self.qkv, 1)

    def when(self, k, place, plan, step):
        pl.when(k == place)(functools.partial(plan.turn, step))


def norm_rows(grads):
    rows = []
    for grad in grads:
        for i in range(grad.shape[0]):
            for q in range(grad.shape[1] // LANES):
                rows.append(grad[i : i + 1, q * LANES : (q + 1) * LANES])
    return jnp.concatenate(rows, axis=0)


def back_plain_kernel(*refs):
    back_steps(Quiet(), *refs)


def back_near_kernel(*refs):
    ins, refs = refs[:12], refs[12:]
    (gout, gup, gdown, gnorm_two), refs = refs[:4], refs[4:]
    (gx_hbm, gsum_hbm, proj_sum, up_sum, down_sum, sort_sum, norm_sum), refs = refs[:7], refs[7:]
    work, refs = refs[:9], refs[9:]
    (gqkv, gsort, gnorm, small, small_sum, send, recv), scratch = refs[:7], refs[7:]
    width = gsort.shape[0]
    sems = (send, recv)
    every = slice(None)
    places = (
        (gqkv, proj_sum, pl.ds(0, 3 * width)), (gout, proj_sum, pl.ds(3 * width, width)),
        (gup, up_sum, every), (gdown, down_sum, every), (small, small_sum, every),
    )
    steps = ReduceSteps(
        *[
            Reduce(part, total, columns, *scratch[5 * b : 5 * b + 5], sems, COPIES * b)
            for b, (part, total, columns) in enumerate(places)
        ]
    )
    meet_neighbours()
    back_steps(steps, *ins, gx_hbm, gsum_hbm, gqkv, gsort, gnorm, *work)
    tile = norm_rows((gnorm[...], gnorm_two[...])).astype(bf16)
    shards = gsort[...].astype(bf16).reshape(SPLIT + (width // 32, LANES))
    small[:, :, :, :, :16] = shards
    for i in range(4):
        for j in range(2):
            for k in range(2):
                for m in range(2):
                    small[i, j, k, m, 16:] = tile
    steps.small.start(0)
    steps.small.turn(0)
    steps.qkv.turn(2)
    for step in range(1, 4):
        steps.small.turn(step)
    steps.qkv.turn(3)
    sort_sum[...] = small_sum[:16, :]
    quarter, eighth = norm_place()
    own = norm_sum.shape[1]
    drop = one_hot((4, 16), lambda r, l: r * 4 + quarter, lambda r, l: l).astype(f32)
    pick = one_hot((LANES, own), lambda r, l: r, lambda r, l: l + eighth * own).astype(f32)

    def exact(left, right):
        return lax.dot_general(
            left, right, (((1,), (0,)), ((), ())),
            precision=lax.Precision.HIGHEST, preferred_element_type=f32,
        )

    norm_sum[...] = exact(exact(drop, small_sum[16:, :]), pick)


def back_steps(
    steps, norms_ref, gskv_hbm, tkv_hbm, states_ref, means_ref, proj_ref, sort_ref,
    x_hbm, normed_hbm, hidden_grad_hbm, gq_hbm, gkv_hbm,
    gx_hbm, gsum_hbm, gproj_ref, gsort_ref, gnorm_ref,
    stage, matrix, low_buf, flip_buf, gproj, gperm, gmeans, low_sem, flip_sem,
):
    steps.begin()
    seq, width = x_hbm.shape
    tiles = seq // TILE
    blocks = seq // BLOCK
    chunks = 2 * width // LANES
    per_tile = TILE // BLOCK

    def low_copy(k, slot):
        rows = pl.ds(pl.multiple_of(k * TILE, TILE), TILE)
        return pltpu.make_async_copy(gskv_hbm.at[rows, :], low_buf.at[slot], low_sem.at[slot])

    group = flip_buf.shape[0] // 2

    def flip_copy(t, slot):
        return pltpu.make_async_copy(tkv_hbm.at[t], flip_buf.at[slot], flip_sem.at[slot])

    low_copy(0, 0).start()
    low_copy(1, 1).start()
    for u in range(group):
        flip_copy(u, u).start()

    def load_step(k, carry):
        rows = pl.ds(pl.multiple_of(k * TILE, TILE), TILE)
        slot = lax.rem(k, 2)
        low_copy(k, slot).wait()
        spread_tokens(stage, matrix[...], k, low_buf[slot])

        @pl.when(k + 2 < tiles)
        def _():
            low_copy(k + 2, slot).start()

        return carry

    matrix[...] = regroup_matrix(False)
    lax.fori_loop(0, tiles, load_step, 0)
    matrix[...] = regroup_matrix(True)
    steps.loaded()

    final = states_ref[2 * SINK_ITERS - 1]
    permute_t = final.T.astype(bf16)
    gperm[...] = jnp.zeros_like(gperm)

    def sort_step(i, carry):
        side = lax.rem(i, 2) * group
        steps.sort(i)

        @pl.when(i + 1 < BLOCK // group)
        def _():
            for u in range(group):
                flip_copy((i + 1) * group + u, group - side + u).start()

        for u in range(group):
            flip_copy(i * group + u, side + u).wait()
        loaded = []
        for u in range(group):
            t = i * group + u
            loaded.append(stage[t].astype(bf16))
        total = gperm[...]
        for u in range(group):
            t = i * group + u
            total = total + dot(loaded[u], flip_buf[side + u])
            stage[t] = dot(permute_t, loaded[u])
        gperm[...] = total
        return carry

    lax.fori_loop(0, BLOCK // group, sort_step, 0)

    grad = gperm[...] * final
    for sweep in reversed(range(SINK_ITERS)):
        grad = grad - states_ref[2 * sweep + 1] * jnp.sum(grad, axis=0, keepdims=True)
        grad = grad - states_ref[2 * sweep] * jnp.sum(grad, axis=1, keepdims=True)
    grad = grad.astype(bf16)
    gsort_ref[...] = dot_tn(means_ref[...], grad).astype(gsort_ref.dtype)
    gmeans[...] = dot_nt(grad, sort_ref[...]) * (1.0 / BLOCK)
    steps.swept()
    gproj[...] = jnp.zeros_like(gproj)
    gnorm_ref[...] = jnp.zeros_like(gnorm_ref)
    gain = norms_ref[0:1, :].astype(f32)

    def weight_step(normed_ref, gq_ref, gkv_ref, gsum_ref):
        k = pl.program_id(0)
        steps.first(k)
        far = collect_tokens(stage, matrix[...], k, TILE)
        gkv = (gkv_ref[...].astype(f32) + far).astype(bf16)
        gsum_ref[...] = gkv
        normed = normed_ref[...]
        gproj[:, :width] += dot_tn(normed, gq_ref[...])
        gproj[:, width:] += dot_tn(normed, gkv)

    def input_step(x_ref, hidden_grad_ref, gq_ref, gsum_ref, gx_ref):
        k = pl.program_id(0)
        steps.second(k)
        gq, gkv = gq_ref[...], gsum_ref[...]
        grad_normed = dot_nt(gq, proj_ref[:, :width]) + dot_nt(gkv, proj_ref[:, width : 3 * width])
        means = gmeans[pl.ds(pl.multiple_of(k * per_tile, per_tile), per_tile), :]
        grad_normed = grad_normed + jnp.broadcast_to(
            means[:, None, :], (per_tile, BLOCK, width)
        ).reshape(TILE, width)
        xhat, inverse = center_scale(x_ref[...].astype(f32))
        gnorm_ref[0:1, :] += jnp.sum(grad_normed * xhat, axis=0, keepdims=True)
        gnorm_ref[1:2, :] += jnp.sum(grad_normed, axis=0, keepdims=True)
        gx_ref[...] = hidden_grad_ref[...] + layer_norm_back(grad_normed, gain, xhat, inverse)

    def rows_of(columns):
        return pl.BlockSpec((TILE, columns), lambda i: (i, 0))

    pltpu.emit_pipeline(
        weight_step,
        grid=(tiles,),
        in_specs=[rows_of(width)] * 2 + [rows_of(2 * width)],
        out_specs=[rows_of(2 * width)],
    )(normed_hbm, gq_hbm, gkv_hbm, gsum_hbm)
    gproj_ref[...] = gproj[...].astype(bf16).reshape(gproj_ref.shape)
    steps.between()
    pltpu.emit_pipeline(
        input_step,
        grid=(tiles,),
        in_specs=[rows_of(width)] * 3 + [rows_of(2 * width)],
        out_specs=[rows_of(width)],
    )(x_hbm, hidden_grad_hbm, gq_hbm, gsum_hbm, gx_hbm)


def back_scratch(seq, width):
    blocks = seq // BLOCK
    return [
            pltpu.VMEM((BLOCK, blocks, 2 * width), f32),
            pltpu.VMEM((GROUP, GROUP), bf16),
            pltpu.VMEM((2, TILE, 2 * width), bf16),
            pltpu.VMEM((8, 2 * width, blocks), bf16),
            pltpu.VMEM((width, 3 * width), f32),
            pltpu.VMEM((blocks, blocks), f32),
            pltpu.VMEM((blocks, width), f32),
            pltpu.SemaphoreType.DMA((2,)),
            pltpu.SemaphoreType.DMA((8,)),
    ]


def back_plain(ins, gout, gup, gdown, gnorm_two):
    seq, width = ins[7].shape
    blocks = seq // BLOCK
    hbm = pl.BlockSpec(memory_space=pl.ANY)
    vmem = pl.BlockSpec(memory_space=pltpu.VMEM)
    gx, unused, gqkv, gsort, gnorm_one = pl.pallas_call(
        back_plain_kernel,
        out_shape=(
            jax.ShapeDtypeStruct((seq, width), f32),
            jax.ShapeDtypeStruct((seq, 2 * width), bf16),
            jax.ShapeDtypeStruct((width, 3 * width), bf16),
            jax.ShapeDtypeStruct((width, blocks), f32),
            jax.ShapeDtypeStruct((2, width), f32),
        ),
        in_specs=[vmem, hbm, hbm, vmem, vmem, vmem, vmem, hbm, hbm, hbm, hbm, hbm],
        out_specs=[hbm, hbm, vmem, vmem, vmem],
        scratch_shapes=back_scratch(seq, width),
        compiler_params=pltpu.CompilerParams(vmem_limit_bytes=VMEM_LIMIT),
        name="back",
    )(*ins)
    return gx, *reduce_plain(gqkv, gout, gup, gdown, gsort, gnorm_one, gnorm_two)


def back_near(ins, gout, gup, gdown, gnorm_two):
    seq, width = ins[7].shape
    blocks = seq // BLOCK
    hbm = pl.BlockSpec(memory_space=pl.ANY)
    vmem = pl.BlockSpec(memory_space=pltpu.VMEM)

    def split(grad):
        return grad.reshape(SPLIT + (grad.shape[0] // 32, grad.shape[1]))

    gout, gup, gdown = split(gout), split(gup), split(gdown)
    rows = width // 32
    small = (32, LANES)
    qkv = (rows, 3 * width)
    scratch = back_scratch(seq, width) + [
        pltpu.VMEM(SPLIT + qkv, bf16),
        pltpu.VMEM((width, blocks), f32),
        pltpu.VMEM((2, width), f32),
        pltpu.VMEM(SPLIT + small, bf16),
        pltpu.VMEM(small, f32),
    ]
    scratch += [pltpu.SemaphoreType.DMA((5 * COPIES,))] * 2
    for shape in (qkv, gout.shape[-2:], gup.shape[-2:], gdown.shape[-2:], small):
        scratch += reduce_scratch(*shape)
    sums = [(rows, 4 * width), gup.shape[-2:], gdown.shape[-2:], (rows, blocks), (4, rows)]
    gx, unused, *totals = pl.pallas_call(
        back_near_kernel,
        out_shape=(
            jax.ShapeDtypeStruct((seq, width), f32),
            jax.ShapeDtypeStruct((seq, 2 * width), bf16),
            *[jax.ShapeDtypeStruct(shape, f32) for shape in sums],
        ),
        in_specs=[vmem, hbm, hbm, vmem, vmem, vmem, vmem, hbm, hbm, hbm, hbm, hbm] + [vmem] * 4,
        out_specs=[hbm, hbm] + [vmem] * 5,
        scratch_shapes=scratch,
        compiler_params=pltpu.CompilerParams(
            collective_id=1, has_side_effects=True, vmem_limit_bytes=VMEM_LIMIT
        ),
        name="back",
    )(*ins, gout, gup, gdown, gnorm_two)
    return gx, *totals


def adamw(master, first, second, grad, rate, decay):
    first_new = beta_first * first + (1.0 - beta_first) * grad
    second_new = beta_second * second + (1.0 - beta_second) * grad * grad
    first_hat = first_new / (1.0 - beta_first**STEP)
    second_hat = second_new / (1.0 - beta_second**STEP)
    master_new = master - rate * (first_hat / (jnp.sqrt(second_hat) + adam_eps) + decay * master)
    return (master_new, first_new, second_new)


RATES = (
    (rate_matrix, weight_decay), (rate_matrix, weight_decay), (rate_matrix, weight_decay),
    (rate_other, weight_decay), (rate_other, 0.0),
)


def update_kernel(*refs):
    sums, states, results = refs[:5], refs[5:20], refs[20:]
    for b, (rate, decay) in enumerate(RATES):
        state = [ref[...] for ref in states[3 * b : 3 * b + 3]]
        for ref, value in zip(
            results[3 * b : 3 * b + 3], adamw(*state, sums[b][...], rate, decay)
        ):
            ref[...] = value


def update(sums, states):
    vmem = pl.BlockSpec(memory_space=pltpu.VMEM)
    return pl.pallas_call(
        update_kernel,
        out_shape=tuple(jax.ShapeDtypeStruct(state.shape, f32) for state in states),
        in_specs=[vmem] * 20,
        out_specs=[vmem] * 15,
        compiler_params=pltpu.CompilerParams(vmem_limit_bytes=VMEM_LIMIT),
        name="update",
    )(*sums, *states)


def gather_plain(proj, up, down, sort, norm):
    def gathered(shard, axis):
        return lax.all_gather(shard.astype(bf16), AXES, axis=axis, tiled=True)

    return (*(gathered(shard, 0) for shard in (proj, up, down, sort)), gathered(norm, 1))


def reduce_plain(gqkv, gout, gup, gdown, gsort, gone, gtwo):
    def summed(grad, axis):
        return lax.psum_scatter(
            grad.astype(f32), AXES, scatter_dimension=axis, tiled=True
        )

    gproj = jnp.concatenate([gqkv, gout], axis=1)
    gnorm = jnp.concatenate([gone, gtwo], axis=0)
    return (*(summed(grad, 0) for grad in (gproj, gup, gdown, gsort)), summed(gnorm, 1))


def body(near, layer_input, doc_lengths, out_cotangent, *states):
    x = layer_input[0]
    cot = out_cotangent[0]
    proj, up, down, sort, norms, normed, qkv, skv, tkv, means, kept = (
        front_near if near else front_plain
    )(doc_lengths, x, *states[::3])
    y, hidden_grad, gq, gkv, gskv, gup, gdown, gout, gnorm_two = middle(
        doc_lengths, norms, x, cot, qkv, skv, proj, up, down
    )
    ins = (norms, gskv, tkv, kept, means, proj, sort, x, normed, hidden_grad, gq, gkv)
    gx, *sums = (back_near if near else back_plain)(ins, gout, gup, gdown, gnorm_two)
    return (y[None], gx[None], *update(sums, states))


def solution(mesh):
    rows3, rows2, columns = P(AXES, None, None), P(AXES, None), P(None, AXES)
    near = (mesh.shape["dp"], mesh.shape["fsdp"]) == (8, 4)
    return jax.shard_map(
        functools.partial(body, near),
        mesh=mesh,
        in_specs=(rows3, rows2, rows3) + (rows2,) * 12 + (columns,) * 3,
        out_specs=(rows3, rows3) + (rows2,) * 12 + (columns,) * 3,
        check_vma=False,
    )
```

```python
import functools
import jax
import jax.numpy as jnp
from jax import lax
from jax.experimental import pallas as pl
from jax.experimental.pallas import tpu as pltpu
from jax.sharding import PartitionSpec as P

HD = 64
BLOCK = 32
SINK_ITERS = 8
STEP = 10
TILE = 512
LANES = 128

mask_penalty = 6.0
score_floor = -1000000000.0
norm_eps = 1e-05
beta_first = 0.9
beta_second = 0.95
adam_eps = 1e-08
weight_decay = 0.1
rate_matrix = 0.1
rate_other = 0.5

bf16 = jnp.bfloat16
f32 = jnp.float32
VMEM_LIMIT = 62 * 2**20


def dot(left, right):
    return lax.dot_general(left, right, (((1,), (0,)), ((), ())), preferred_element_type=f32)


def dot_nt(left, right):
    return lax.dot_general(left, right, (((1,), (1,)), ((), ())), preferred_element_type=f32)


def dot_tn(left, right):
    return lax.dot_general(left, right, (((0,), (0,)), ((), ())), preferred_element_type=f32)


def doc_ends(lengths_ref):
    total = lengths_ref[0, 0]
    ends = [total]
    for k in range(1, lengths_ref.shape[1]):
        total = total + lengths_ref[0, k]
        ends.append(total)
    return ends


def segments_of(places, ends):
    count = jnp.zeros(places.shape, jnp.int32)
    for end in ends:
        count = count + (places >= end).astype(jnp.int32)
    return count


def center_scale(values):
    centre = values - jnp.mean(values, axis=-1, keepdims=True)
    spread = jnp.mean(centre * centre, axis=-1, keepdims=True)
    inverse = lax.rsqrt(spread + norm_eps)
    return centre * inverse, inverse


def log_sum_exp(logits, axis):
    top = jnp.max(logits, axis=axis, keepdims=True)
    return top + jnp.log(jnp.sum(jnp.exp(logits - top), axis=axis, keepdims=True))


MESH_ID = pl.DeviceIdType.MESH
AXES = ("dp", "fsdp")
SPLIT = (4, 2, 2, 2)
COPIES = 8


def coordinates():
    dp, fsdp = lax.axis_index("dp"), lax.axis_index("fsdp")
    return dp // 2, dp % 2, fsdp // 2, fsdp % 2


def device_of(z, x, y, c):
    return (z * 2 + x, y * 2 + c)


def z_others(z):
    return (z + 1 - 2 * (z % 2), (z + 2) % 4, 3 - z)


def xy_others(x, y):
    return ((1 - x, y), (x, 1 - y), (1 - x, 1 - y))


def neighbours():
    z, x, y, c = coordinates()
    return (
        [device_of(one, x, y, c) for one in z_others(z)]
        + [device_of(z, *one, c) for one in xy_others(x, y)]
        + [device_of(z, x, y, 1 - c)]
    )


def greet_neighbours():
    for peer in neighbours():
        pl.semaphore_signal(
            pltpu.get_barrier_semaphore(), inc=1, device_id=peer, device_id_type=MESH_ID
        )


def await_neighbours():
    pl.semaphore_wait(pltpu.get_barrier_semaphore(), len(neighbours()))


def remote(source, target, sems, index, device):
    send, recv = sems
    return pltpu.make_async_remote_copy(
        src_ref=source, dst_ref=target, send_sem=send.at[index], recv_sem=recv.at[index],
        device_id=device, device_id_type=MESH_ID,
    )


def gather_stages(full, sems, base, start=0, size=None):
    z, x, y, c = coordinates()
    whole = (slice(None), pl.ds(start, size or full.shape[-1]))
    every = slice(None)

    def same(index, place, device):
        part = full.at[place + whole]
        return remote(part, part, sems, base + index, device)

    def stage_z():
        return [
            same(k, (z, x, y, c), device_of(one, x, y, c)) for k, one in enumerate(z_others(z))
        ]

    def stage_xy():
        return [
            same(3 + k, (every, x, y, c), device_of(z, *one, c))
            for k, one in enumerate(xy_others(x, y))
        ]

    def stage_core():
        return [same(6, (every, every, every, c), device_of(z, x, y, 1 - c))]

    return [stage_z, stage_xy, stage_core]


def gather_by_halves(full, sems, base, start=0, size=None):
    z, x, y, c = coordinates()
    size = size or full.shape[-1]
    every = slice(None)
    first = (every, pl.ds(start, size // 2))
    second = (every, pl.ds(start + size // 2, size // 2))
    whole = (every, pl.ds(start, size))
    to_x, to_y = device_of(z, 1 - x, y, c), device_of(z, x, 1 - y, c)

    def same(index, place, device):
        part = full.at[place]
        return remote(part, part, sems, base + index, device)

    def stage_z():
        return [
            same(k, (z, x, y, c) + whole, device_of(one, x, y, c))
            for k, one in enumerate(z_others(z))
        ]

    def stage_one():
        return [
            same(3, (every, x, y, c) + first, to_x), same(4, (every, x, y, c) + second, to_y)
        ]

    def stage_two():
        return [
            same(5, (every, every, y, c) + first, to_y),
            same(6, (every, x, every, c) + second, to_x),
        ]

    def stage_core():
        return [same(7, (every, every, every, c) + whole, device_of(z, x, y, 1 - c))]

    return [stage_z, stage_one, stage_two, stage_core]


def start_all(copies):
    for copy in copies:
        copy.start()


def wait_all(copies):
    for copy in copies:
        copy.wait()


def one_hot(shape, row_of, column_of):
    rows = lax.broadcasted_iota(jnp.int32, shape, 0)
    columns = lax.broadcasted_iota(jnp.int32, shape, 1)
    return row_of(rows, columns) == column_of(rows, columns)


def norm_place():
    z, x, y, c = coordinates()
    device = (z * 2 + x) * 4 + y * 2 + c
    return device // 8, device % 8


GROUP = 8 * BLOCK


def regroup_matrix(inverse):
    rows = lax.broadcasted_iota(jnp.int32, (GROUP, GROUP), 1 if inverse else 0)
    columns = lax.broadcasted_iota(jnp.int32, (GROUP, GROUP), 0 if inverse else 1)
    hit = (rows // 8 == columns % BLOCK) & (rows % 8 == columns // BLOCK)
    return hit.astype(f32).astype(bf16)


def spread_tokens(stage, matrix, k, part):
    columns = part.shape[1]
    for g in range(part.shape[0] // GROUP):
        place = pl.multiple_of((k * (part.shape[0] // GROUP) + g) * 8, 8)
        moved = dot(matrix, part[g * GROUP : (g + 1) * GROUP])
        stage[:, pl.ds(place, 8), :] = moved.reshape(BLOCK, 8, columns)


def collect_tokens(stage, matrix, k, rows):
    parts = []
    for g in range(rows // GROUP):
        place = pl.multiple_of((k * (rows // GROUP) + g) * 8, 8)
        part = stage[:, pl.ds(place, 8), :].reshape(GROUP, stage.shape[2]).astype(bf16)
        parts.append(dot(matrix, part))
    return jnp.concatenate(parts, axis=0)


class Quiet:
    def __getattr__(self, name):
        return lambda *unused: None


GATHERS = 6


class GatherSteps:
    def __init__(self, proj, up, down, small, sems):
        width = proj.shape[-1] // 4
        pieces = [(small, 0, None)]
        pieces += [(proj, width, 2 * width), (proj, 0, width), (proj, 3 * width, width)]
        pieces += [(up, 0, None), (down, 0, None)]
        plans = [
            (gather_stages if b < 3 else gather_by_halves)(piece[0], sems, COPIES * b, *piece[1:])
            for b, piece in enumerate(pieces)
        ]
        self.small, self.pair, self.queries, self.out, self.up, self.down = plans

    def start(self, plan):
        start_all(plan[0]())

    def turn(self, plan, step):
        wait_all(plan[step]())
        if step + 1 < len(plan):
            start_all(plan[step + 1]())

    def centred(self, quarter):
        if quarter == 0:
            await_neighbours()
            self.start(self.small)
            self.start(self.pair)
        else:
            self.turn(self.small, quarter - 1)
        if quarter == 1:
            self.turn(self.pair, 0)
        if quarter == 2:
            self.start(self.queries)
        if quarter == 3:
            self.start(self.up)
            self.start(self.out)

    def half_normed(self):
        self.turn(self.queries, 0)
        self.start(self.down)
        self.turn(self.pair, 1)

    def before_project(self):
        self.turn(self.pair, 2)

    def project(self, k):
        self.when(k, 1, self.queries, 1)
        self.when(k, 2, self.up, 0)
        self.when(k, 2, self.out, 0)
        self.when(k, 3, self.queries, 2)
        self.when(k, 4, self.down, 0)
        self.when(k, 6, self.up, 1)
        self.when(k, 7, self.out, 1)

    def sort(self, i):
        self.when(i, 1, self.down, 1)
        self.when(i, 5, self.up, 2)
        self.when(i, 6, self.out, 2)

    def low(self, k):
        self.when(k, 3, self.down, 2)
        self.when(k, 5, self.up, 3)
        self.when(k, 6, self.out, 3)

    def end(self):
        self.turn(self.down, 3)

    def when(self, k, place, plan, step):
        if step < 0:
            pl.when(k == place)(functools.partial(self.start, plan))
        else:
            pl.when(k == place)(functools.partial(self.turn, plan, step))


def front_near_kernel(
    lengths_ref, x_ref, proj_own, up_own, down_own, sort_own, norm_own,
    proj, up, down, sort_ref, norms_ref, *rest,
):
    rest, (small, send, recv) = rest[:-3], rest[-3:]
    greet_neighbours()
    mine = coordinates()
    proj[mine] = proj_own[...].astype(bf16)
    up[mine] = up_own[...].astype(bf16)
    down[mine] = down_own[...].astype(bf16)
    quarter, eighth = norm_place()
    own = norm_own.shape[1]
    spread = one_hot((own, LANES), lambda r, l: r + eighth * own, lambda r, l: l)
    lanes = dot(norm_own[...].astype(bf16), spread.astype(f32).astype(bf16)).astype(bf16)
    lift = one_hot((16, 4), lambda r, l: r, lambda r, l: l * 4 + quarter)
    tile = dot(lift.astype(f32).astype(bf16), lanes).astype(bf16)
    small[mine] = jnp.concatenate([sort_own[...].astype(bf16), tile], axis=0)
    steps = GatherSteps(proj, up, down, small, (send, recv))

    def arrived():
        pieces = small[...].reshape(-1, 32, LANES)
        sort_ref[...] = pieces[:, :16].reshape(sort_ref.shape)
        tile = jnp.sum(pieces[:, 16:].astype(f32), axis=0)
        norms_ref[...] = jnp.concatenate(
            [
                jnp.concatenate([tile[4 * i + q : 4 * i + q + 1] for q in range(4)], axis=1)
                for i in range(4)
            ],
            axis=0,
        )

    steps.arrived = arrived

    def columns_of(columns):
        return proj[:, :, :, :, :, columns].reshape(x_ref.shape[1], -1)

    front_steps(steps, columns_of, lengths_ref, norms_ref, x_ref, sort_ref, *rest)


def front_plain_kernel(lengths_ref, norms_ref, x_ref, proj_ref, sort_ref, *rest):
    front_steps(
        Quiet(), lambda columns: proj_ref[:, columns], lengths_ref, norms_ref, x_ref, sort_ref, *rest
    )


def front_steps(
    steps, proj_columns, lengths_ref, norms_ref, x_ref, sort_ref,
    normed_hbm, qkv_hbm, skv_hbm, tkv_hbm, means_ref, states_ref,
    normed_s, stage, matrix, pair_buf, query_buf, low_buf, flip_buf,
    copy_sem, pair_sem, query_sem, low_sem, flip_sem,
):
    seq, width = x_ref.shape
    tiles = seq // TILE
    blocks = seq // BLOCK
    per_tile = TILE // BLOCK
    chunks = 2 * width // LANES
    ends = doc_ends(lengths_ref)
    def centre_step(k, carry):
        rows = pl.ds(pl.multiple_of(k * TILE, TILE), TILE)
        xhat, unused = center_scale(x_ref[rows, :].astype(f32))
        stage[pl.ds(k * (TILE // blocks), TILE // blocks), :, :width] = xhat.reshape(
            TILE // blocks, blocks, width
        )
        return carry

    for quarter in range(4):
        lax.fori_loop(quarter * tiles // 4, (quarter + 1) * tiles // 4, centre_step, 0)
        steps.centred(quarter)
    steps.arrived()
    gain = norms_ref[0:1, :].astype(f32)
    shift = norms_ref[1:2, :].astype(f32)

    def norm_step(k, carry):
        rows = pl.ds(pl.multiple_of(k * TILE, TILE), TILE)
        xhat = stage[pl.ds(k * (TILE // blocks), TILE // blocks), :, :width].reshape(TILE, width)
        normed = (xhat * gain + shift).astype(bf16)
        normed_s[rows, :] = normed
        sums = jnp.sum(normed.astype(f32).reshape(per_tile, BLOCK, width), axis=1)
        means_ref[pl.ds(pl.multiple_of(k * per_tile, per_tile), per_tile), :] = (
            sums * (1.0 / BLOCK)
        ).astype(bf16)
        return carry

    lax.fori_loop(0, tiles // 2, norm_step, 0)
    steps.half_normed()
    lax.fori_loop(tiles // 2, tiles, norm_step, 0)
    normed_copy = pltpu.make_async_copy(normed_s, normed_hbm, copy_sem)
    normed_copy.start()

    logits = dot(means_ref[...], sort_ref[...])
    first_i = segments_of(lax.broadcasted_iota(jnp.int32, (blocks, blocks), 0) * BLOCK, ends)
    first_j = segments_of(lax.broadcasted_iota(jnp.int32, (blocks, blocks), 1) * BLOCK, ends)
    logits = jnp.where(first_i != first_j, logits - mask_penalty, logits)

    def pair_copy(k, slot):
        place = (pl.ds(pl.multiple_of(k * TILE, TILE), TILE), pl.ds(width, 2 * width))
        return pltpu.make_async_copy(pair_buf.at[slot], qkv_hbm.at[place], pair_sem.at[slot])

    def query_copy(k, slot):
        place = (pl.ds(pl.multiple_of(k * TILE, TILE), TILE), pl.ds(0, width))
        return pltpu.make_async_copy(query_buf.at[slot], qkv_hbm.at[place], query_sem.at[slot])

    def project_step(k, logits):
        rows = pl.ds(pl.multiple_of(k * TILE, TILE), TILE)
        slot = lax.rem(k, 2)

        @pl.when(k >= 2)
        def _():
            pair_copy(k - 2, slot).wait()

        steps.project(k)
        logits = logits - log_sum_exp(logits, 1)
        states_ref[2 * k] = jnp.exp(logits)
        logits = logits - log_sum_exp(logits, 0)
        states_ref[2 * k + 1] = jnp.exp(logits)
        normed = normed_s[rows, :]
        product = dot(normed, proj_columns(slice(width, 3 * width))).astype(bf16)
        pair_buf[slot] = product
        spread_tokens(stage, matrix[...], k, product)
        pair_copy(k, slot).start()
        return logits

    assert tiles == SINK_ITERS == BLOCK // flip_buf.shape[0]
    steps.before_project()
    matrix[...] = regroup_matrix(False)
    lax.fori_loop(0, tiles, project_step, logits)
    permute = states_ref[2 * SINK_ITERS - 1].astype(bf16)

    def flip_copy(t, slot):
        return pltpu.make_async_copy(flip_buf.at[slot], tkv_hbm.at[t], flip_sem.at[slot])

    def sort_step(i, carry):
        group = flip_buf.shape[0]
        steps.sort(i)
        rows = pl.ds(pl.multiple_of(i * TILE, TILE), TILE)
        slot = lax.rem(i, 2)

        @pl.when(i >= 2)
        def _():
            query_copy(i - 2, slot).wait()

        query_buf[slot] = dot(normed_s[rows, :], proj_columns(slice(0, width))).astype(bf16)
        query_copy(i, slot).start()

        @pl.when(i >= 1)
        def _():
            for u in range(group):
                flip_copy((i - 1) * group + u, u).wait()

        loaded = []
        for u in range(group):
            t = i * group + u
            loaded.append(stage[t].astype(bf16))
        for u in range(group):
            t = i * group + u
            flip_buf[u] = loaded[u].astype(f32).T.astype(bf16)
            flip_copy(t, u).start()
            stage[t] = dot(permute, loaded[u])
        return carry

    group = flip_buf.shape[0]
    lax.fori_loop(0, BLOCK // group, sort_step, 0)

    def low_copy(k, slot):
        rows = pl.ds(pl.multiple_of(k * TILE, TILE), TILE)
        return pltpu.make_async_copy(low_buf.at[slot], skv_hbm.at[rows, :], low_sem.at[slot])

    def low_step(k, carry):
        rows = pl.ds(pl.multiple_of(k * TILE, TILE), TILE)
        slot = lax.rem(k, 2)

        @pl.when(k >= 2)
        def _():
            low_copy(k - 2, slot).wait()

        steps.low(k)
        low_buf[slot] = collect_tokens(stage, matrix[...], k, TILE).astype(bf16)
        low_copy(k, slot).start()
        return carry

    matrix[...] = regroup_matrix(True)
    lax.fori_loop(0, tiles, low_step, 0)
    for u in range(group):
        flip_copy(BLOCK - group + u, u).wait()
    for k in (tiles - 2, tiles - 1):
        pair_copy(k, k % 2).wait()
        query_copy(k, k % 2).wait()
        low_copy(k, k % 2).wait()
    normed_copy.wait()
    steps.end()


def front_shapes(seq, width):
    blocks = seq // BLOCK
    hbm = pl.BlockSpec(memory_space=pl.ANY)
    vmem = pl.BlockSpec(memory_space=pltpu.VMEM)
    shapes = (
        jax.ShapeDtypeStruct((seq, width), bf16),
        jax.ShapeDtypeStruct((seq, 3 * width), bf16),
        jax.ShapeDtypeStruct((seq, 2 * width), bf16),
        jax.ShapeDtypeStruct((BLOCK, 2 * width, blocks), bf16),
        jax.ShapeDtypeStruct((blocks, width), bf16),
        jax.ShapeDtypeStruct((2 * SINK_ITERS, blocks, blocks), f32),
    )
    scratch = [
            pltpu.VMEM((seq, width), bf16),
            pltpu.VMEM((BLOCK, blocks, 2 * width), f32),
            pltpu.VMEM((GROUP, GROUP), bf16),
            pltpu.VMEM((2, TILE, 2 * width), bf16),
            pltpu.VMEM((2, TILE, width), bf16),
            pltpu.VMEM((2, TILE, 2 * width), bf16),
            pltpu.VMEM((4, 2 * width, blocks), bf16),
            pltpu.SemaphoreType.DMA,
            pltpu.SemaphoreType.DMA((2,)),
            pltpu.SemaphoreType.DMA((2,)),
            pltpu.SemaphoreType.DMA((2,)),
            pltpu.SemaphoreType.DMA((8,)),
    ]
    return shapes, [hbm, hbm, hbm, hbm, vmem, vmem], scratch


def front_plain(lengths, x, *shards):
    proj, up, down, sort, norms = gather_plain(*shards)
    shapes, specs, scratch = front_shapes(*x.shape)
    vmem = pl.BlockSpec(memory_space=pltpu.VMEM)
    results = pl.pallas_call(
        front_plain_kernel,
        out_shape=shapes,
        in_specs=[pl.BlockSpec(memory_space=pltpu.SMEM), vmem, vmem, vmem, vmem],
        out_specs=specs,
        scratch_shapes=scratch,
        compiler_params=pltpu.CompilerParams(vmem_limit_bytes=VMEM_LIMIT),
        name="front",
    )(lengths, norms, x, proj, sort)
    return (proj, up, down, sort, norms, *results)


def front_near(lengths, x, proj, up, down, sort, norm):
    seq, width = x.shape
    shapes, specs, scratch = front_shapes(seq, width)
    vmem = pl.BlockSpec(memory_space=pltpu.VMEM)
    fulls = [jax.ShapeDtypeStruct(SPLIT + own.shape, bf16) for own in (proj, up, down)]
    fulls += [jax.ShapeDtypeStruct((32 * sort.shape[0], LANES), bf16)]
    fulls += [jax.ShapeDtypeStruct((4, width), f32)]
    scratch = scratch + [pltpu.VMEM(SPLIT + (32, LANES), bf16)]
    scratch += [pltpu.SemaphoreType.DMA((GATHERS * COPIES,))] * 2
    results = pl.pallas_call(
        front_near_kernel,
        out_shape=tuple(fulls) + shapes,
        in_specs=[pl.BlockSpec(memory_space=pltpu.SMEM)] + [vmem] * 6,
        out_specs=[vmem] * 5 + specs,
        scratch_shapes=scratch,
        compiler_params=pltpu.CompilerParams(
            collective_id=0, has_side_effects=True, vmem_limit_bytes=VMEM_LIMIT
        ),
        name="front",
    )(lengths, x, proj, up, down, sort, norm)
    return tuple(full.reshape(-1, full.shape[-1]) for full in results[:3]) + tuple(results[3:])


def layer_norm_back(grad, gain, xhat, inverse):
    scaled = grad * gain
    mean_one = jnp.mean(scaled, axis=-1, keepdims=True)
    mean_two = jnp.mean(scaled * xhat, axis=-1, keepdims=True)
    return (scaled - mean_one - xhat * mean_two) * inverse


def middle_kernel(
    lengths_ref, norms_ref, x_ref, cot_ref, qkv_ref, skv_ref, out_proj_ref, up_ref, down_ref,
    y_ref, hidden_grad_ref, gq_ref, gkv_ref, gskv_ref, gup_ref, gdown_ref, gout_ref, gnorm_ref,
    gup, gdown, gout, probs_s, context_s, gcontext_s, gq_s, gkv_s, gskv_s, grads_s,
):
    step = pl.program_id(0)
    tile, width = x_ref.shape
    hidden_units = up_ref.shape[1]
    pairs = tile // (2 * BLOCK)
    head_pairs = width // LANES
    scale = HD ** (-0.5)
    ends = doc_ends(lengths_ref)

    @pl.when(step == 0)
    def _():
        gup[...] = jnp.zeros_like(gup)
        gdown[...] = jnp.zeros_like(gdown)
        gout[...] = jnp.zeros_like(gout)
        gnorm_ref[...] = jnp.zeros_like(gnorm_ref)

    lane = lax.broadcasted_iota(jnp.int32, (1, LANES), 1)
    low_head = lane < HD
    low_block = lax.rem(lane, 2 * BLOCK) < BLOCK
    head_one = low_head.astype(f32).astype(bf16)
    head_two = (1.0 - low_head.astype(f32)).astype(bf16)
    block_one = low_block.astype(f32).astype(bf16)
    block_two = (1.0 - low_block.astype(f32)).astype(bf16)

    def two_heads(part):
        return jnp.concatenate(
            [part * head_one, part * head_two], axis=0
        )

    def two_blocks(part):
        return jnp.concatenate(
            [part * block_one, part * block_two], axis=0
        )

    def stack_keys(own, far):
        return jnp.concatenate(
            [own[:BLOCK], far[:BLOCK], own[BLOCK:], far[BLOCK:]], axis=0
        )

    def pick_block(full):
        return jnp.where(low_block, full[: 2 * BLOCK], full[2 * BLOCK :])

    def pick_head(full):
        return jnp.where(low_head, full[: 2 * BLOCK], full[2 * BLOCK :])

    def attend(p, carry):
        rows = pl.ds(pl.multiple_of(p * 2 * BLOCK, 2 * BLOCK), 2 * BLOCK)
        base = step * tile + p * 2 * BLOCK
        query_seg = segments_of(base + lax.rem(lane, 2 * BLOCK), ends)
        key_place = (
            base
            + jnp.where(low_block, 0, BLOCK)
            + lax.broadcasted_iota(jnp.int32, (BLOCK, LANES), 0)
        )
        same = segments_of(key_place, ends) == query_seg
        for hp in range(head_pairs):
            cols = slice(hp * LANES, (hp + 1) * LANES)
            key_cols = slice(width + hp * LANES, width + (hp + 1) * LANES)
            value_cols = slice(2 * width + hp * LANES, 2 * width + (hp + 1) * LANES)
            queries = two_heads(qkv_ref[rows, cols])
            keys = stack_keys(qkv_ref[rows, key_cols], skv_ref[rows, cols])
            values = stack_keys(qkv_ref[rows, value_cols], skv_ref[rows, key_cols])
            scores = pick_block(dot(keys, queries.astype(f32).T.astype(bf16))) * scale
            scores = jnp.concatenate(
                [jnp.where(same, scores[:BLOCK], score_floor), scores[BLOCK:]], axis=0
            )
            exps = jnp.exp(scores - jnp.max(scores, axis=0, keepdims=True))
            probs = (exps / jnp.sum(exps, axis=0, keepdims=True)).astype(bf16)
            probs_s[p * head_pairs + hp] = probs
            context_s[rows, cols] = pick_head(dot_tn(two_blocks(probs), values)).astype(bf16)
        return carry

    lax.fori_loop(0, pairs, attend, 0, unroll=8)

    inputs = x_ref[...].astype(f32)
    context = context_s[...]
    hidden = inputs + dot(context, out_proj_ref[...])
    xhat_two, inverse_two = center_scale(hidden)
    gain_two = norms_ref[2:3, :].astype(f32)
    normed_two = (xhat_two * gain_two + norms_ref[3:4, :].astype(f32)).astype(bf16)
    normed_two_t = normed_two.T
    cot = cot_ref[...]
    total_out = hidden
    grad_normed_two = None
    root = 0.7978845608028654
    for c in range(hidden_units // TILE):
        cols = slice(c * TILE, (c + 1) * TILE)
        pre = dot(normed_two, up_ref[:, cols])
        grad_act = dot_nt(cot, down_ref[cols, :])
        square = pre * pre
        half_tanh = 0.5 + 0.5 * jnp.tanh(pre * (root + (root * 0.044715) * square))
        act = pre * half_tanh
        slope = half_tanh + act * (1.0 - half_tanh) * (
            2.0 * root + (6.0 * root * 0.044715) * square
        )
        act = act.astype(bf16)
        grad_pre = (grad_act * slope).astype(bf16)
        total_out = total_out + dot(act, down_ref[cols, :])
        back = dot_nt(grad_pre, up_ref[:, cols])
        grad_normed_two = back if grad_normed_two is None else grad_normed_two + back
        gup[:, cols] += dot(normed_two_t, grad_pre)
        gdown[cols, :] += dot_tn(act, cot)
    y_ref[...] = total_out.astype(bf16)
    gnorm_ref[0:1, :] += jnp.sum(grad_normed_two * xhat_two, axis=0, keepdims=True)
    gnorm_ref[1:2, :] += jnp.sum(grad_normed_two, axis=0, keepdims=True)
    hidden_grad = cot.astype(f32) + layer_norm_back(
        grad_normed_two, gain_two, xhat_two, inverse_two
    )
    grad_attn = hidden_grad.astype(bf16)
    hidden_grad_ref[...] = grad_attn
    gout[...] += dot_tn(context, grad_attn)
    gcontext_s[...] = dot_nt(grad_attn, out_proj_ref[...]).astype(bf16)

    def attend_back(p, carry):
        rows = pl.ds(pl.multiple_of(p * 2 * BLOCK, 2 * BLOCK), 2 * BLOCK)
        for hp in range(head_pairs):
            cols = slice(hp * LANES, (hp + 1) * LANES)
            key_cols = slice(width + hp * LANES, width + (hp + 1) * LANES)
            value_cols = slice(2 * width + hp * LANES, 2 * width + (hp + 1) * LANES)
            values = stack_keys(qkv_ref[rows, value_cols], skv_ref[rows, key_cols])
            gcontext = two_heads(gcontext_s[rows, cols])
            wide = probs_s[p * head_pairs + hp].astype(f32)
            grad_probs = pick_block(dot(values, gcontext.astype(f32).T.astype(bf16)))
            weighted = wide * grad_probs
            grad_scores = weighted - wide * jnp.sum(weighted, axis=0, keepdims=True)
            grad_scores = (grad_scores * scale).astype(bf16)
            grads_s[p * head_pairs + hp] = grad_scores
        return carry

    lax.fori_loop(0, pairs, attend_back, 0, unroll=8)

    def attend_last(p, carry):
        rows = pl.ds(pl.multiple_of(p * 2 * BLOCK, 2 * BLOCK), 2 * BLOCK)
        for hp in range(head_pairs):
            cols = slice(hp * LANES, (hp + 1) * LANES)
            key_cols = slice(width + hp * LANES, width + (hp + 1) * LANES)
            value_cols = slice(2 * width + hp * LANES, 2 * width + (hp + 1) * LANES)
            keys = stack_keys(qkv_ref[rows, key_cols], skv_ref[rows, cols])
            gq_s[rows, cols] = pick_head(dot_tn(two_blocks(grads_s[p * head_pairs + hp]), keys)).astype(bf16)
            gkeys = dot(two_blocks(grads_s[p * head_pairs + hp]), two_heads(qkv_ref[rows, cols])).astype(bf16)
            gvalues = dot(two_blocks(probs_s[p * head_pairs + hp]), two_heads(gcontext_s[rows, cols])).astype(bf16)
            for grads, where in ((gkeys, cols), (gvalues, key_cols)):
                gkv_s[rows, where] = jnp.concatenate(
                    [grads[:BLOCK], grads[2 * BLOCK : 3 * BLOCK]], axis=0
                )
                gskv_s[rows, where] = jnp.concatenate(
                    [grads[BLOCK : 2 * BLOCK], grads[3 * BLOCK :]], axis=0
                )
        return carry

    lax.fori_loop(0, pairs, attend_last, 0, unroll=8)
    gq_ref[...] = gq_s[...]
    gkv_ref[...] = gkv_s[...]
    gskv_ref[...] = gskv_s[...]

    @pl.when(step == pl.num_programs(0) - 1)
    def _():
        gup_ref[...] = gup[...].astype(bf16)
        gdown_ref[...] = gdown[...].astype(bf16)
        gout_ref[...] = gout[...].astype(bf16)


def middle(lengths, norms, x, cot, qkv, skv, proj, up, down):
    seq, width = x.shape
    hidden_units = up.shape[1]
    tiles = seq // TILE

    def rows(columns):
        return pl.BlockSpec((TILE, columns), lambda i: (i, 0))

    def fixed(shape, index=(0, 0)):
        return pl.BlockSpec(shape, lambda i: index, pipeline_mode=pl.Buffered(1))

    return pl.pallas_call(
        middle_kernel,
        grid=(tiles,),
        out_shape=(
            jax.ShapeDtypeStruct((seq, width), bf16),
            jax.ShapeDtypeStruct((seq, width), bf16),
            jax.ShapeDtypeStruct((seq, width), bf16),
            jax.ShapeDtypeStruct((seq, 2 * width), bf16),
            jax.ShapeDtypeStruct((seq, 2 * width), bf16),
            jax.ShapeDtypeStruct((width, hidden_units), bf16),
            jax.ShapeDtypeStruct((hidden_units, width), bf16),
            jax.ShapeDtypeStruct((width, width), bf16),
            jax.ShapeDtypeStruct((2, width), f32),
        ),
        in_specs=[
            pl.BlockSpec(memory_space=pltpu.SMEM),
            fixed(norms.shape),
            rows(width),
            rows(width),
            rows(3 * width),
            rows(2 * width),
            fixed((width, width), (0, 3)),
            fixed(up.shape),
            fixed(down.shape),
        ],
        out_specs=[
            rows(width),
            rows(width),
            rows(width),
            rows(2 * width),
            rows(2 * width),
            fixed((width, hidden_units)),
            fixed((hidden_units, width)),
            fixed((width, width)),
            fixed((2, width)),
        ],
        scratch_shapes=[
            pltpu.VMEM((width, hidden_units), f32),
            pltpu.VMEM((hidden_units, width), f32),
            pltpu.VMEM((width, width), f32),
            pltpu.VMEM((TILE // (2 * BLOCK) * (width // LANES), 2 * BLOCK, LANES), bf16),
            pltpu.VMEM((TILE, width), bf16),
            pltpu.VMEM((TILE, width), bf16),pltpu.VMEM((TILE, width), bf16),pltpu.VMEM((TILE, 2*width), bf16),pltpu.VMEM((TILE, 2*width), bf16),
            pltpu.VMEM((TILE // (2 * BLOCK) * (width // LANES), 2 * BLOCK, LANES), bf16),
        ],
        compiler_params=pltpu.CompilerParams(vmem_limit_bytes=VMEM_LIMIT),
        name="middle",
    )(lengths, norms, x, cot, qkv, skv, proj, up, down)


def add_low(*parts):
    total = parts[0].astype(f32)
    for part in parts[1:]:
        total = total + part.astype(f32)
    return total


class Reduce:
    def __init__(self, part, total, columns, got_c, got_xy, got_z, sems, base):
        self.part, self.total, self.columns = part, total, columns
        self.whole = (slice(None), columns)
        self.got_c, self.got_xy, self.got_z = got_c, got_xy, got_z
        self.sems, self.base = sems, base

    def copies(self, step):
        z, x, y, c = coordinates()
        every = slice(None)

        def one(source, target, index, device):
            return remote(source, target, self.sems, self.base + index, device)

        if step == 0:
            away = self.part.at[(every, every, every, 1 - c) + self.whole]
            return [one(away, self.got_c, 0, device_of(z, x, y, 1 - c))]
        if step == 1:
            return [
                one(self.got_c.at[(every,) + other], self.got_xy.at[k], 1 + k, device_of(z, *other, c))
                for k, other in enumerate(xy_others(x, y))
            ]
        return [
            one(self.got_c.at[other, x, y], self.got_z.at[k], 4 + k, device_of(other, x, y, c))
            for k, other in enumerate(z_others(z))
        ]

    def start(self, step):
        start_all(self.copies(step))

    def turn(self, step):
        wait_all(self.copies(step))
        self.add(step)
        if step < 2:
            self.start(step + 1)

    def add(self, step):
        z, x, y, c = coordinates()
        if step == 2:
            self.total[:, self.columns] = add_low(
                self.got_c[z, x, y], *[self.got_z[k] for k in range(3)]
            )
            return

        def line(i, carry):
            if step == 0:
                for j in range(2):
                    for k in range(2):
                        self.got_c[i, j, k] = add_low(
                            self.part[(i, j, k, c) + self.whole], self.got_c[i, j, k]
                        ).astype(bf16)
            else:
                self.got_c[i, x, y] = add_low(
                    self.got_c[i, x, y], *[self.got_xy[k, i] for k in range(3)]
                ).astype(bf16)
            return carry

        lax.fori_loop(0, 4, line, 0)


def reduce_scratch(rows, columns):
    shapes = ((4, 2, 2, rows, columns), (3, 4, rows, columns), (3, rows, columns))
    return [pltpu.VMEM(shape, bf16) for shape in shapes]


class ReduceSteps:
    def __init__(self, plans):
        self.up, self.down, self.out, self.query = plans

    def begin(self):
        pass

    def send(self):
        await_neighbours()
        self.up.start(0)
        self.down.start(0)
        self.out.start(0)

    def during_query(self, k):
        pl.when(k == 1)(self.send)
        self.when(k, 4, self.up, 0)
        self.when(k, 7, self.down, 0)

    def queried(self):
        self.query.start(0)
        self.out.turn(0)

    def load(self, k):
        self.when(k, 4, self.query, 0)

    def loaded(self):
        pass

    def sort(self, i):
        self.when(i, 4, self.up, 1)

    def swept(self):
        self.down.turn(1)
        self.up.turn(2)

    def weights(self, k):
        self.when(k, 1, self.out, 1)
        self.when(k, 2, self.query, 1)
        self.when(k, 5, self.down, 2)

    def end(self):
        self.out.turn(2)

    def inputs(self, k, pair):
        self.when(k, 2, pair, 0)
        self.when(k, 4, self.query, 2)
        self.when(k, 7, pair, 1)

    def when(self, k, place, plan, step):
        pl.when(k == place)(functools.partial(plan.turn, step))


def norm_rows(grads):
    rows = []
    for grad in grads:
        for i in range(grad.shape[0]):
            for q in range(grad.shape[1] // LANES):
                rows.append(grad[i : i + 1, q * LANES : (q + 1) * LANES])
    return jnp.concatenate(rows, axis=0)


def back_near_kernel(*refs):
    ins, refs = refs[:8], refs[8:]
    (gout, gup, gdown, gtwo_ref, norms_ref, proj_ref, x_hbm), refs = refs[:7], refs[7:]
    gx_hbm, refs = refs[0], refs[1:]
    (query_sum, pair_sum, out_sum, up_sum, down_sum, sort_sum, norm_sum), refs = refs[:7], refs[7:]
    work, refs = refs[:8], refs[8:]
    (gsum, gpair, gsort, gmeans, gquery, gone_ref, small, small_sum), refs = refs[:8], refs[8:]
    (send, recv), scratch = refs[:2], refs[2:]
    greet_neighbours()
    every = slice(None)
    places = (
        (gup, up_sum, every), (gdown, down_sum, every), (gout, out_sum, every),
        (gquery, query_sum, every), (gpair, pair_sum, every), (small, small_sum, every),
    )
    plans = [
        Reduce(*place, *scratch[3 * b : 3 * b + 3], (send, recv), COPIES * b)
        for b, place in enumerate(places)
    ]
    pair, small_plan = plans[4:]
    steps = ReduceSteps(plans[:4])
    back_steps(steps, *ins, gsum, gpair, gsort, gmeans, gquery, *work)
    pair.start(0)
    seq, width = x_hbm.shape
    gone_ref[...] = jnp.zeros_like(gone_ref)

    def input_step(x_ref, gq_ref, gx_ref):
        k = pl.program_id(0)
        steps.inputs(k, pair)
        part = TILE // BLOCK
        means = gmeans[pl.ds(pl.multiple_of(k * part, part), part), :]
        gkv = gsum[pl.ds(pl.multiple_of(k * TILE, TILE), TILE), :]
        input_tile(norms_ref, x_ref, gq_ref, gkv, means, proj_ref, gx_ref, gone_ref)

    def rows_of(columns):
        return pl.BlockSpec((TILE, columns), lambda i: (i, 0))

    pltpu.emit_pipeline(
        input_step,
        grid=(seq // TILE,),
        in_specs=[rows_of(width)] * 2,
        out_specs=[rows_of(width)],
    )(x_hbm, ins[6], gx_hbm)
    tile = norm_rows((gone_ref[...], gtwo_ref[...])).astype(bf16)
    small[:, :, :, :, :16] = gsort[...].astype(bf16).reshape(SPLIT + (width // 32, LANES))
    for i in range(4):
        for j in range(2):
            for k in range(2):
                for m in range(2):
                    small[i, j, k, m, 16:] = tile
    small_plan.start(0)
    for step in range(3):
        small_plan.turn(step)
    pair.turn(2)
    sort_sum[...] = small_sum[:16, :]
    quarter, eighth = norm_place()
    own = norm_sum.shape[1]
    drop = one_hot((4, 16), lambda r, l: r * 4 + quarter, lambda r, l: l).astype(f32)
    pick = one_hot((LANES, own), lambda r, l: r, lambda r, l: l + eighth * own).astype(f32)

    def exact(left, right):
        return lax.dot_general(
            left, right, (((1,), (0,)), ((), ())),
            precision=lax.Precision.HIGHEST, preferred_element_type=f32,
        )

    norm_sum[...] = exact(exact(drop, small_sum[16:, :]), pick)


def back_plain_kernel(*refs):
    back_steps(Quiet(), *refs)


def back_steps(
    steps, gskv_hbm, tkv_hbm, states_ref, means_ref, sort_ref,
    normed_hbm, gq_hbm, gkv_hbm,
    gsum, gpair_ref, gsort_ref, gmeans, gquery_ref,
    stage, matrix, low_buf, flip_buf, gproj, gperm, low_sem, flip_sem,
):
    steps.begin()
    seq, width = normed_hbm.shape
    tiles = seq // TILE
    blocks = seq // BLOCK
    chunks = 2 * width // LANES
    per_tile = TILE // BLOCK

    def low_copy(k, slot):
        rows = pl.ds(pl.multiple_of(k * TILE, TILE), TILE)
        return pltpu.make_async_copy(gskv_hbm.at[rows, :], low_buf.at[slot], low_sem.at[slot])

    group = flip_buf.shape[0] // 2

    def flip_copy(t, slot):
        return pltpu.make_async_copy(tkv_hbm.at[t], flip_buf.at[slot], flip_sem.at[slot])

    low_copy(0, 0).start()
    low_copy(1, 1).start()
    for u in range(group):
        flip_copy(u, u).start()

    def load_step(k, carry):
        rows = pl.ds(pl.multiple_of(k * TILE, TILE), TILE)
        slot = lax.rem(k, 2)
        low_copy(k, slot).wait()
        steps.load(k)
        spread_tokens(stage, matrix[...], k, low_buf[slot])

        @pl.when(k + 2 < tiles)
        def _():
            low_copy(k + 2, slot).start()

        return carry

    def rows_of(columns):
        return pl.BlockSpec((TILE, columns), lambda i: (i, 0))

    gproj[...] = jnp.zeros_like(gproj)

    def query_step(normed_ref, gq_ref):
        steps.during_query(pl.program_id(0))
        gproj[:, :width] += dot_tn(normed_ref[...], gq_ref[...])

    pltpu.emit_pipeline(query_step, grid=(tiles,), in_specs=[rows_of(width)] * 2)(
        normed_hbm, gq_hbm
    )
    gquery_ref[...] = gproj[:, :width].astype(bf16).reshape(gquery_ref.shape)
    steps.queried()
    matrix[...] = regroup_matrix(False)
    lax.fori_loop(0, tiles, load_step, 0)
    matrix[...] = regroup_matrix(True)
    steps.loaded()

    final = states_ref[2 * SINK_ITERS - 1]
    permute_t = final.T.astype(bf16)
    gperm[...] = jnp.zeros_like(gperm)

    def sort_step(i, carry):
        side = lax.rem(i, 2) * group
        steps.sort(i)

        @pl.when(i + 1 < BLOCK // group)
        def _():
            for u in range(group):
                flip_copy((i + 1) * group + u, group - side + u).start()

        for u in range(group):
            flip_copy(i * group + u, side + u).wait()
        loaded = []
        for u in range(group):
            t = i * group + u
            loaded.append(stage[t].astype(bf16))
        total = gperm[...]
        for u in range(group):
            t = i * group + u
            total = total + dot(loaded[u], flip_buf[side + u])
            stage[t] = dot(permute_t, loaded[u])
        gperm[...] = total
        return carry

    lax.fori_loop(0, BLOCK // group, sort_step, 0)

    grad = gperm[...] * final
    for sweep in reversed(range(SINK_ITERS)):
        grad = grad - states_ref[2 * sweep + 1] * jnp.sum(grad, axis=0, keepdims=True)
        grad = grad - states_ref[2 * sweep] * jnp.sum(grad, axis=1, keepdims=True)
    grad = grad.astype(bf16)
    gsort_ref[...] = dot_tn(means_ref[...], grad).astype(gsort_ref.dtype)
    gmeans[...] = dot_nt(grad, sort_ref[...]) * (1.0 / BLOCK)
    steps.swept()

    def weight_step(normed_ref, gkv_ref):
        k = pl.program_id(0)
        steps.weights(k)
        gkv = (gkv_ref[...].astype(f32) + collect_tokens(stage, matrix[...], k, TILE)).astype(bf16)
        gsum[pl.ds(pl.multiple_of(k * TILE, TILE), TILE), :] = gkv
        gproj[:, width:] += dot_tn(normed_ref[...], gkv)

    pltpu.emit_pipeline(
        weight_step,
        grid=(tiles,),
        in_specs=[rows_of(width), rows_of(2 * width)],
    )(normed_hbm, gkv_hbm)
    gpair_ref[...] = gproj[:, width:].astype(bf16).reshape(gpair_ref.shape)
    steps.end()


def back_scratch(seq, width):
    blocks = seq // BLOCK
    return [
            pltpu.VMEM((BLOCK, blocks, 2 * width), f32),
            pltpu.VMEM((GROUP, GROUP), bf16),
            pltpu.VMEM((2, TILE, 2 * width), bf16),
            pltpu.VMEM((8, 2 * width, blocks), bf16),
            pltpu.VMEM((width, 3 * width), f32),
            pltpu.VMEM((blocks, blocks), f32),
            pltpu.SemaphoreType.DMA((2,)),
            pltpu.SemaphoreType.DMA((8,)),
    ]


def back_shapes(seq, width):
    hbm = pl.BlockSpec(memory_space=pl.ANY)
    vmem = pl.BlockSpec(memory_space=pltpu.VMEM)
    blocks = seq // BLOCK
    shapes = (
        jax.ShapeDtypeStruct((seq, 2 * width), bf16),
        jax.ShapeDtypeStruct((width, 2 * width), bf16),
        jax.ShapeDtypeStruct((width, blocks), f32),
        jax.ShapeDtypeStruct((blocks, width), f32),
    )
    return shapes, [hbm, hbm, vmem, vmem, vmem, hbm, hbm, hbm], [vmem, vmem, vmem, vmem]


def back_plain(seq, width, ins, gout, gup, gdown):
    shapes, in_specs, out_specs = back_shapes(seq, width)
    gsum, gpair, gsort, gmeans, gquery = pl.pallas_call(
        back_plain_kernel,
        out_shape=shapes + (jax.ShapeDtypeStruct((width, width), bf16),),
        in_specs=in_specs,
        out_specs=out_specs + [pl.BlockSpec(memory_space=pltpu.VMEM)],
        scratch_shapes=back_scratch(seq, width),
        compiler_params=pltpu.CompilerParams(vmem_limit_bytes=VMEM_LIMIT),
        name="back",
    )(*ins)
    return gsum, gpair, gsort, gmeans, gquery, gout, gup, gdown


def split_shards(grad):
    return grad.reshape(SPLIT + (grad.shape[0] // 32, grad.shape[1]))


def back_near(seq, width, ins, gout, gup, gdown, gtwo, norms, proj, x):
    shapes, in_specs, unused = back_shapes(seq, width)
    hbm = pl.BlockSpec(memory_space=pl.ANY)
    vmem = pl.BlockSpec(memory_space=pltpu.VMEM)
    gout, gup, gdown = split_shards(gout), split_shards(gup), split_shards(gdown)
    blocks = seq // BLOCK
    query, pair, small = (width // 32, width), (width // 32, 2 * width), (32, LANES)
    scratch = back_scratch(seq, width) + [
        pltpu.VMEM((seq, 2 * width), bf16),
        pltpu.VMEM(SPLIT + pair, bf16),
        pltpu.VMEM((width, blocks), f32),
        pltpu.VMEM((blocks, width), f32),
        pltpu.VMEM(SPLIT + query, bf16),
        pltpu.VMEM((2, width), f32),
        pltpu.VMEM(SPLIT + small, bf16),
        pltpu.VMEM(small, f32),
    ]
    scratch += [pltpu.SemaphoreType.DMA((6 * COPIES,))] * 2
    for shape in (gup.shape[-2:], gdown.shape[-2:], gout.shape[-2:], query, pair, small):
        scratch += reduce_scratch(*shape)
    sums = [query, pair, gout.shape[-2:], gup.shape[-2:], gdown.shape[-2:]]
    sums += [(width // 32, blocks), (4, width // 32)]
    gx, *totals = pl.pallas_call(
        back_near_kernel,
        out_shape=(jax.ShapeDtypeStruct((seq, width), bf16),)
        + tuple(jax.ShapeDtypeStruct(shape, f32) for shape in sums),
        in_specs=in_specs + [vmem] * 6 + [hbm],
        out_specs=[hbm] + [vmem] * 7,
        scratch_shapes=scratch,
        compiler_params=pltpu.CompilerParams(
            collective_id=1, has_side_effects=True, vmem_limit_bytes=VMEM_LIMIT
        ),
        name="back",
    )(*ins, gout, gup, gdown, gtwo, norms, proj, x)
    return gx, totals


def input_tile(
    norms_ref, x_ref, gq_ref, gkv, means, proj_ref, gx_ref, gnorm_ref
):
    tile, width = x_ref.shape
    grad_normed = dot_nt(gq_ref[...], proj_ref[:, :width])
    grad_normed = grad_normed + dot_nt(gkv, proj_ref[:, width : 3 * width])
    grad_normed = grad_normed + jnp.broadcast_to(
        means[:, None, :], (tile // BLOCK, BLOCK, width)
    ).reshape(tile, width)
    xhat, inverse = center_scale(x_ref[...].astype(f32))
    gnorm_ref[0:1, :] += jnp.sum(grad_normed * xhat, axis=0, keepdims=True)
    gnorm_ref[1:2, :] += jnp.sum(grad_normed, axis=0, keepdims=True)
    gain = norms_ref[0:1, :].astype(f32)
    gx_ref[...] = layer_norm_back(grad_normed, gain, xhat, inverse).astype(bf16)


def inputs_kernel(
    norms_ref, x_ref, gq_ref, gsum_ref, gmeans_ref, proj_ref, gx_ref, gnorm_ref
):
    @pl.when(pl.program_id(0) == 0)
    def _():
        gnorm_ref[...] = jnp.zeros_like(gnorm_ref)

    input_tile(
        norms_ref, x_ref, gq_ref, gsum_ref[...], gmeans_ref[...], proj_ref, gx_ref, gnorm_ref
    )


def inputs_back(norms, x, gq, gsum, gmeans, proj):
    seq, width = x.shape

    def rows(columns):
        return pl.BlockSpec((TILE, columns), lambda i: (i, 0))

    def fixed(shape):
        return pl.BlockSpec(shape, lambda i: (0, 0), pipeline_mode=pl.Buffered(1))

    return pl.pallas_call(
        inputs_kernel,
        grid=(seq // TILE,),
        out_shape=(
            jax.ShapeDtypeStruct((seq, width), bf16),
            jax.ShapeDtypeStruct((2, width), f32),
        ),
        in_specs=[
            fixed(norms.shape), rows(width), rows(width), rows(2 * width),
            pl.BlockSpec((TILE // BLOCK, width), lambda i: (i, 0)), fixed(proj.shape),
        ],
        out_specs=[rows(width), fixed((2, width))],
        compiler_params=pltpu.CompilerParams(vmem_limit_bytes=VMEM_LIMIT),
        name="inputs",
    )(norms, x, gq, gsum, gmeans, proj)


def last_plain(gpair, gsort, gone, gtwo, gquery, gout, gup, gdown):
    grads = (gquery, gpair, gout, gup, gdown, gsort, jnp.concatenate([gone, gtwo], axis=0))
    return tuple(
        lax.psum_scatter(
            grad.astype(f32), AXES, scatter_dimension=1 if b == 6 else 0, tiled=True
        )
        for b, grad in enumerate(grads)
    )


def adamw(master, first, second, grad, rate, decay):
    first_new = beta_first * first + (1.0 - beta_first) * grad
    second_new = beta_second * second + (1.0 - beta_second) * grad * grad
    first_hat = first_new / (1.0 - beta_first**STEP)
    second_hat = second_new / (1.0 - beta_second**STEP)
    master_new = master - rate * (first_hat / (jnp.sqrt(second_hat) + adam_eps) + decay * master)
    return (master_new, first_new, second_new)


RATES = (
    (rate_matrix, weight_decay), (rate_matrix, weight_decay), (rate_matrix, weight_decay),
    (rate_other, weight_decay), (rate_other, 0.0),
)


def update_kernel(*refs):
    parts, sums, states, gx_out, results = refs[:2], refs[2:9], refs[9:24], refs[24], refs[25:]

    def add_step(hidden_grad, norm_grad, target):
        pl.when(pl.program_id(0) == 1)(functools.partial(update_shards, sums, states, results))
        target[...] = hidden_grad[...].astype(f32) + norm_grad[...].astype(f32)

    rows = pl.BlockSpec((TILE, gx_out.shape[1]), lambda i: (i, 0))
    pltpu.emit_pipeline(
        add_step, grid=(gx_out.shape[0] // TILE,), in_specs=[rows] * 2, out_specs=[rows]
    )(*parts, gx_out)


def update_shards(sums, states, results):
    sums = [jnp.concatenate([ref[...] for ref in sums[:3]], axis=1)] + [ref[...] for ref in sums[3:]]
    for b, (rate, decay) in enumerate(RATES):
        state = [ref[...] for ref in states[3 * b : 3 * b + 3]]
        for ref, value in zip(
            results[3 * b : 3 * b + 3], adamw(*state, sums[b], rate, decay)
        ):
            ref[...] = value


def update(hidden_grad, gx, sums, states):
    vmem = pl.BlockSpec(memory_space=pltpu.VMEM)
    hbm = pl.BlockSpec(memory_space=pl.ANY)
    return pl.pallas_call(
        update_kernel,
        out_shape=tuple(jax.ShapeDtypeStruct(array.shape, f32) for array in (gx, *states)),
        in_specs=[hbm] * 2 + [vmem] * 22,
        out_specs=[hbm] + [vmem] * 15,
        compiler_params=pltpu.CompilerParams(vmem_limit_bytes=VMEM_LIMIT),
        name="update",
    )(hidden_grad, gx, *sums, *states)


def gather_plain(proj, up, down, sort, norm):
    def gathered(shard, axis):
        return lax.all_gather(shard.astype(bf16), AXES, axis=axis, tiled=True)

    return (*(gathered(shard, 0) for shard in (proj, up, down, sort)), gathered(norm, 1))


def body(near, layer_input, doc_lengths, out_cotangent, *states):
    x = layer_input[0]
    cot = out_cotangent[0]
    proj, up, down, sort, norms, normed, qkv, skv, tkv, means, kept = (
        front_near if near else front_plain
    )(doc_lengths, x, *states[::3])
    y, hidden_grad, gq, gkv, gskv, gup, gdown, gout, gnorm_two = middle(
        doc_lengths, norms, x, cot, qkv, skv, proj, up, down
    )
    ins = (gskv, tkv, kept, means, sort, normed, gq, gkv)
    if near:
        gx, sums = back_near(
            *x.shape, ins, gout, gup, gdown, gnorm_two, norms, proj, x
        )
    else:
        gsum, gpair, gsort, gmeans, *done = back_plain(*x.shape, ins, gout, gup, gdown)
        gx, gnorm_one = inputs_back(norms, x, gq, gsum, gmeans, proj)
        sums = last_plain(gpair, gsort, gnorm_one, gnorm_two, *done)
    gx, *updates = update(hidden_grad, gx, sums, states)
    return (y[None], gx[None], *updates)


def solution(mesh):
    rows3, rows2, columns = P(AXES, None, None), P(AXES, None), P(None, AXES)
    near = (mesh.shape["dp"], mesh.shape["fsdp"]) == (8, 4)
    return jax.shard_map(
        functools.partial(body, near),
        mesh=mesh,
        in_specs=(rows3, rows2, rows3) + (rows2,) * 12 + (columns,) * 3,
        out_specs=(rows3, rows3) + (rows2,) * 12 + (columns,) * 3,
        check_vma=False,
    )
```

```python
import functools
import jax
import jax.numpy as jnp
from jax import lax
from jax.experimental import pallas as pl
from jax.experimental.pallas import tpu as pltpu
from jax.sharding import PartitionSpec as P

HD = 64
BLOCK = 32
SINK_ITERS = 8
STEP = 10
TILE = 512
LANES = 128

mask_penalty = 6.0
score_floor = -1000000000.0
norm_eps = 1e-05
beta_first = 0.9
beta_second = 0.95
adam_eps = 1e-08
weight_decay = 0.1
rate_matrix = 0.1
rate_other = 0.5

bf16 = jnp.bfloat16
f32 = jnp.float32
VMEM_LIMIT = 62 * 2**20


def dot(left, right):
    return lax.dot_general(left, right, (((1,), (0,)), ((), ())), preferred_element_type=f32)


def dot_nt(left, right):
    return lax.dot_general(left, right, (((1,), (1,)), ((), ())), preferred_element_type=f32)


def dot_tn(left, right):
    return lax.dot_general(left, right, (((0,), (0,)), ((), ())), preferred_element_type=f32)


def doc_ends(lengths_ref):
    total = lengths_ref[0, 0]
    ends = [total]
    for k in range(1, lengths_ref.shape[1]):
        total = total + lengths_ref[0, k]
        ends.append(total)
    return ends


def segments_of(places, ends):
    count = jnp.zeros(places.shape, jnp.int32)
    for end in ends:
        count = count + (places >= end).astype(jnp.int32)
    return count


def center_scale(values):
    centre = values - jnp.mean(values, axis=-1, keepdims=True)
    spread = jnp.mean(centre * centre, axis=-1, keepdims=True)
    inverse = lax.rsqrt(spread + norm_eps)
    return centre * inverse, inverse


def log_sum_exp(logits, axis):
    top = jnp.max(logits, axis=axis, keepdims=True)
    return top + jnp.log(jnp.sum(jnp.exp(logits - top), axis=axis, keepdims=True))


MESH_ID = pl.DeviceIdType.MESH
AXES = ("dp", "fsdp")
SPLIT = (4, 2, 2, 2)
COPIES = 8


def coordinates():
    dp, fsdp = lax.axis_index("dp"), lax.axis_index("fsdp")
    return dp // 2, dp % 2, fsdp // 2, fsdp % 2


def device_of(z, x, y, c):
    return (z * 2 + x, y * 2 + c)


def z_others(z):
    return (z + 1 - 2 * (z % 2), (z + 2) % 4, 3 - z)


def xy_others(x, y):
    return ((1 - x, y), (x, 1 - y), (1 - x, 1 - y))


def neighbours():
    z, x, y, c = coordinates()
    return (
        [device_of(one, x, y, c) for one in z_others(z)]
        + [device_of(z, *one, c) for one in xy_others(x, y)]
        + [device_of(z, x, y, 1 - c)]
    )


def greet_neighbours():
    for peer in neighbours():
        pl.semaphore_signal(
            pltpu.get_barrier_semaphore(), inc=1, device_id=peer, device_id_type=MESH_ID
        )


def await_neighbours():
    pl.semaphore_wait(pltpu.get_barrier_semaphore(), len(neighbours()))


def remote(source, target, sems, index, device):
    send, recv = sems
    return pltpu.make_async_remote_copy(
        src_ref=source, dst_ref=target, send_sem=send.at[index], recv_sem=recv.at[index],
        device_id=device, device_id_type=MESH_ID,
    )


def gather_stages(full, sems, base, start=0, size=None):
    z, x, y, c = coordinates()
    whole = (slice(None), pl.ds(start, size or full.shape[-1]))
    every = slice(None)

    def same(index, place, device):
        part = full.at[place + whole]
        return remote(part, part, sems, base + index, device)

    def stage_z():
        return [
            same(k, (z, x, y, c), device_of(one, x, y, c)) for k, one in enumerate(z_others(z))
        ]

    def stage_xy():
        return [
            same(3 + k, (every, x, y, c), device_of(z, *one, c))
            for k, one in enumerate(xy_others(x, y))
        ]

    def stage_core():
        return [same(6, (every, every, every, c), device_of(z, x, y, 1 - c))]

    return [stage_z, stage_xy, stage_core]


def gather_by_halves(full, sems, base, start=0, size=None):
    z, x, y, c = coordinates()
    size = size or full.shape[-1]
    every = slice(None)
    first = (every, pl.ds(start, size // 2))
    second = (every, pl.ds(start + size // 2, size // 2))
    whole = (every, pl.ds(start, size))
    to_x, to_y = device_of(z, 1 - x, y, c), device_of(z, x, 1 - y, c)

    def same(index, place, device):
        part = full.at[place]
        return remote(part, part, sems, base + index, device)

    def stage_z():
        return [
            same(k, (z, x, y, c) + whole, device_of(one, x, y, c))
            for k, one in enumerate(z_others(z))
        ]

    def stage_one():
        return [
            same(3, (every, x, y, c) + first, to_x), same(4, (every, x, y, c) + second, to_y)
        ]

    def stage_two():
        return [
            same(5, (every, every, y, c) + first, to_y),
            same(6, (every, x, every, c) + second, to_x),
        ]

    def stage_core():
        return [same(7, (every, every, every, c) + whole, device_of(z, x, y, 1 - c))]

    return [stage_z, stage_one, stage_two, stage_core]


def start_all(copies):
    for copy in copies:
        copy.start()


def wait_all(copies):
    for copy in copies:
        copy.wait()


def one_hot(shape, row_of, column_of):
    rows = lax.broadcasted_iota(jnp.int32, shape, 0)
    columns = lax.broadcasted_iota(jnp.int32, shape, 1)
    return row_of(rows, columns) == column_of(rows, columns)


def norm_place():
    z, x, y, c = coordinates()
    device = (z * 2 + x) * 4 + y * 2 + c
    return device // 8, device % 8


GROUP = 8 * BLOCK


def regroup_matrix(inverse):
    rows = lax.broadcasted_iota(jnp.int32, (GROUP, GROUP), 1 if inverse else 0)
    columns = lax.broadcasted_iota(jnp.int32, (GROUP, GROUP), 0 if inverse else 1)
    hit = (rows // 8 == columns % BLOCK) & (rows % 8 == columns // BLOCK)
    return hit.astype(f32).astype(bf16)


def spread_tokens(stage, matrix, k, part):
    columns = part.shape[1]
    for g in range(part.shape[0] // GROUP):
        place = pl.multiple_of((k * (part.shape[0] // GROUP) + g) * 8, 8)
        moved = dot(matrix, part[g * GROUP : (g + 1) * GROUP])
        stage[:, pl.ds(place, 8), :] = moved.reshape(BLOCK, 8, columns)


def collect_tokens(stage, matrix, k, rows):
    parts = []
    for g in range(rows // GROUP):
        place = pl.multiple_of((k * (rows // GROUP) + g) * 8, 8)
        part = stage[:, pl.ds(place, 8), :].reshape(GROUP, stage.shape[2]).astype(bf16)
        parts.append(dot(matrix, part))
    return jnp.concatenate(parts, axis=0)


class Quiet:
    def __getattr__(self, name):
        return lambda *unused: None


GATHERS = 6


class GatherSteps:
    def __init__(self, proj, up, down, small, sems):
        width = proj.shape[-1] // 4
        pieces = [(small, 0, None)]
        pieces += [(proj, width, 2 * width), (proj, 0, width), (proj, 3 * width, width)]
        pieces += [(up, 0, None), (down, 0, None)]
        plans = [
            (gather_stages if b < 3 else gather_by_halves)(piece[0], sems, COPIES * b, *piece[1:])
            for b, piece in enumerate(pieces)
        ]
        self.small, self.pair, self.queries, self.out, self.up, self.down = plans

    def start(self, plan):
        start_all(plan[0]())

    def turn(self, plan, step):
        wait_all(plan[step]())
        if step + 1 < len(plan):
            start_all(plan[step + 1]())

    def centred(self, quarter):
        if quarter == 0:
            await_neighbours()
            self.start(self.small)
            self.start(self.pair)
        else:
            self.turn(self.small, quarter - 1)
        if quarter == 1:
            self.turn(self.pair, 0)
        if quarter == 2:
            self.start(self.queries)
        if quarter == 3:
            self.start(self.up)
            self.start(self.out)

    def half_normed(self):
        self.turn(self.queries, 0)
        self.start(self.down)
        self.turn(self.pair, 1)

    def before_project(self):
        self.turn(self.pair, 2)

    def project(self, k):
        self.when(k, 1, self.queries, 1)
        self.when(k, 2, self.up, 0)
        self.when(k, 2, self.out, 0)
        self.when(k, 3, self.queries, 2)
        self.when(k, 4, self.down, 0)
        self.when(k, 6, self.up, 1)
        self.when(k, 7, self.out, 1)

    def sort(self, i):
        self.when(i, 2, self.down, 1)
        self.when(i, 7, self.up, 2)

    def low(self, k):
        self.when(k, 0, self.out, 2)
        self.when(k, 5, self.down, 2)
        self.when(k, 6, self.up, 3)
        self.when(k, 7, self.out, 3)

    def end(self):
        self.turn(self.down, 3)

    def when(self, k, place, plan, step):
        if step < 0:
            pl.when(k == place)(functools.partial(self.start, plan))
        else:
            pl.when(k == place)(functools.partial(self.turn, plan, step))


def front_near_kernel(
    lengths_ref, x_ref, proj_own, up_own, down_own, sort_own, norm_own,
    proj, up, down, sort_ref, norms_ref, *rest,
):
    rest, (small, send, recv) = rest[:-3], rest[-3:]
    greet_neighbours()
    mine = coordinates()
    proj[mine] = proj_own[...].astype(bf16)
    up[mine] = up_own[...].astype(bf16)
    down[mine] = down_own[...].astype(bf16)
    quarter, eighth = norm_place()
    own = norm_own.shape[1]
    spread = one_hot((own, LANES), lambda r, l: r + eighth * own, lambda r, l: l)
    lanes = dot(norm_own[...].astype(bf16), spread.astype(f32).astype(bf16)).astype(bf16)
    lift = one_hot((16, 4), lambda r, l: r, lambda r, l: l * 4 + quarter)
    tile = dot(lift.astype(f32).astype(bf16), lanes).astype(bf16)
    small[mine] = jnp.concatenate([sort_own[...].astype(bf16), tile], axis=0)
    steps = GatherSteps(proj, up, down, small, (send, recv))

    def arrived():
        pieces = small[...].reshape(-1, 32, LANES)
        sort_ref[...] = pieces[:, :16].reshape(sort_ref.shape)
        tile = jnp.sum(pieces[:, 16:].astype(f32), axis=0)
        norms_ref[...] = jnp.concatenate(
            [
                jnp.concatenate([tile[4 * i + q : 4 * i + q + 1] for q in range(4)], axis=1)
                for i in range(4)
            ],
            axis=0,
        )

    steps.arrived = arrived

    def columns_of(columns):
        return proj[:, :, :, :, :, columns].reshape(x_ref.shape[1], -1)

    front_steps(steps, columns_of, lengths_ref, norms_ref, x_ref, sort_ref, *rest)


def front_plain_kernel(lengths_ref, norms_ref, x_ref, proj_ref, sort_ref, *rest):
    front_steps(
        Quiet(), lambda columns: proj_ref[:, columns], lengths_ref, norms_ref, x_ref, sort_ref, *rest
    )


def front_steps(
    steps, proj_columns, lengths_ref, norms_ref, x_ref, sort_ref,
    normed_hbm, qkv_hbm, skv_hbm, tkv_hbm, means_ref, states_ref,
    normed_s, stage, matrix, pair_buf, query_buf, low_buf, flip_buf,
    copy_sem, pair_sem, query_sem, low_sem, flip_sem,
):
    seq, width = x_ref.shape
    tiles = seq // TILE
    blocks = seq // BLOCK
    per_tile = TILE // BLOCK
    chunks = 2 * width // LANES
    ends = doc_ends(lengths_ref)
    def centre_step(k, carry):
        rows = pl.ds(pl.multiple_of(k * TILE, TILE), TILE)
        xhat, unused = center_scale(x_ref[rows, :].astype(f32))
        stage[pl.ds(k * (TILE // blocks), TILE // blocks), :, :width] = xhat.reshape(
            TILE // blocks, blocks, width
        )
        return carry

    for quarter in range(4):
        lax.fori_loop(quarter * tiles // 4, (quarter + 1) * tiles // 4, centre_step, 0)
        steps.centred(quarter)
    steps.arrived()
    gain = norms_ref[0:1, :].astype(f32)
    shift = norms_ref[1:2, :].astype(f32)

    def norm_step(k, carry):
        rows = pl.ds(pl.multiple_of(k * TILE, TILE), TILE)
        xhat = stage[pl.ds(k * (TILE // blocks), TILE // blocks), :, :width].reshape(TILE, width)
        normed = (xhat * gain + shift).astype(bf16)
        normed_s[rows, :] = normed
        sums = jnp.sum(normed.astype(f32).reshape(per_tile, BLOCK, width), axis=1)
        means_ref[pl.ds(pl.multiple_of(k * per_tile, per_tile), per_tile), :] = (
            sums * (1.0 / BLOCK)
        ).astype(bf16)
        return carry

    lax.fori_loop(0, tiles // 2, norm_step, 0)
    steps.half_normed()
    lax.fori_loop(tiles // 2, tiles, norm_step, 0)
    normed_copy = pltpu.make_async_copy(normed_s, normed_hbm, copy_sem)
    normed_copy.start()

    logits = dot(means_ref[...], sort_ref[...])
    first_i = segments_of(lax.broadcasted_iota(jnp.int32, (blocks, blocks), 0) * BLOCK, ends)
    first_j = segments_of(lax.broadcasted_iota(jnp.int32, (blocks, blocks), 1) * BLOCK, ends)
    logits = jnp.where(first_i != first_j, logits - mask_penalty, logits)

    def pair_copy(k, slot):
        place = (pl.ds(pl.multiple_of(k * TILE, TILE), TILE), pl.ds(width, 2 * width))
        return pltpu.make_async_copy(pair_buf.at[slot], qkv_hbm.at[place], pair_sem.at[slot])

    def query_copy(k, slot):
        place = (pl.ds(pl.multiple_of(k * TILE, TILE), TILE), pl.ds(0, width))
        return pltpu.make_async_copy(query_buf.at[slot], qkv_hbm.at[place], query_sem.at[slot])

    def project_step(k, logits):
        rows = pl.ds(pl.multiple_of(k * TILE, TILE), TILE)
        slot = lax.rem(k, 2)

        @pl.when(k >= 2)
        def _():
            pair_copy(k - 2, slot).wait()

        steps.project(k)
        logits = logits - log_sum_exp(logits, 1)
        states_ref[2 * k] = jnp.exp(logits)
        logits = logits - log_sum_exp(logits, 0)
        states_ref[2 * k + 1] = jnp.exp(logits)
        normed = normed_s[rows, :]
        product = dot(normed, proj_columns(slice(width, 3 * width))).astype(bf16)
        pair_buf[slot] = product
        spread_tokens(stage, matrix[...], k, product)
        pair_copy(k, slot).start()
        return logits

    assert tiles == SINK_ITERS == BLOCK // flip_buf.shape[0]
    steps.before_project()
    matrix[...] = regroup_matrix(False)
    lax.fori_loop(0, tiles, project_step, logits)
    permute = states_ref[2 * SINK_ITERS - 1].astype(bf16)

    def flip_copy(t, slot):
        return pltpu.make_async_copy(flip_buf.at[slot], tkv_hbm.at[t], flip_sem.at[slot])

    def sort_step(i, carry):
        group = flip_buf.shape[0]
        steps.sort(i)
        rows = pl.ds(pl.multiple_of(i * TILE, TILE), TILE)
        slot = lax.rem(i, 2)

        @pl.when(i >= 2)
        def _():
            query_copy(i - 2, slot).wait()

        query_buf[slot] = dot(normed_s[rows, :], proj_columns(slice(0, width))).astype(bf16)
        query_copy(i, slot).start()

        @pl.when(i >= 1)
        def _():
            for u in range(group):
                flip_copy((i - 1) * group + u, u).wait()

        loaded = []
        for u in range(group):
            t = i * group + u
            loaded.append(stage[t].astype(bf16))
        for u in range(group):
            t = i * group + u
            flip_buf[u] = loaded[u].astype(f32).T.astype(bf16)
            flip_copy(t, u).start()
            stage[t] = dot(permute, loaded[u])
        return carry

    group = flip_buf.shape[0]
    lax.fori_loop(0, BLOCK // group, sort_step, 0)

    def low_copy(k, slot):
        rows = pl.ds(pl.multiple_of(k * TILE, TILE), TILE)
        return pltpu.make_async_copy(low_buf.at[slot], skv_hbm.at[rows, :], low_sem.at[slot])

    def low_step(k, carry):
        rows = pl.ds(pl.multiple_of(k * TILE, TILE), TILE)
        slot = lax.rem(k, 2)

        @pl.when(k >= 2)
        def _():
            low_copy(k - 2, slot).wait()

        steps.low(k)
        low_buf[slot] = collect_tokens(stage, matrix[...], k, TILE).astype(bf16)
        low_copy(k, slot).start()
        return carry

    matrix[...] = regroup_matrix(True)
    lax.fori_loop(0, tiles, low_step, 0)
    for u in range(group):
        flip_copy(BLOCK - group + u, u).wait()
    for k in (tiles - 2, tiles - 1):
        pair_copy(k, k % 2).wait()
        query_copy(k, k % 2).wait()
        low_copy(k, k % 2).wait()
    normed_copy.wait()
    steps.end()


def front_shapes(seq, width):
    blocks = seq // BLOCK
    hbm = pl.BlockSpec(memory_space=pl.ANY)
    vmem = pl.BlockSpec(memory_space=pltpu.VMEM)
    shapes = (
        jax.ShapeDtypeStruct((seq, width), bf16),
        jax.ShapeDtypeStruct((seq, 3 * width), bf16),
        jax.ShapeDtypeStruct((seq, 2 * width), bf16),
        jax.ShapeDtypeStruct((BLOCK, 2 * width, blocks), bf16),
        jax.ShapeDtypeStruct((blocks, width), bf16),
        jax.ShapeDtypeStruct((2 * SINK_ITERS, blocks, blocks), f32),
    )
    scratch = [
            pltpu.VMEM((seq, width), bf16),
            pltpu.VMEM((BLOCK, blocks, 2 * width), f32),
            pltpu.VMEM((GROUP, GROUP), bf16),
            pltpu.VMEM((2, TILE, 2 * width), bf16),
            pltpu.VMEM((2, TILE, width), bf16),
            pltpu.VMEM((2, TILE, 2 * width), bf16),
            pltpu.VMEM((4, 2 * width, blocks), bf16),
            pltpu.SemaphoreType.DMA,
            pltpu.SemaphoreType.DMA((2,)),
            pltpu.SemaphoreType.DMA((2,)),
            pltpu.SemaphoreType.DMA((2,)),
            pltpu.SemaphoreType.DMA((8,)),
    ]
    return shapes, [hbm, hbm, hbm, hbm, vmem, vmem], scratch


def front_plain(lengths, x, *shards):
    proj, up, down, sort, norms = gather_plain(*shards)
    shapes, specs, scratch = front_shapes(*x.shape)
    vmem = pl.BlockSpec(memory_space=pltpu.VMEM)
    results = pl.pallas_call(
        front_plain_kernel,
        out_shape=shapes,
        in_specs=[pl.BlockSpec(memory_space=pltpu.SMEM), vmem, vmem, vmem, vmem],
        out_specs=specs,
        scratch_shapes=scratch,
        compiler_params=pltpu.CompilerParams(vmem_limit_bytes=VMEM_LIMIT),
        name="front",
    )(lengths, norms, x, proj, sort)
    return (proj, up, down, sort, norms, *results)


def front_near(lengths, x, proj, up, down, sort, norm):
    seq, width = x.shape
    shapes, specs, scratch = front_shapes(seq, width)
    vmem = pl.BlockSpec(memory_space=pltpu.VMEM)
    fulls = [jax.ShapeDtypeStruct(SPLIT + own.shape, bf16) for own in (proj, up, down)]
    fulls += [jax.ShapeDtypeStruct((32 * sort.shape[0], LANES), bf16)]
    fulls += [jax.ShapeDtypeStruct((4, width), f32)]
    scratch = scratch + [pltpu.VMEM(SPLIT + (32, LANES), bf16)]
    scratch += [pltpu.SemaphoreType.DMA((GATHERS * COPIES,))] * 2
    results = pl.pallas_call(
        front_near_kernel,
        out_shape=tuple(fulls) + shapes,
        in_specs=[pl.BlockSpec(memory_space=pltpu.SMEM)] + [vmem] * 6,
        out_specs=[vmem] * 5 + specs,
        scratch_shapes=scratch,
        compiler_params=pltpu.CompilerParams(
            collective_id=0, has_side_effects=True, vmem_limit_bytes=VMEM_LIMIT
        ),
        name="front",
    )(lengths, x, proj, up, down, sort, norm)
    return tuple(full.reshape(-1, full.shape[-1]) for full in results[:3]) + tuple(results[3:])


def layer_norm_back(grad, gain, xhat, inverse):
    scaled = grad * gain
    mean_one = jnp.mean(scaled, axis=-1, keepdims=True)
    mean_two = jnp.mean(scaled * xhat, axis=-1, keepdims=True)
    return (scaled - mean_one - xhat * mean_two) * inverse


def middle_kernel(
    lengths_ref, norms_ref, x_ref, cot_ref, qkv_ref, skv_ref, out_proj_ref, up_ref, down_ref,
    y_ref, hidden_grad_ref, gq_ref, gkv_ref, gskv_ref, gup_ref, gdown_ref, gout_ref, gnorm_ref,
    gup, gdown, gout, probs_s, context_s, gcontext_s, gq_s, gkv_s, gskv_s, grads_s,
):
    step = pl.program_id(0)
    tile, width = x_ref.shape
    hidden_units = up_ref.shape[1]
    pairs = tile // (2 * BLOCK)
    head_pairs = width // LANES
    scale = HD ** (-0.5)
    ends = doc_ends(lengths_ref)

    @pl.when(step == 0)
    def _():
        gup[...] = jnp.zeros_like(gup)
        gdown[...] = jnp.zeros_like(gdown)
        gout[...] = jnp.zeros_like(gout)
        gnorm_ref[...] = jnp.zeros_like(gnorm_ref)

    lane = lax.broadcasted_iota(jnp.int32, (1, LANES), 1)
    low_head = lane < HD
    low_block = lax.rem(lane, 2 * BLOCK) < BLOCK
    head_one = low_head.astype(f32).astype(bf16)
    head_two = (1.0 - low_head.astype(f32)).astype(bf16)
    block_one = low_block.astype(f32).astype(bf16)
    block_two = (1.0 - low_block.astype(f32)).astype(bf16)

    def two_heads(part):
        return jnp.concatenate(
            [part * head_one, part * head_two], axis=0
        )

    def two_blocks(part):
        return jnp.concatenate(
            [part * block_one, part * block_two], axis=0
        )

    def stack_keys(own, far):
        return jnp.concatenate(
            [own[:BLOCK], far[:BLOCK], own[BLOCK:], far[BLOCK:]], axis=0
        )

    def pick_block(full):
        return jnp.where(low_block, full[: 2 * BLOCK], full[2 * BLOCK :])

    def pick_head(full):
        return jnp.where(low_head, full[: 2 * BLOCK], full[2 * BLOCK :])

    def attend(p, carry):
        rows = pl.ds(pl.multiple_of(p * 2 * BLOCK, 2 * BLOCK), 2 * BLOCK)
        base = step * tile + p * 2 * BLOCK
        query_seg = segments_of(base + lax.rem(lane, 2 * BLOCK), ends)
        key_place = (
            base
            + jnp.where(low_block, 0, BLOCK)
            + lax.broadcasted_iota(jnp.int32, (BLOCK, LANES), 0)
        )
        same = segments_of(key_place, ends) == query_seg
        for hp in range(head_pairs):
            cols = slice(hp * LANES, (hp + 1) * LANES)
            key_cols = slice(width + hp * LANES, width + (hp + 1) * LANES)
            value_cols = slice(2 * width + hp * LANES, 2 * width + (hp + 1) * LANES)
            queries = two_heads(qkv_ref[rows, cols])
            keys = stack_keys(qkv_ref[rows, key_cols], skv_ref[rows, cols])
            values = stack_keys(qkv_ref[rows, value_cols], skv_ref[rows, key_cols])
            scores = pick_block(dot(keys, queries.astype(f32).T.astype(bf16))) * scale
            scores = jnp.concatenate(
                [jnp.where(same, scores[:BLOCK], score_floor), scores[BLOCK:]], axis=0
            )
            exps = jnp.exp(scores - jnp.max(scores, axis=0, keepdims=True))
            probs = (exps / jnp.sum(exps, axis=0, keepdims=True)).astype(bf16)
            probs_s[p * head_pairs + hp] = probs
            context_s[rows, cols] = pick_head(dot_tn(two_blocks(probs), values)).astype(bf16)
        return carry

    lax.fori_loop(0, pairs, attend, 0, unroll=8)

    inputs = x_ref[...].astype(f32)
    context = context_s[...]
    hidden = inputs + dot(context, out_proj_ref[...])
    xhat_two, inverse_two = center_scale(hidden)
    gain_two = norms_ref[2:3, :].astype(f32)
    normed_two = (xhat_two * gain_two + norms_ref[3:4, :].astype(f32)).astype(bf16)
    normed_two_t = normed_two.T
    cot = cot_ref[...]
    total_out = hidden
    grad_normed_two = None
    root = 0.7978845608028654
    for c in range(hidden_units // TILE):
        cols = slice(c * TILE, (c + 1) * TILE)
        pre = dot(normed_two, up_ref[:, cols])
        grad_act = dot_nt(cot, down_ref[cols, :])
        square = pre * pre
        half_tanh = 0.5 + 0.5 * jnp.tanh(pre * (root + (root * 0.044715) * square))
        act = pre * half_tanh
        slope = half_tanh + act * (1.0 - half_tanh) * (
            2.0 * root + (6.0 * root * 0.044715) * square
        )
        act = act.astype(bf16)
        grad_pre = (grad_act * slope).astype(bf16)
        total_out = total_out + dot(act, down_ref[cols, :])
        back = dot_nt(grad_pre, up_ref[:, cols])
        grad_normed_two = back if grad_normed_two is None else grad_normed_two + back
        gup[:, cols] += dot(normed_two_t, grad_pre)
        gdown[cols, :] += dot_tn(act, cot)
    y_ref[...] = total_out.astype(bf16)
    gnorm_ref[0:1, :] += jnp.sum(grad_normed_two * xhat_two, axis=0, keepdims=True)
    gnorm_ref[1:2, :] += jnp.sum(grad_normed_two, axis=0, keepdims=True)
    hidden_grad = cot.astype(f32) + layer_norm_back(
        grad_normed_two, gain_two, xhat_two, inverse_two
    )
    grad_attn = hidden_grad.astype(bf16)
    hidden_grad_ref[...] = grad_attn
    gout[...] += dot_tn(context, grad_attn)
    gcontext_s[...] = dot_nt(grad_attn, out_proj_ref[...]).astype(bf16)

    def attend_back(p, carry):
        rows = pl.ds(pl.multiple_of(p * 2 * BLOCK, 2 * BLOCK), 2 * BLOCK)
        for hp in range(head_pairs):
            cols = slice(hp * LANES, (hp + 1) * LANES)
            key_cols = slice(width + hp * LANES, width + (hp + 1) * LANES)
            value_cols = slice(2 * width + hp * LANES, 2 * width + (hp + 1) * LANES)
            values = stack_keys(qkv_ref[rows, value_cols], skv_ref[rows, key_cols])
            gcontext = two_heads(gcontext_s[rows, cols])
            wide = probs_s[p * head_pairs + hp].astype(f32)
            grad_probs = pick_block(dot(values, gcontext.astype(f32).T.astype(bf16)))
            weighted = wide * grad_probs
            grad_scores = weighted - wide * jnp.sum(weighted, axis=0, keepdims=True)
            grad_scores = (grad_scores * scale).astype(bf16)
            grads_s[p * head_pairs + hp] = grad_scores
        return carry

    lax.fori_loop(0, pairs, attend_back, 0, unroll=8)

    def attend_last(p, carry):
        rows = pl.ds(pl.multiple_of(p * 2 * BLOCK, 2 * BLOCK), 2 * BLOCK)
        for hp in range(head_pairs):
            cols = slice(hp * LANES, (hp + 1) * LANES)
            key_cols = slice(width + hp * LANES, width + (hp + 1) * LANES)
            value_cols = slice(2 * width + hp * LANES, 2 * width + (hp + 1) * LANES)
            keys = stack_keys(qkv_ref[rows, key_cols], skv_ref[rows, cols])
            gq_s[rows, cols] = pick_head(dot_tn(two_blocks(grads_s[p * head_pairs + hp]), keys)).astype(bf16)
            gkeys = dot(two_blocks(grads_s[p * head_pairs + hp]), two_heads(qkv_ref[rows, cols])).astype(bf16)
            gvalues = dot(two_blocks(probs_s[p * head_pairs + hp]), two_heads(gcontext_s[rows, cols])).astype(bf16)
            for grads, where in ((gkeys, cols), (gvalues, key_cols)):
                gkv_s[rows, where] = jnp.concatenate(
                    [grads[:BLOCK], grads[2 * BLOCK : 3 * BLOCK]], axis=0
                )
                gskv_s[rows, where] = jnp.concatenate(
                    [grads[BLOCK : 2 * BLOCK], grads[3 * BLOCK :]], axis=0
                )
        return carry

    lax.fori_loop(0, pairs, attend_last, 0, unroll=8)
    gq_ref[...] = gq_s[...]
    gkv_ref[...] = gkv_s[...]
    gskv_ref[...] = gskv_s[...]

    @pl.when(step == pl.num_programs(0) - 1)
    def _():
        gup_ref[...] = gup[...].astype(bf16)
        gdown_ref[...] = gdown[...].astype(bf16)
        gout_ref[...] = gout[...].astype(bf16)


def middle(lengths, norms, x, cot, qkv, skv, proj, up, down):
    seq, width = x.shape
    hidden_units = up.shape[1]
    tiles = seq // TILE

    def rows(columns):
        return pl.BlockSpec((TILE, columns), lambda i: (i, 0))

    def fixed(shape, index=(0, 0)):
        return pl.BlockSpec(shape, lambda i: index, pipeline_mode=pl.Buffered(1))

    return pl.pallas_call(
        middle_kernel,
        grid=(tiles,),
        out_shape=(
            jax.ShapeDtypeStruct((seq, width), bf16),
            jax.ShapeDtypeStruct((seq, width), bf16),
            jax.ShapeDtypeStruct((seq, width), bf16),
            jax.ShapeDtypeStruct((seq, 2 * width), bf16),
            jax.ShapeDtypeStruct((seq, 2 * width), bf16),
            jax.ShapeDtypeStruct((width, hidden_units), bf16),
            jax.ShapeDtypeStruct((hidden_units, width), bf16),
            jax.ShapeDtypeStruct((width, width), bf16),
            jax.ShapeDtypeStruct((2, width), f32),
        ),
        in_specs=[
            pl.BlockSpec(memory_space=pltpu.SMEM),
            fixed(norms.shape),
            rows(width),
            rows(width),
            rows(3 * width),
            rows(2 * width),
            fixed((width, width), (0, 3)),
            fixed(up.shape),
            fixed(down.shape),
        ],
        out_specs=[
            rows(width),
            rows(width),
            rows(width),
            rows(2 * width),
            rows(2 * width),
            fixed((width, hidden_units)),
            fixed((hidden_units, width)),
            fixed((width, width)),
            fixed((2, width)),
        ],
        scratch_shapes=[
            pltpu.VMEM((width, hidden_units), f32),
            pltpu.VMEM((hidden_units, width), f32),
            pltpu.VMEM((width, width), f32),
            pltpu.VMEM((TILE // (2 * BLOCK) * (width // LANES), 2 * BLOCK, LANES), bf16),
            pltpu.VMEM((TILE, width), bf16),
            pltpu.VMEM((TILE, width), bf16),pltpu.VMEM((TILE, width), bf16),pltpu.VMEM((TILE, 2*width), bf16),pltpu.VMEM((TILE, 2*width), bf16),
            pltpu.VMEM((TILE // (2 * BLOCK) * (width // LANES), 2 * BLOCK, LANES), bf16),
        ],
        compiler_params=pltpu.CompilerParams(vmem_limit_bytes=VMEM_LIMIT),
        name="middle",
    )(lengths, norms, x, cot, qkv, skv, proj, up, down)


def add_low(*parts):
    total = parts[0].astype(f32)
    for part in parts[1:]:
        total = total + part.astype(f32)
    return total


class Reduce:
    def __init__(self, part, total, columns, got_c, got_xy, got_z, sems, base):
        self.part, self.total, self.columns = part, total, columns
        self.whole = (slice(None), columns)
        self.got_c, self.got_xy, self.got_z = got_c, got_xy, got_z
        self.sems, self.base = sems, base

    def copies(self, step):
        z, x, y, c = coordinates()
        every = slice(None)

        def one(source, target, index, device):
            return remote(source, target, self.sems, self.base + index, device)

        if step == 0:
            away = self.part.at[(every, every, every, 1 - c) + self.whole]
            return [one(away, self.got_c, 0, device_of(z, x, y, 1 - c))]
        if step == 1:
            return [
                one(self.got_c.at[(every,) + other], self.got_xy.at[k], 1 + k, device_of(z, *other, c))
                for k, other in enumerate(xy_others(x, y))
            ]
        return [
            one(self.got_c.at[other, x, y], self.got_z.at[k], 4 + k, device_of(other, x, y, c))
            for k, other in enumerate(z_others(z))
        ]

    def start(self, step):
        start_all(self.copies(step))

    def turn(self, step):
        wait_all(self.copies(step))
        self.add(step)
        if step < 2:
            self.start(step + 1)

    def add(self, step):
        z, x, y, c = coordinates()
        if step == 2:
            self.total[:, self.columns] = add_low(
                self.got_c[z, x, y], *[self.got_z[k] for k in range(3)]
            )
            return

        def line(i, carry):
            if step == 0:
                for j in range(2):
                    for k in range(2):
                        self.got_c[i, j, k] = add_low(
                            self.part[(i, j, k, c) + self.whole], self.got_c[i, j, k]
                        ).astype(bf16)
            else:
                self.got_c[i, x, y] = add_low(
                    self.got_c[i, x, y], *[self.got_xy[k, i] for k in range(3)]
                ).astype(bf16)
            return carry

        lax.fori_loop(0, 4, line, 0)


def reduce_scratch(rows, columns):
    shapes = ((4, 2, 2, rows, columns), (3, 4, rows, columns), (3, rows, columns))
    return [pltpu.VMEM(shape, bf16) for shape in shapes]


class ReduceSteps:
    def __init__(self, plans):
        self.up, self.down, self.out, self.query = plans

    def begin(self):
        pass

    def send(self):
        await_neighbours()
        self.up.start(0)
        self.down.start(0)
        self.out.start(0)

    def during_query(self, k):
        pl.when(k == 1)(self.send)
        self.when(k, 6, self.up, 0)

    def queried(self):
        self.query.start(0)

    def load(self, k):
        self.when(k, 1, self.down, 0)
        self.when(k, 3, self.out, 0)
        self.when(k, 6, self.query, 0)

    def loaded(self):
        pass

    def sort(self, i):
        self.when(i, 7, self.up, 1)

    def swept(self):
        pass

    def weights(self, k):
        self.when(k, 2, self.down, 1)
        self.when(k, 4, self.out, 1)
        self.when(k, 5, self.query, 1)
        self.when(k, 6, self.up, 2)

    def end(self):
        pass

    def inputs(self, k, pair):
        self.when(k, 1, self.down, 2)
        self.when(k, 2, pair, 0)
        self.when(k, 3, self.out, 2)
        self.when(k, 5, self.query, 2)

    def when(self, k, place, plan, step):
        pl.when(k == place)(functools.partial(plan.turn, step))


def norm_rows(grads):
    rows = []
    for grad in grads:
        for i in range(grad.shape[0]):
            for q in range(grad.shape[1] // LANES):
                rows.append(grad[i : i + 1, q * LANES : (q + 1) * LANES])
    return jnp.concatenate(rows, axis=0)


def back_near_kernel(*refs):
    ins, refs = refs[:8], refs[8:]
    (gout, gup, gdown, gtwo_ref, norms_ref, proj_ref, x_hbm), refs = refs[:7], refs[7:]
    gx_hbm, refs = refs[0], refs[1:]
    (query_sum, pair_sum, out_sum, up_sum, down_sum, sort_sum, norm_sum), refs = refs[:7], refs[7:]
    work, refs = refs[:8], refs[8:]
    (gsum, gpair, gsort, gmeans, gquery, gone_ref, small, small_sum), refs = refs[:8], refs[8:]
    (send, recv), scratch = refs[:2], refs[2:]
    greet_neighbours()
    every = slice(None)
    places = (
        (gup, up_sum, every), (gdown, down_sum, every), (gout, out_sum, every),
        (gquery, query_sum, every), (gpair, pair_sum, every), (small, small_sum, every),
    )
    plans = [
        Reduce(*place, *scratch[3 * b : 3 * b + 3], (send, recv), COPIES * b)
        for b, place in enumerate(places)
    ]
    pair, small_plan = plans[4:]
    steps = ReduceSteps(plans[:4])
    back_steps(steps, *ins, gsum, gpair, gsort, gmeans, gquery, *work)
    pair.start(0)
    seq, width = x_hbm.shape
    gone_ref[...] = jnp.zeros_like(gone_ref)

    def input_step(x_ref, gq_ref, gx_ref):
        k = pl.program_id(0)
        steps.inputs(k, pair)
        part = TILE // BLOCK
        means = gmeans[pl.ds(pl.multiple_of(k * part, part), part), :]
        gkv = gsum[pl.ds(pl.multiple_of(k * TILE, TILE), TILE), :]
        input_tile(norms_ref, x_ref, gq_ref, gkv, means, proj_ref, gx_ref, gone_ref)

    def rows_of(columns):
        return pl.BlockSpec((TILE, columns), lambda i: (i, 0))

    pltpu.emit_pipeline(
        input_step,
        grid=(seq // TILE,),
        in_specs=[rows_of(width)] * 2,
        out_specs=[rows_of(width)],
    )(x_hbm, ins[6], gx_hbm)
    tile = norm_rows((gone_ref[...], gtwo_ref[...])).astype(bf16)
    small[:, :, :, :, :16] = gsort[...].astype(bf16).reshape(SPLIT + (width // 32, LANES))
    for i in range(4):
        for j in range(2):
            for k in range(2):
                for m in range(2):
                    small[i, j, k, m, 16:] = tile
    small_plan.start(0)
    small_plan.turn(0)
    pair.turn(1)
    small_plan.turn(1)
    small_plan.turn(2)
    pair.turn(2)
    sort_sum[...] = small_sum[:16, :]
    quarter, eighth = norm_place()
    own = norm_sum.shape[1]
    drop = one_hot((4, 16), lambda r, l: r * 4 + quarter, lambda r, l: l).astype(f32)
    pick = one_hot((LANES, own), lambda r, l: r, lambda r, l: l + eighth * own).astype(f32)

    def exact(left, right):
        return lax.dot_general(
            left, right, (((1,), (0,)), ((), ())),
            precision=lax.Precision.HIGHEST, preferred_element_type=f32,
        )

    norm_sum[...] = exact(exact(drop, small_sum[16:, :]), pick)


def back_plain_kernel(*refs):
    back_steps(Quiet(), *refs)


def back_steps(
    steps, gskv_hbm, tkv_hbm, states_ref, means_ref, sort_ref,
    normed_hbm, gq_hbm, gkv_hbm,
    gsum, gpair_ref, gsort_ref, gmeans, gquery_ref,
    stage, matrix, low_buf, flip_buf, gproj, gperm, low_sem, flip_sem,
):
    steps.begin()
    seq, width = normed_hbm.shape
    tiles = seq // TILE
    blocks = seq // BLOCK
    chunks = 2 * width // LANES
    per_tile = TILE // BLOCK

    def low_copy(k, slot):
        rows = pl.ds(pl.multiple_of(k * TILE, TILE), TILE)
        return pltpu.make_async_copy(gskv_hbm.at[rows, :], low_buf.at[slot], low_sem.at[slot])

    group = flip_buf.shape[0] // 2

    def flip_copy(t, slot):
        return pltpu.make_async_copy(tkv_hbm.at[t], flip_buf.at[slot], flip_sem.at[slot])

    low_copy(0, 0).start()
    low_copy(1, 1).start()
    for u in range(group):
        flip_copy(u, u).start()

    def load_step(k, carry):
        rows = pl.ds(pl.multiple_of(k * TILE, TILE), TILE)
        slot = lax.rem(k, 2)
        low_copy(k, slot).wait()
        steps.load(k)
        spread_tokens(stage, matrix[...], k, low_buf[slot])

        @pl.when(k + 2 < tiles)
        def _():
            low_copy(k + 2, slot).start()

        return carry

    def rows_of(columns):
        return pl.BlockSpec((TILE, columns), lambda i: (i, 0))

    gproj[...] = jnp.zeros_like(gproj)

    def query_step(normed_ref, gq_ref):
        steps.during_query(pl.program_id(0))
        gproj[:, :width] += dot_tn(normed_ref[...], gq_ref[...])

    pltpu.emit_pipeline(query_step, grid=(tiles,), in_specs=[rows_of(width)] * 2)(
        normed_hbm, gq_hbm
    )
    gquery_ref[...] = gproj[:, :width].astype(bf16).reshape(gquery_ref.shape)
    steps.queried()
    matrix[...] = regroup_matrix(False)
    lax.fori_loop(0, tiles, load_step, 0)
    matrix[...] = regroup_matrix(True)
    steps.loaded()

    final = states_ref[2 * SINK_ITERS - 1]
    permute_t = final.T.astype(bf16)
    gperm[...] = jnp.zeros_like(gperm)

    def sort_step(i, carry):
        side = lax.rem(i, 2) * group
        steps.sort(i)

        @pl.when(i + 1 < BLOCK // group)
        def _():
            for u in range(group):
                flip_copy((i + 1) * group + u, group - side + u).start()

        for u in range(group):
            flip_copy(i * group + u, side + u).wait()
        loaded = []
        for u in range(group):
            t = i * group + u
            loaded.append(stage[t].astype(bf16))
        total = gperm[...]
        for u in range(group):
            t = i * group + u
            total = total + dot(loaded[u], flip_buf[side + u])
            stage[t] = dot(permute_t, loaded[u])
        gperm[...] = total
        return carry

    lax.fori_loop(0, BLOCK // group, sort_step, 0)

    grad = gperm[...] * final
    for sweep in reversed(range(SINK_ITERS)):
        grad = grad - states_ref[2 * sweep + 1] * jnp.sum(grad, axis=0, keepdims=True)
        grad = grad - states_ref[2 * sweep] * jnp.sum(grad, axis=1, keepdims=True)
    grad = grad.astype(bf16)
    gsort_ref[...] = dot_tn(means_ref[...], grad).astype(gsort_ref.dtype)
    gmeans[...] = dot_nt(grad, sort_ref[...]) * (1.0 / BLOCK)
    steps.swept()

    def weight_step(normed_ref, gkv_ref):
        k = pl.program_id(0)
        steps.weights(k)
        gkv = (gkv_ref[...].astype(f32) + collect_tokens(stage, matrix[...], k, TILE)).astype(bf16)
        gsum[pl.ds(pl.multiple_of(k * TILE, TILE), TILE), :] = gkv
        gproj[:, width:] += dot_tn(normed_ref[...], gkv)

    pltpu.emit_pipeline(
        weight_step,
        grid=(tiles,),
        in_specs=[rows_of(width), rows_of(2 * width)],
    )(normed_hbm, gkv_hbm)
    gpair_ref[...] = gproj[:, width:].astype(bf16).reshape(gpair_ref.shape)
    steps.end()


def back_scratch(seq, width):
    blocks = seq // BLOCK
    return [
            pltpu.VMEM((BLOCK, blocks, 2 * width), f32),
            pltpu.VMEM((GROUP, GROUP), bf16),
            pltpu.VMEM((2, TILE, 2 * width), bf16),
            pltpu.VMEM((8, 2 * width, blocks), bf16),
            pltpu.VMEM((width, 3 * width), f32),
            pltpu.VMEM((blocks, blocks), f32),
            pltpu.SemaphoreType.DMA((2,)),
            pltpu.SemaphoreType.DMA((8,)),
    ]


def back_shapes(seq, width):
    hbm = pl.BlockSpec(memory_space=pl.ANY)
    vmem = pl.BlockSpec(memory_space=pltpu.VMEM)
    blocks = seq // BLOCK
    shapes = (
        jax.ShapeDtypeStruct((seq, 2 * width), bf16),
        jax.ShapeDtypeStruct((width, 2 * width), bf16),
        jax.ShapeDtypeStruct((width, blocks), f32),
        jax.ShapeDtypeStruct((blocks, width), f32),
    )
    return shapes, [hbm, hbm, vmem, vmem, vmem, hbm, hbm, hbm], [vmem, vmem, vmem, vmem]


def back_plain(seq, width, ins, gout, gup, gdown):
    shapes, in_specs, out_specs = back_shapes(seq, width)
    gsum, gpair, gsort, gmeans, gquery = pl.pallas_call(
        back_plain_kernel,
        out_shape=shapes + (jax.ShapeDtypeStruct((width, width), bf16),),
        in_specs=in_specs,
        out_specs=out_specs + [pl.BlockSpec(memory_space=pltpu.VMEM)],
        scratch_shapes=back_scratch(seq, width),
        compiler_params=pltpu.CompilerParams(vmem_limit_bytes=VMEM_LIMIT),
        name="back",
    )(*ins)
    return gsum, gpair, gsort, gmeans, gquery, gout, gup, gdown


def split_shards(grad):
    return grad.reshape(SPLIT + (grad.shape[0] // 32, grad.shape[1]))


def back_near(seq, width, ins, gout, gup, gdown, gtwo, norms, proj, x):
    shapes, in_specs, unused = back_shapes(seq, width)
    hbm = pl.BlockSpec(memory_space=pl.ANY)
    vmem = pl.BlockSpec(memory_space=pltpu.VMEM)
    gout, gup, gdown = split_shards(gout), split_shards(gup), split_shards(gdown)
    blocks = seq // BLOCK
    query, pair, small = (width // 32, width), (width // 32, 2 * width), (32, LANES)
    scratch = back_scratch(seq, width) + [
        pltpu.VMEM((seq, 2 * width), bf16),
        pltpu.VMEM(SPLIT + pair, bf16),
        pltpu.VMEM((width, blocks), f32),
        pltpu.VMEM((blocks, width), f32),
        pltpu.VMEM(SPLIT + query, bf16),
        pltpu.VMEM((2, width), f32),
        pltpu.VMEM(SPLIT + small, bf16),
        pltpu.VMEM(small, f32),
    ]
    scratch += [pltpu.SemaphoreType.DMA((6 * COPIES,))] * 2
    for shape in (gup.shape[-2:], gdown.shape[-2:], gout.shape[-2:], query, pair, small):
        scratch += reduce_scratch(*shape)
    sums = [query, pair, gout.shape[-2:], gup.shape[-2:], gdown.shape[-2:]]
    sums += [(width // 32, blocks), (4, width // 32)]
    gx, *totals = pl.pallas_call(
        back_near_kernel,
        out_shape=(jax.ShapeDtypeStruct((seq, width), bf16),)
        + tuple(jax.ShapeDtypeStruct(shape, f32) for shape in sums),
        in_specs=in_specs + [vmem] * 6 + [hbm],
        out_specs=[hbm] + [vmem] * 7,
        scratch_shapes=scratch,
        compiler_params=pltpu.CompilerParams(
            collective_id=1, has_side_effects=True, vmem_limit_bytes=VMEM_LIMIT
        ),
        name="back",
    )(*ins, gout, gup, gdown, gtwo, norms, proj, x)
    return gx, totals


def input_tile(
    norms_ref, x_ref, gq_ref, gkv, means, proj_ref, gx_ref, gnorm_ref
):
    tile, width = x_ref.shape
    grad_normed = dot_nt(gq_ref[...], proj_ref[:, :width])
    grad_normed = grad_normed + dot_nt(gkv, proj_ref[:, width : 3 * width])
    grad_normed = grad_normed + jnp.broadcast_to(
        means[:, None, :], (tile // BLOCK, BLOCK, width)
    ).reshape(tile, width)
    xhat, inverse = center_scale(x_ref[...].astype(f32))
    gnorm_ref[0:1, :] += jnp.sum(grad_normed * xhat, axis=0, keepdims=True)
    gnorm_ref[1:2, :] += jnp.sum(grad_normed, axis=0, keepdims=True)
    gain = norms_ref[0:1, :].astype(f32)
    gx_ref[...] = layer_norm_back(grad_normed, gain, xhat, inverse).astype(bf16)


def inputs_kernel(
    norms_ref, x_ref, gq_ref, gsum_ref, gmeans_ref, proj_ref, gx_ref, gnorm_ref
):
    @pl.when(pl.program_id(0) == 0)
    def _():
        gnorm_ref[...] = jnp.zeros_like(gnorm_ref)

    input_tile(
        norms_ref, x_ref, gq_ref, gsum_ref[...], gmeans_ref[...], proj_ref, gx_ref, gnorm_ref
    )


def inputs_back(norms, x, gq, gsum, gmeans, proj):
    seq, width = x.shape

    def rows(columns):
        return pl.BlockSpec((TILE, columns), lambda i: (i, 0))

    def fixed(shape):
        return pl.BlockSpec(shape, lambda i: (0, 0), pipeline_mode=pl.Buffered(1))

    return pl.pallas_call(
        inputs_kernel,
        grid=(seq // TILE,),
        out_shape=(
            jax.ShapeDtypeStruct((seq, width), bf16),
            jax.ShapeDtypeStruct((2, width), f32),
        ),
        in_specs=[
            fixed(norms.shape), rows(width), rows(width), rows(2 * width),
            pl.BlockSpec((TILE // BLOCK, width), lambda i: (i, 0)), fixed(proj.shape),
        ],
        out_specs=[rows(width), fixed((2, width))],
        compiler_params=pltpu.CompilerParams(vmem_limit_bytes=VMEM_LIMIT),
        name="inputs",
    )(norms, x, gq, gsum, gmeans, proj)


def last_plain(gpair, gsort, gone, gtwo, gquery, gout, gup, gdown):
    grads = (gquery, gpair, gout, gup, gdown, gsort, jnp.concatenate([gone, gtwo], axis=0))
    return tuple(
        lax.psum_scatter(
            grad.astype(f32), AXES, scatter_dimension=1 if b == 6 else 0, tiled=True
        )
        for b, grad in enumerate(grads)
    )


def adamw(master, first, second, grad, rate, decay):
    first_new = beta_first * first + (1.0 - beta_first) * grad
    second_new = beta_second * second + (1.0 - beta_second) * grad * grad
    first_hat = first_new / (1.0 - beta_first**STEP)
    second_hat = second_new / (1.0 - beta_second**STEP)
    master_new = master - rate * (first_hat / (jnp.sqrt(second_hat) + adam_eps) + decay * master)
    return (master_new, first_new, second_new)


RATES = (
    (rate_matrix, weight_decay), (rate_matrix, weight_decay), (rate_matrix, weight_decay),
    (rate_other, weight_decay), (rate_other, 0.0),
)


def update_kernel(*refs):
    parts, sums, states, gx_out, results = refs[:2], refs[2:9], refs[9:24], refs[24], refs[25:]

    def add_step(hidden_grad, norm_grad, target):
        pl.when(pl.program_id(0) == 1)(functools.partial(update_shards, sums, states, results))
        target[...] = hidden_grad[...].astype(f32) + norm_grad[...].astype(f32)

    rows = pl.BlockSpec((2 * TILE, gx_out.shape[1]), lambda i: (i, 0))
    pltpu.emit_pipeline(
        add_step, grid=(gx_out.shape[0] // (2 * TILE),), in_specs=[rows] * 2, out_specs=[rows]
    )(*parts, gx_out)


def update_shards(sums, states, results):
    sums = [jnp.concatenate([ref[...] for ref in sums[:3]], axis=1)] + [ref[...] for ref in sums[3:]]
    for b, (rate, decay) in enumerate(RATES):
        state = [ref[...] for ref in states[3 * b : 3 * b + 3]]
        for ref, value in zip(
            results[3 * b : 3 * b + 3], adamw(*state, sums[b], rate, decay)
        ):
            ref[...] = value


def update(hidden_grad, gx, sums, states):
    vmem = pl.BlockSpec(memory_space=pltpu.VMEM)
    hbm = pl.BlockSpec(memory_space=pl.ANY)
    return pl.pallas_call(
        update_kernel,
        out_shape=tuple(jax.ShapeDtypeStruct(array.shape, f32) for array in (gx, *states)),
        in_specs=[hbm] * 2 + [vmem] * 22,
        out_specs=[hbm] + [vmem] * 15,
        compiler_params=pltpu.CompilerParams(vmem_limit_bytes=VMEM_LIMIT),
        name="update",
    )(hidden_grad, gx, *sums, *states)


def gather_plain(proj, up, down, sort, norm):
    def gathered(shard, axis):
        return lax.all_gather(shard.astype(bf16), AXES, axis=axis, tiled=True)

    return (*(gathered(shard, 0) for shard in (proj, up, down, sort)), gathered(norm, 1))


def body(near, layer_input, doc_lengths, out_cotangent, *states):
    x = layer_input[0]
    cot = out_cotangent[0]
    proj, up, down, sort, norms, normed, qkv, skv, tkv, means, kept = (
        front_near if near else front_plain
    )(doc_lengths, x, *states[::3])
    y, hidden_grad, gq, gkv, gskv, gup, gdown, gout, gnorm_two = middle(
        doc_lengths, norms, x, cot, qkv, skv, proj, up, down
    )
    ins = (gskv, tkv, kept, means, sort, normed, gq, gkv)
    if near:
        gx, sums = back_near(
            *x.shape, ins, gout, gup, gdown, gnorm_two, norms, proj, x
        )
    else:
        gsum, gpair, gsort, gmeans, *done = back_plain(*x.shape, ins, gout, gup, gdown)
        gx, gnorm_one = inputs_back(norms, x, gq, gsum, gmeans, proj)
        sums = last_plain(gpair, gsort, gnorm_one, gnorm_two, *done)
    gx, *updates = update(hidden_grad, gx, sums, states)
    return (y[None], gx[None], *updates)


def solution(mesh):
    rows3, rows2, columns = P(AXES, None, None), P(AXES, None), P(None, AXES)
    near = (mesh.shape["dp"], mesh.shape["fsdp"]) == (8, 4)
    return jax.shard_map(
        functools.partial(body, near),
        mesh=mesh,
        in_specs=(rows3, rows2, rows3) + (rows2,) * 12 + (columns,) * 3,
        out_specs=(rows3, rows3) + (rows2,) * 12 + (columns,) * 3,
        check_vma=False,
    )
```

```python
import functools
import jax
import jax.numpy as jnp
from jax import lax
from jax.experimental import pallas as pl
from jax.experimental.pallas import tpu as pltpu
from jax.sharding import PartitionSpec as P

HD = 64
BLOCK = 32
SINK_ITERS = 8
STEP = 10
TILE = 512
LANES = 128

mask_penalty = 6.0
score_floor = -1000000000.0
norm_eps = 1e-05
beta_first = 0.9
beta_second = 0.95
adam_eps = 1e-08
weight_decay = 0.1
rate_matrix = 0.1
rate_other = 0.5

bf16 = jnp.bfloat16
f32 = jnp.float32
VMEM_LIMIT = 62 * 2**20


def dot(left, right):
    return lax.dot_general(left, right, (((1,), (0,)), ((), ())), preferred_element_type=f32)


def dot_nt(left, right):
    return lax.dot_general(left, right, (((1,), (1,)), ((), ())), preferred_element_type=f32)


def dot_tn(left, right):
    return lax.dot_general(left, right, (((0,), (0,)), ((), ())), preferred_element_type=f32)


def doc_ends(lengths_ref):
    total = lengths_ref[0, 0]
    ends = [total]
    for k in range(1, lengths_ref.shape[1]):
        total = total + lengths_ref[0, k]
        ends.append(total)
    return ends


def segments_of(places, ends):
    count = jnp.zeros(places.shape, jnp.int32)
    for end in ends:
        count = count + (places >= end).astype(jnp.int32)
    return count


def center_scale(values):
    centre = values - jnp.mean(values, axis=-1, keepdims=True)
    spread = jnp.mean(centre * centre, axis=-1, keepdims=True)
    inverse = lax.rsqrt(spread + norm_eps)
    return centre * inverse, inverse


def log_sum_exp(logits, axis):
    top = jnp.max(logits, axis=axis, keepdims=True)
    return top + jnp.log(jnp.sum(jnp.exp(logits - top), axis=axis, keepdims=True))


MESH_ID = pl.DeviceIdType.MESH
AXES = ("dp", "fsdp")
SPLIT = (4, 2, 2, 2)
COPIES = 8


def coordinates():
    dp, fsdp = lax.axis_index("dp"), lax.axis_index("fsdp")
    return dp // 2, dp % 2, fsdp // 2, fsdp % 2


def device_of(z, x, y, c):
    return (z * 2 + x, y * 2 + c)


def z_others(z):
    return (z + 1 - 2 * (z % 2), (z + 2) % 4, 3 - z)


def xy_others(x, y):
    return ((1 - x, y), (x, 1 - y), (1 - x, 1 - y))


def neighbours():
    z, x, y, c = coordinates()
    return (
        [device_of(one, x, y, c) for one in z_others(z)]
        + [device_of(z, *one, c) for one in xy_others(x, y)]
        + [device_of(z, x, y, 1 - c)]
    )


def greet_neighbours():
    for peer in neighbours():
        pl.semaphore_signal(
            pltpu.get_barrier_semaphore(), inc=1, device_id=peer, device_id_type=MESH_ID
        )


def await_neighbours():
    pl.semaphore_wait(pltpu.get_barrier_semaphore(), len(neighbours()))


def remote(source, target, sems, index, device):
    send, recv = sems
    return pltpu.make_async_remote_copy(
        src_ref=source, dst_ref=target, send_sem=send.at[index], recv_sem=recv.at[index],
        device_id=device, device_id_type=MESH_ID,
    )


def gather_stages(full, sems, base, start=0, size=None):
    z, x, y, c = coordinates()
    whole = (slice(None), pl.ds(start, size or full.shape[-1]))
    every = slice(None)

    def same(index, place, device):
        part = full.at[place + whole]
        return remote(part, part, sems, base + index, device)

    def stage_z():
        return [
            same(k, (z, x, y, c), device_of(one, x, y, c)) for k, one in enumerate(z_others(z))
        ]

    def stage_xy():
        return [
            same(3 + k, (every, x, y, c), device_of(z, *one, c))
            for k, one in enumerate(xy_others(x, y))
        ]

    def stage_core():
        return [same(6, (every, every, every, c), device_of(z, x, y, 1 - c))]

    return [stage_z, stage_xy, stage_core]


def gather_by_halves(full, sems, base, start=0, size=None):
    z, x, y, c = coordinates()
    size = size or full.shape[-1]
    every = slice(None)
    first = (every, pl.ds(start, size // 2))
    second = (every, pl.ds(start + size // 2, size // 2))
    whole = (every, pl.ds(start, size))
    to_x, to_y = device_of(z, 1 - x, y, c), device_of(z, x, 1 - y, c)

    def same(index, place, device):
        part = full.at[place]
        return remote(part, part, sems, base + index, device)

    def stage_z():
        return [
            same(k, (z, x, y, c) + whole, device_of(one, x, y, c))
            for k, one in enumerate(z_others(z))
        ]

    def stage_one():
        return [
            same(3, (every, x, y, c) + first, to_x), same(4, (every, x, y, c) + second, to_y)
        ]

    def stage_two():
        return [
            same(5, (every, every, y, c) + first, to_y),
            same(6, (every, x, every, c) + second, to_x),
        ]

    def stage_core():
        return [same(7, (every, every, every, c) + whole, device_of(z, x, y, 1 - c))]

    return [stage_z, stage_one, stage_two, stage_core]


def start_all(copies):
    for copy in copies:
        copy.start()


def wait_all(copies):
    for copy in copies:
        copy.wait()


def one_hot(shape, row_of, column_of):
    rows = lax.broadcasted_iota(jnp.int32, shape, 0)
    columns = lax.broadcasted_iota(jnp.int32, shape, 1)
    return row_of(rows, columns) == column_of(rows, columns)


def norm_place():
    z, x, y, c = coordinates()
    device = (z * 2 + x) * 4 + y * 2 + c
    return device // 8, device % 8


GROUP = 8 * BLOCK


def regroup_matrix(inverse):
    rows = lax.broadcasted_iota(jnp.int32, (GROUP, GROUP), 1 if inverse else 0)
    columns = lax.broadcasted_iota(jnp.int32, (GROUP, GROUP), 0 if inverse else 1)
    hit = (rows // 8 == columns % BLOCK) & (rows % 8 == columns // BLOCK)
    return hit.astype(f32).astype(bf16)


def spread_tokens(stage, matrix, k, part):
    columns = part.shape[1]
    for g in range(part.shape[0] // GROUP):
        place = pl.multiple_of((k * (part.shape[0] // GROUP) + g) * 8, 8)
        moved = dot(matrix, part[g * GROUP : (g + 1) * GROUP])
        stage[:, pl.ds(place, 8), :] = moved.reshape(BLOCK, 8, columns)


def collect_tokens(stage, matrix, k, rows):
    parts = []
    for g in range(rows // GROUP):
        place = pl.multiple_of((k * (rows // GROUP) + g) * 8, 8)
        part = stage[:, pl.ds(place, 8), :].reshape(GROUP, stage.shape[2]).astype(bf16)
        parts.append(dot(matrix, part))
    return jnp.concatenate(parts, axis=0)


class Quiet:
    def __getattr__(self, name):
        return lambda *unused: None


GATHERS = 6


class GatherSteps:
    def __init__(self, proj, up, down, small, sems):
        width = proj.shape[-1] // 4
        pieces = [(small, 0, None)]
        pieces += [(proj, width, 2 * width), (proj, 0, width), (proj, 3 * width, width)]
        pieces += [(up, 0, None), (down, 0, None)]
        plans = [
            (gather_stages if b < 3 else gather_by_halves)(piece[0], sems, COPIES * b, *piece[1:])
            for b, piece in enumerate(pieces)
        ]
        self.small, self.pair, self.queries, self.out, self.up, self.down = plans

    def start(self, plan):
        start_all(plan[0]())

    def turn(self, plan, step):
        wait_all(plan[step]())
        if step + 1 < len(plan):
            start_all(plan[step + 1]())

    def centred(self, quarter):
        if quarter == 0:
            await_neighbours()
            self.start(self.small)
            self.start(self.pair)
        else:
            self.turn(self.small, quarter - 1)
        if quarter == 1:
            self.turn(self.pair, 0)
        if quarter == 2:
            self.start(self.queries)
        if quarter == 3:
            self.start(self.up)
            self.start(self.out)

    def half_normed(self):
        self.turn(self.queries, 0)
        self.start(self.down)
        self.turn(self.pair, 1)

    def before_project(self):
        self.turn(self.pair, 2)

    def project(self, k):
        self.when(k, 1, self.queries, 1)
        self.when(k, 2, self.up, 0)
        self.when(k, 2, self.out, 0)
        self.when(k, 3, self.queries, 2)
        self.when(k, 4, self.down, 0)
        self.when(k, 6, self.up, 1)
        self.when(k, 7, self.out, 1)

    def sort(self, i):
        self.when(i, 2, self.down, 1)
        self.when(i, 7, self.up, 2)

    def low(self, k):
        self.when(k, 0, self.out, 2)
        self.when(k, 5, self.down, 2)
        self.when(k, 6, self.up, 3)
        self.when(k, 7, self.out, 3)

    def end(self):
        self.turn(self.down, 3)

    def when(self, k, place, plan, step):
        if step < 0:
            pl.when(k == place)(functools.partial(self.start, plan))
        else:
            pl.when(k == place)(functools.partial(self.turn, plan, step))


def front_near_kernel(
    lengths_ref, x_ref, proj_own, up_own, down_own, sort_own, norm_own,
    proj, up, down, sort_ref, norms_ref, *rest,
):
    rest, (small, send, recv) = rest[:-3], rest[-3:]
    greet_neighbours()
    mine = coordinates()
    proj[mine] = proj_own[...].astype(bf16)
    up[mine] = up_own[...].astype(bf16)
    down[mine] = down_own[...].astype(bf16)
    quarter, eighth = norm_place()
    own = norm_own.shape[1]
    spread = one_hot((own, LANES), lambda r, l: r + eighth * own, lambda r, l: l)
    lanes = dot(norm_own[...].astype(bf16), spread.astype(f32).astype(bf16)).astype(bf16)
    lift = one_hot((16, 4), lambda r, l: r, lambda r, l: l * 4 + quarter)
    tile = dot(lift.astype(f32).astype(bf16), lanes).astype(bf16)
    small[mine] = jnp.concatenate([sort_own[...].astype(bf16), tile], axis=0)
    steps = GatherSteps(proj, up, down, small, (send, recv))

    def arrived():
        pieces = small[...].reshape(-1, 32, LANES)
        sort_ref[...] = pieces[:, :16].reshape(sort_ref.shape)
        tile = jnp.sum(pieces[:, 16:].astype(f32), axis=0)
        norms_ref[...] = jnp.concatenate(
            [
                jnp.concatenate([tile[4 * i + q : 4 * i + q + 1] for q in range(4)], axis=1)
                for i in range(4)
            ],
            axis=0,
        )

    steps.arrived = arrived

    def columns_of(columns):
        return proj[:, :, :, :, :, columns].reshape(x_ref.shape[1], -1)

    front_steps(steps, columns_of, lengths_ref, norms_ref, x_ref, sort_ref, *rest)


def front_plain_kernel(lengths_ref, norms_ref, x_ref, proj_ref, sort_ref, *rest):
    front_steps(
        Quiet(), lambda columns: proj_ref[:, columns], lengths_ref, norms_ref, x_ref, sort_ref, *rest
    )


def front_steps(
    steps, proj_columns, lengths_ref, norms_ref, x_ref, sort_ref,
    normed_hbm, qkv_hbm, skv_hbm, tkv_hbm, means_ref, states_ref,
    normed_s, stage, matrix, pair_buf, query_buf, low_buf, flip_buf,
    copy_sem, pair_sem, query_sem, low_sem, flip_sem,
):
    seq, width = x_ref.shape
    tiles = seq // TILE
    blocks = seq // BLOCK
    per_tile = TILE // BLOCK
    chunks = 2 * width // LANES
    ends = doc_ends(lengths_ref)
    def centre_step(k, carry):
        rows = pl.ds(pl.multiple_of(k * TILE, TILE), TILE)
        xhat, unused = center_scale(x_ref[rows, :].astype(f32))
        stage[pl.ds(k * (TILE // blocks), TILE // blocks), :, :width] = xhat.reshape(
            TILE // blocks, blocks, width
        )
        return carry

    for quarter in range(4):
        lax.fori_loop(quarter * tiles // 4, (quarter + 1) * tiles // 4, centre_step, 0)
        steps.centred(quarter)
    steps.arrived()
    gain = norms_ref[0:1, :].astype(f32)
    shift = norms_ref[1:2, :].astype(f32)

    def norm_step(k, carry):
        rows = pl.ds(pl.multiple_of(k * TILE, TILE), TILE)
        xhat = stage[pl.ds(k * (TILE // blocks), TILE // blocks), :, :width].reshape(TILE, width)
        normed = (xhat * gain + shift).astype(bf16)
        normed_s[rows, :] = normed
        sums = jnp.sum(normed.astype(f32).reshape(per_tile, BLOCK, width), axis=1)
        means_ref[pl.ds(pl.multiple_of(k * per_tile, per_tile), per_tile), :] = (
            sums * (1.0 / BLOCK)
        ).astype(bf16)
        return carry

    lax.fori_loop(0, tiles // 2, norm_step, 0)
    steps.half_normed()
    lax.fori_loop(tiles // 2, tiles, norm_step, 0)
    normed_copy = pltpu.make_async_copy(normed_s, normed_hbm, copy_sem)
    normed_copy.start()

    logits = dot(means_ref[...], sort_ref[...])
    first_i = segments_of(lax.broadcasted_iota(jnp.int32, (blocks, blocks), 0) * BLOCK, ends)
    first_j = segments_of(lax.broadcasted_iota(jnp.int32, (blocks, blocks), 1) * BLOCK, ends)
    logits = jnp.where(first_i != first_j, logits - mask_penalty, logits)

    def pair_copy(k, slot):
        place = (pl.ds(pl.multiple_of(k * TILE, TILE), TILE), pl.ds(width, 2 * width))
        return pltpu.make_async_copy(pair_buf.at[slot], qkv_hbm.at[place], pair_sem.at[slot])

    def query_copy(k, slot):
        place = (pl.ds(pl.multiple_of(k * TILE, TILE), TILE), pl.ds(0, width))
        return pltpu.make_async_copy(query_buf.at[slot], qkv_hbm.at[place], query_sem.at[slot])

    def project_step(k, logits):
        rows = pl.ds(pl.multiple_of(k * TILE, TILE), TILE)
        slot = lax.rem(k, 2)

        @pl.when(k >= 2)
        def _():
            pair_copy(k - 2, slot).wait()

        steps.project(k)
        logits = logits - log_sum_exp(logits, 1)
        states_ref[2 * k] = jnp.exp(logits)
        logits = logits - log_sum_exp(logits, 0)
        states_ref[2 * k + 1] = jnp.exp(logits)
        normed = normed_s[rows, :]
        product = dot(normed, proj_columns(slice(width, 3 * width))).astype(bf16)
        pair_buf[slot] = product
        spread_tokens(stage, matrix[...], k, product)
        pair_copy(k, slot).start()
        return logits

    assert tiles == SINK_ITERS == BLOCK // flip_buf.shape[0]
    steps.before_project()
    matrix[...] = regroup_matrix(False)
    lax.fori_loop(0, tiles, project_step, logits)
    permute = states_ref[2 * SINK_ITERS - 1].astype(bf16)

    def flip_copy(t, slot):
        return pltpu.make_async_copy(flip_buf.at[slot], tkv_hbm.at[t], flip_sem.at[slot])

    def sort_step(i, carry):
        group = flip_buf.shape[0]
        steps.sort(i)
        rows = pl.ds(pl.multiple_of(i * TILE, TILE), TILE)
        slot = lax.rem(i, 2)

        @pl.when(i >= 2)
        def _():
            query_copy(i - 2, slot).wait()

        query_buf[slot] = dot(normed_s[rows, :], proj_columns(slice(0, width))).astype(bf16)
        query_copy(i, slot).start()

        @pl.when(i >= 1)
        def _():
            for u in range(group):
                flip_copy((i - 1) * group + u, u).wait()

        loaded = []
        for u in range(group):
            t = i * group + u
            loaded.append(stage[t].astype(bf16))
        for u in range(group):
            t = i * group + u
            flip_buf[u] = loaded[u].astype(f32).T.astype(bf16)
            flip_copy(t, u).start()
            stage[t] = dot(permute, loaded[u])
        return carry

    group = flip_buf.shape[0]
    lax.fori_loop(0, BLOCK // group, sort_step, 0)

    def low_copy(k, slot):
        rows = pl.ds(pl.multiple_of(k * TILE, TILE), TILE)
        return pltpu.make_async_copy(low_buf.at[slot], skv_hbm.at[rows, :], low_sem.at[slot])

    def low_step(k, carry):
        rows = pl.ds(pl.multiple_of(k * TILE, TILE), TILE)
        slot = lax.rem(k, 2)

        @pl.when(k >= 2)
        def _():
            low_copy(k - 2, slot).wait()

        steps.low(k)
        low_buf[slot] = collect_tokens(stage, matrix[...], k, TILE).astype(bf16)
        low_copy(k, slot).start()
        return carry

    matrix[...] = regroup_matrix(True)
    lax.fori_loop(0, tiles, low_step, 0)
    for u in range(group):
        flip_copy(BLOCK - group + u, u).wait()
    for k in (tiles - 2, tiles - 1):
        pair_copy(k, k % 2).wait()
        query_copy(k, k % 2).wait()
        low_copy(k, k % 2).wait()
    normed_copy.wait()
    steps.end()


def front_shapes(seq, width):
    blocks = seq // BLOCK
    hbm = pl.BlockSpec(memory_space=pl.ANY)
    vmem = pl.BlockSpec(memory_space=pltpu.VMEM)
    shapes = (
        jax.ShapeDtypeStruct((seq, width), bf16),
        jax.ShapeDtypeStruct((seq, 3 * width), bf16),
        jax.ShapeDtypeStruct((seq, 2 * width), bf16),
        jax.ShapeDtypeStruct((BLOCK, 2 * width, blocks), bf16),
        jax.ShapeDtypeStruct((blocks, width), bf16),
        jax.ShapeDtypeStruct((2 * SINK_ITERS, blocks, blocks), f32),
    )
    scratch = [
            pltpu.VMEM((seq, width), bf16),
            pltpu.VMEM((BLOCK, blocks, 2 * width), f32),
            pltpu.VMEM((GROUP, GROUP), bf16),
            pltpu.VMEM((2, TILE, 2 * width), bf16),
            pltpu.VMEM((2, TILE, width), bf16),
            pltpu.VMEM((2, TILE, 2 * width), bf16),
            pltpu.VMEM((4, 2 * width, blocks), bf16),
            pltpu.SemaphoreType.DMA,
            pltpu.SemaphoreType.DMA((2,)),
            pltpu.SemaphoreType.DMA((2,)),
            pltpu.SemaphoreType.DMA((2,)),
            pltpu.SemaphoreType.DMA((8,)),
    ]
    return shapes, [hbm, hbm, hbm, hbm, vmem, vmem], scratch


def front_plain(lengths, x, *shards):
    proj, up, down, sort, norms = gather_plain(*shards)
    shapes, specs, scratch = front_shapes(*x.shape)
    vmem = pl.BlockSpec(memory_space=pltpu.VMEM)
    results = pl.pallas_call(
        front_plain_kernel,
        out_shape=shapes,
        in_specs=[pl.BlockSpec(memory_space=pltpu.SMEM), vmem, vmem, vmem, vmem],
        out_specs=specs,
        scratch_shapes=scratch,
        compiler_params=pltpu.CompilerParams(vmem_limit_bytes=VMEM_LIMIT),
        name="front",
    )(lengths, norms, x, proj, sort)
    return (proj, up, down, sort, norms, *results)


def front_near(lengths, x, proj, up, down, sort, norm):
    seq, width = x.shape
    shapes, specs, scratch = front_shapes(seq, width)
    vmem = pl.BlockSpec(memory_space=pltpu.VMEM)
    fulls = [jax.ShapeDtypeStruct(SPLIT + own.shape, bf16) for own in (proj, up, down)]
    fulls += [jax.ShapeDtypeStruct((32 * sort.shape[0], LANES), bf16)]
    fulls += [jax.ShapeDtypeStruct((4, width), f32)]
    scratch = scratch + [pltpu.VMEM(SPLIT + (32, LANES), bf16)]
    scratch += [pltpu.SemaphoreType.DMA((GATHERS * COPIES,))] * 2
    results = pl.pallas_call(
        front_near_kernel,
        out_shape=tuple(fulls) + shapes,
        in_specs=[pl.BlockSpec(memory_space=pltpu.SMEM)] + [vmem] * 6,
        out_specs=[vmem] * 5 + specs,
        scratch_shapes=scratch,
        compiler_params=pltpu.CompilerParams(
            collective_id=0, has_side_effects=True, vmem_limit_bytes=VMEM_LIMIT
        ),
        name="front",
    )(lengths, x, proj, up, down, sort, norm)
    return tuple(full.reshape(-1, full.shape[-1]) for full in results[:3]) + tuple(results[3:])


def layer_norm_back(grad, gain, xhat, inverse):
    scaled = grad * gain
    mean_one = jnp.mean(scaled, axis=-1, keepdims=True)
    mean_two = jnp.mean(scaled * xhat, axis=-1, keepdims=True)
    return (scaled - mean_one - xhat * mean_two) * inverse


def middle_kernel(
    lengths_ref, norms_ref, x_ref, cot_ref, qkv_ref, skv_ref, out_proj_ref, up_hbm, down_hbm,
    y_ref, hidden_grad_ref, gq_ref, gkv_ref, gskv_ref, gup_ref, gdown_ref, gout_ref, gnorm_ref,
    gup, gdown, gout, probs_s, context_s, gcontext_s, gq_s, gkv_s, gskv_s, grads_s,
    up_ref, down_ref, weight_sem,
):
    step = pl.program_id(0)
    tile, width = x_ref.shape
    hidden_units = up_ref.shape[1]
    pairs = tile // (2 * BLOCK)
    head_pairs = width // LANES
    scale = HD ** (-0.5)
    ends = doc_ends(lengths_ref)

    weight_copies = [
        pltpu.make_async_copy(source, target, weight_sem.at[i])
        for i, (source, target) in enumerate(((up_hbm, up_ref), (down_hbm, down_ref)))
    ]

    @pl.when(step == 0)
    def _():
        start_all(weight_copies)
        gup[...] = jnp.zeros_like(gup)
        gdown[...] = jnp.zeros_like(gdown)
        gout[...] = jnp.zeros_like(gout)
        gnorm_ref[...] = jnp.zeros_like(gnorm_ref)

    lane = lax.broadcasted_iota(jnp.int32, (1, LANES), 1)
    low_head = lane < HD
    low_block = lax.rem(lane, 2 * BLOCK) < BLOCK
    head_one = low_head.astype(f32).astype(bf16)
    head_two = (1.0 - low_head.astype(f32)).astype(bf16)
    block_one = low_block.astype(f32).astype(bf16)
    block_two = (1.0 - low_block.astype(f32)).astype(bf16)

    def two_heads(part):
        return jnp.concatenate(
            [part * head_one, part * head_two], axis=0
        )

    def two_blocks(part):
        return jnp.concatenate(
            [part * block_one, part * block_two], axis=0
        )

    def stack_keys(own, far):
        return jnp.concatenate(
            [own[:BLOCK], far[:BLOCK], own[BLOCK:], far[BLOCK:]], axis=0
        )

    def pick_block(full):
        return jnp.where(low_block, full[: 2 * BLOCK], full[2 * BLOCK :])

    def pick_head(full):
        return jnp.where(low_head, full[: 2 * BLOCK], full[2 * BLOCK :])

    def attend(p, carry):
        rows = pl.ds(pl.multiple_of(p * 2 * BLOCK, 2 * BLOCK), 2 * BLOCK)
        base = step * tile + p * 2 * BLOCK
        query_seg = segments_of(base + lax.rem(lane, 2 * BLOCK), ends)
        key_place = (
            base
            + jnp.where(low_block, 0, BLOCK)
            + lax.broadcasted_iota(jnp.int32, (BLOCK, LANES), 0)
        )
        same = segments_of(key_place, ends) == query_seg
        for hp in range(head_pairs):
            cols = slice(hp * LANES, (hp + 1) * LANES)
            key_cols = slice(width + hp * LANES, width + (hp + 1) * LANES)
            value_cols = slice(2 * width + hp * LANES, 2 * width + (hp + 1) * LANES)
            queries = two_heads(qkv_ref[rows, cols])
            keys = stack_keys(qkv_ref[rows, key_cols], skv_ref[rows, cols])
            values = stack_keys(qkv_ref[rows, value_cols], skv_ref[rows, key_cols])
            scores = pick_block(dot(keys, queries.astype(f32).T.astype(bf16))) * scale
            scores = jnp.concatenate(
                [jnp.where(same, scores[:BLOCK], score_floor), scores[BLOCK:]], axis=0
            )
            exps = jnp.exp(scores - jnp.max(scores, axis=0, keepdims=True))
            probs = (exps / jnp.sum(exps, axis=0, keepdims=True)).astype(bf16)
            probs_s[p * head_pairs + hp] = probs
            context_s[rows, cols] = pick_head(dot_tn(two_blocks(probs), values)).astype(bf16)
        return carry

    lax.fori_loop(0, pairs, attend, 0, unroll=8)

    pl.when(step == 0)(lambda: wait_all(weight_copies))
    inputs = x_ref[...].astype(f32)
    context = context_s[...]
    hidden = inputs + dot(context, out_proj_ref[...])
    xhat_two, inverse_two = center_scale(hidden)
    gain_two = norms_ref[2:3, :].astype(f32)
    normed_two = (xhat_two * gain_two + norms_ref[3:4, :].astype(f32)).astype(bf16)
    normed_two_t = normed_two.T
    cot = cot_ref[...]
    total_out = hidden
    grad_normed_two = None
    root = 0.7978845608028654
    for c in range(hidden_units // TILE):
        cols = slice(c * TILE, (c + 1) * TILE)
        pre = dot(normed_two, up_ref[:, cols])
        grad_act = dot_nt(cot, down_ref[cols, :])
        square = pre * pre
        half_tanh = 0.5 + 0.5 * jnp.tanh(pre * (root + (root * 0.044715) * square))
        act = pre * half_tanh
        slope = half_tanh + act * (1.0 - half_tanh) * (
            2.0 * root + (6.0 * root * 0.044715) * square
        )
        act = act.astype(bf16)
        grad_pre = (grad_act * slope).astype(bf16)
        total_out = total_out + dot(act, down_ref[cols, :])
        back = dot_nt(grad_pre, up_ref[:, cols])
        grad_normed_two = back if grad_normed_two is None else grad_normed_two + back
        gup[:, cols] += dot(normed_two_t, grad_pre)
        gdown[cols, :] += dot_tn(act, cot)
    y_ref[...] = total_out.astype(bf16)
    gnorm_ref[0:1, :] += jnp.sum(grad_normed_two * xhat_two, axis=0, keepdims=True)
    gnorm_ref[1:2, :] += jnp.sum(grad_normed_two, axis=0, keepdims=True)
    hidden_grad = cot.astype(f32) + layer_norm_back(
        grad_normed_two, gain_two, xhat_two, inverse_two
    )
    grad_attn = hidden_grad.astype(bf16)
    hidden_grad_ref[...] = grad_attn
    gout[...] += dot_tn(context, grad_attn)
    gcontext_s[...] = dot_nt(grad_attn, out_proj_ref[...]).astype(bf16)

    def attend_back(p, carry):
        rows = pl.ds(pl.multiple_of(p * 2 * BLOCK, 2 * BLOCK), 2 * BLOCK)
        for hp in range(head_pairs):
            cols = slice(hp * LANES, (hp + 1) * LANES)
            key_cols = slice(width + hp * LANES, width + (hp + 1) * LANES)
            value_cols = slice(2 * width + hp * LANES, 2 * width + (hp + 1) * LANES)
            values = stack_keys(qkv_ref[rows, value_cols], skv_ref[rows, key_cols])
            gcontext = two_heads(gcontext_s[rows, cols])
            wide = probs_s[p * head_pairs + hp].astype(f32)
            grad_probs = pick_block(dot(values, gcontext.astype(f32).T.astype(bf16)))
            weighted = wide * grad_probs
            grad_scores = weighted - wide * jnp.sum(weighted, axis=0, keepdims=True)
            grad_scores = (grad_scores * scale).astype(bf16)
            grads_s[p * head_pairs + hp] = grad_scores
        return carry

    lax.fori_loop(0, pairs, attend_back, 0, unroll=8)

    def attend_last(p, carry):
        rows = pl.ds(pl.multiple_of(p * 2 * BLOCK, 2 * BLOCK), 2 * BLOCK)
        for hp in range(head_pairs):
            cols = slice(hp * LANES, (hp + 1) * LANES)
            key_cols = slice(width + hp * LANES, width + (hp + 1) * LANES)
            value_cols = slice(2 * width + hp * LANES, 2 * width + (hp + 1) * LANES)
            keys = stack_keys(qkv_ref[rows, key_cols], skv_ref[rows, cols])
            gq_s[rows, cols] = pick_head(dot_tn(two_blocks(grads_s[p * head_pairs + hp]), keys)).astype(bf16)
            gkeys = dot(two_blocks(grads_s[p * head_pairs + hp]), two_heads(qkv_ref[rows, cols])).astype(bf16)
            gvalues = dot(two_blocks(probs_s[p * head_pairs + hp]), two_heads(gcontext_s[rows, cols])).astype(bf16)
            for grads, where in ((gkeys, cols), (gvalues, key_cols)):
                gkv_s[rows, where] = jnp.concatenate(
                    [grads[:BLOCK], grads[2 * BLOCK : 3 * BLOCK]], axis=0
                )
                gskv_s[rows, where] = jnp.concatenate(
                    [grads[BLOCK : 2 * BLOCK], grads[3 * BLOCK :]], axis=0
                )
        return carry

    lax.fori_loop(0, pairs, attend_last, 0, unroll=8)
    gq_ref[...] = gq_s[...]
    gkv_ref[...] = gkv_s[...]
    gskv_ref[...] = gskv_s[...]

    @pl.when(step == pl.num_programs(0) - 1)
    def _():
        gup_ref[...] = gup[...].astype(bf16)
        gdown_ref[...] = gdown[...].astype(bf16)
        gout_ref[...] = gout[...].astype(bf16)


def middle(lengths, norms, x, cot, qkv, skv, proj, up, down):
    seq, width = x.shape
    hidden_units = up.shape[1]
    tiles = seq // TILE

    def rows(columns):
        return pl.BlockSpec((TILE, columns), lambda i: (i, 0))

    def fixed(shape, index=(0, 0)):
        return pl.BlockSpec(shape, lambda i: index, pipeline_mode=pl.Buffered(1))

    return pl.pallas_call(
        middle_kernel,
        grid=(tiles,),
        out_shape=(
            jax.ShapeDtypeStruct((seq, width), bf16),
            jax.ShapeDtypeStruct((seq, width), bf16),
            jax.ShapeDtypeStruct((seq, width), bf16),
            jax.ShapeDtypeStruct((seq, 2 * width), bf16),
            jax.ShapeDtypeStruct((seq, 2 * width), bf16),
            jax.ShapeDtypeStruct((width, hidden_units), bf16),
            jax.ShapeDtypeStruct((hidden_units, width), bf16),
            jax.ShapeDtypeStruct((width, width), bf16),
            jax.ShapeDtypeStruct((2, width), f32),
        ),
        in_specs=[
            pl.BlockSpec(memory_space=pltpu.SMEM),
            fixed(norms.shape),
            rows(width),
            rows(width),
            rows(3 * width),
            rows(2 * width),
            fixed((width, width), (0, 3)),
            pl.BlockSpec(memory_space=pl.ANY),
            pl.BlockSpec(memory_space=pl.ANY),
        ],
        out_specs=[
            rows(width),
            rows(width),
            rows(width),
            rows(2 * width),
            rows(2 * width),
            fixed((width, hidden_units)),
            fixed((hidden_units, width)),
            fixed((width, width)),
            fixed((2, width)),
        ],
        scratch_shapes=[
            pltpu.VMEM((width, hidden_units), f32),
            pltpu.VMEM((hidden_units, width), f32),
            pltpu.VMEM((width, width), f32),
            pltpu.VMEM((TILE // (2 * BLOCK) * (width // LANES), 2 * BLOCK, LANES), bf16),
            pltpu.VMEM((TILE, width), bf16),
            pltpu.VMEM((TILE, width), bf16),pltpu.VMEM((TILE, width), bf16),pltpu.VMEM((TILE, 2*width), bf16),pltpu.VMEM((TILE, 2*width), bf16),
            pltpu.VMEM((TILE // (2 * BLOCK) * (width // LANES), 2 * BLOCK, LANES), bf16),
            pltpu.VMEM(up.shape, bf16),
            pltpu.VMEM(down.shape, bf16),
            pltpu.SemaphoreType.DMA((2,)),
        ],
        compiler_params=pltpu.CompilerParams(vmem_limit_bytes=VMEM_LIMIT),
        name="middle",
    )(lengths, norms, x, cot, qkv, skv, proj, up, down)


def add_low(*parts):
    total = parts[0].astype(f32)
    for part in parts[1:]:
        total = total + part.astype(f32)
    return total


class Reduce:
    def __init__(self, part, total, columns, got_c, got_xy, got_z, sems, base):
        self.part, self.total, self.columns = part, total, columns
        self.whole = (slice(None), columns)
        self.got_c, self.got_xy, self.got_z = got_c, got_xy, got_z
        self.sems, self.base = sems, base

    def copies(self, step):
        z, x, y, c = coordinates()
        every = slice(None)

        def one(source, target, index, device):
            return remote(source, target, self.sems, self.base + index, device)

        if step == 0:
            away = self.part.at[(every, every, every, 1 - c) + self.whole]
            return [one(away, self.got_c, 0, device_of(z, x, y, 1 - c))]
        if step == 1:
            return [
                one(self.got_c.at[(every,) + other], self.got_xy.at[k], 1 + k, device_of(z, *other, c))
                for k, other in enumerate(xy_others(x, y))
            ]
        return [
            one(self.got_c.at[other, x, y], self.got_z.at[k], 4 + k, device_of(other, x, y, c))
            for k, other in enumerate(z_others(z))
        ]

    def start(self, step):
        start_all(self.copies(step))

    def turn(self, step):
        wait_all(self.copies(step))
        self.add(step)
        if step < 2:
            self.start(step + 1)

    def add(self, step):
        z, x, y, c = coordinates()
        if step == 2:
            self.total[:, self.columns] = add_low(
                self.got_c[z, x, y], *[self.got_z[k] for k in range(3)]
            )
            return

        def line(i, carry):
            if step == 0:
                for j in range(2):
                    for k in range(2):
                        self.got_c[i, j, k] = add_low(
                            self.part[(i, j, k, c) + self.whole], self.got_c[i, j, k]
                        ).astype(bf16)
            else:
                self.got_c[i, x, y] = add_low(
                    self.got_c[i, x, y], *[self.got_xy[k, i] for k in range(3)]
                ).astype(bf16)
            return carry

        lax.fori_loop(0, 4, line, 0)


def reduce_scratch(rows, columns):
    shapes = ((4, 2, 2, rows, columns), (3, 4, rows, columns), (3, rows, columns))
    return [pltpu.VMEM(shape, bf16) for shape in shapes]


class ReduceSteps:
    def __init__(self, plans):
        self.up, self.down, self.out, self.query = plans

    def begin(self):
        pass

    def send(self):
        await_neighbours()
        self.up.start(0)
        self.down.start(0)
        self.out.start(0)

    def during_query(self, k):
        pl.when(k == 1)(self.send)
        self.when(k, 6, self.up, 0)

    def queried(self):
        self.query.start(0)

    def load(self, k):
        self.when(k, 1, self.down, 0)
        self.when(k, 3, self.out, 0)
        self.when(k, 6, self.query, 0)

    def loaded(self):
        pass

    def sort(self, i):
        self.when(i, 7, self.up, 1)

    def swept(self):
        pass

    def weights(self, k):
        self.when(k, 2, self.down, 1)
        self.when(k, 4, self.out, 1)
        self.when(k, 5, self.query, 1)
        self.when(k, 6, self.up, 2)

    def end(self):
        pass

    def inputs(self, k, pair):
        self.when(k, 1, self.down, 2)
        self.when(k, 2, pair, 0)
        self.when(k, 3, self.out, 2)
        self.when(k, 5, self.query, 2)

    def when(self, k, place, plan, step):
        pl.when(k == place)(functools.partial(plan.turn, step))


def norm_rows(grads):
    rows = []
    for grad in grads:
        for i in range(grad.shape[0]):
            for q in range(grad.shape[1] // LANES):
                rows.append(grad[i : i + 1, q * LANES : (q + 1) * LANES])
    return jnp.concatenate(rows, axis=0)


def back_near_kernel(*refs):
    ins, refs = refs[:8], refs[8:]
    (gout, gup, gdown, gtwo_ref, norms_ref, proj_ref, x_hbm), refs = refs[:7], refs[7:]
    gx_hbm, refs = refs[0], refs[1:]
    (query_sum, pair_sum, out_sum, up_sum, down_sum, sort_sum, norm_sum), refs = refs[:7], refs[7:]
    work, refs = refs[:8], refs[8:]
    (gsum, gpair, gsort, gmeans, gquery, gone_ref, small, small_sum), refs = refs[:8], refs[8:]
    (send, recv), scratch = refs[:2], refs[2:]
    greet_neighbours()
    every = slice(None)
    places = (
        (gup, up_sum, every), (gdown, down_sum, every), (gout, out_sum, every),
        (gquery, query_sum, every), (gpair, pair_sum, every), (small, small_sum, every),
    )
    plans = [
        Reduce(*place, *scratch[3 * b : 3 * b + 3], (send, recv), COPIES * b)
        for b, place in enumerate(places)
    ]
    pair, small_plan = plans[4:]
    steps = ReduceSteps(plans[:4])
    back_steps(steps, *ins, gsum, gpair, gsort, gmeans, gquery, *work)
    pair.start(0)
    seq, width = x_hbm.shape
    gone_ref[...] = jnp.zeros_like(gone_ref)

    def input_step(x_ref, gq_ref, gx_ref):
        k = pl.program_id(0)
        steps.inputs(k, pair)
        part = TILE // BLOCK
        means = gmeans[pl.ds(pl.multiple_of(k * part, part), part), :]
        gkv = gsum[pl.ds(pl.multiple_of(k * TILE, TILE), TILE), :]
        input_tile(norms_ref, x_ref, gq_ref, gkv, means, proj_ref, gx_ref, gone_ref)

    def rows_of(columns):
        return pl.BlockSpec((TILE, columns), lambda i: (i, 0))

    pltpu.emit_pipeline(
        input_step,
        grid=(seq // TILE,),
        in_specs=[rows_of(width)] * 2,
        out_specs=[rows_of(width)],
    )(x_hbm, ins[6], gx_hbm)
    tile = norm_rows((gone_ref[...], gtwo_ref[...])).astype(bf16)
    small[:, :, :, :, :16] = gsort[...].astype(bf16).reshape(SPLIT + (width // 32, LANES))
    for i in range(4):
        for j in range(2):
            for k in range(2):
                for m in range(2):
                    small[i, j, k, m, 16:] = tile
    small_plan.start(0)
    small_plan.turn(0)
    pair.turn(1)
    small_plan.turn(1)
    small_plan.turn(2)
    pair.turn(2)
    sort_sum[...] = small_sum[:16, :]
    quarter, eighth = norm_place()
    own = norm_sum.shape[1]
    drop = one_hot((4, 16), lambda r, l: r * 4 + quarter, lambda r, l: l).astype(f32)
    pick = one_hot((LANES, own), lambda r, l: r, lambda r, l: l + eighth * own).astype(f32)

    def exact(left, right):
        return lax.dot_general(
            left, right, (((1,), (0,)), ((), ())),
            precision=lax.Precision.HIGHEST, preferred_element_type=f32,
        )

    norm_sum[...] = exact(exact(drop, small_sum[16:, :]), pick)


def back_plain_kernel(*refs):
    back_steps(Quiet(), *refs)


def back_steps(
    steps, gskv_hbm, tkv_hbm, states_ref, means_ref, sort_ref,
    normed_hbm, gq_hbm, gkv_hbm,
    gsum, gpair_ref, gsort_ref, gmeans, gquery_ref,
    stage, matrix, low_buf, flip_buf, gproj, gperm, low_sem, flip_sem,
):
    steps.begin()
    seq, width = normed_hbm.shape
    tiles = seq // TILE
    blocks = seq // BLOCK
    chunks = 2 * width // LANES
    per_tile = TILE // BLOCK

    def low_copy(k, slot):
        rows = pl.ds(pl.multiple_of(k * TILE, TILE), TILE)
        return pltpu.make_async_copy(gskv_hbm.at[rows, :], low_buf.at[slot], low_sem.at[slot])

    group = flip_buf.shape[0] // 2

    def flip_copy(t, slot):
        return pltpu.make_async_copy(tkv_hbm.at[t], flip_buf.at[slot], flip_sem.at[slot])

    low_copy(0, 0).start()
    low_copy(1, 1).start()
    for u in range(group):
        flip_copy(u, u).start()

    def load_step(k, carry):
        rows = pl.ds(pl.multiple_of(k * TILE, TILE), TILE)
        slot = lax.rem(k, 2)
        low_copy(k, slot).wait()
        steps.load(k)
        spread_tokens(stage, matrix[...], k, low_buf[slot])

        @pl.when(k + 2 < tiles)
        def _():
            low_copy(k + 2, slot).start()

        return carry

    def rows_of(columns):
        return pl.BlockSpec((TILE, columns), lambda i: (i, 0))

    gproj[...] = jnp.zeros_like(gproj)

    def query_step(normed_ref, gq_ref):
        steps.during_query(pl.program_id(0))
        gproj[:, :width] += dot_tn(normed_ref[...], gq_ref[...])

    pltpu.emit_pipeline(query_step, grid=(tiles,), in_specs=[rows_of(width)] * 2)(
        normed_hbm, gq_hbm
    )
    gquery_ref[...] = gproj[:, :width].astype(bf16).reshape(gquery_ref.shape)
    steps.queried()
    matrix[...] = regroup_matrix(False)
    lax.fori_loop(0, tiles, load_step, 0)
    matrix[...] = regroup_matrix(True)
    steps.loaded()

    final = states_ref[2 * SINK_ITERS - 1]
    permute_t = final.T.astype(bf16)
    gperm[...] = jnp.zeros_like(gperm)

    def sort_step(i, carry):
        side = lax.rem(i, 2) * group
        steps.sort(i)

        @pl.when(i + 1 < BLOCK // group)
        def _():
            for u in range(group):
                flip_copy((i + 1) * group + u, group - side + u).start()

        for u in range(group):
            flip_copy(i * group + u, side + u).wait()
        loaded = []
        for u in range(group):
            t = i * group + u
            loaded.append(stage[t].astype(bf16))
        total = gperm[...]
        for u in range(group):
            t = i * group + u
            total = total + dot(loaded[u], flip_buf[side + u])
            stage[t] = dot(permute_t, loaded[u])
        gperm[...] = total
        return carry

    lax.fori_loop(0, BLOCK // group, sort_step, 0)

    grad = gperm[...] * final
    for sweep in reversed(range(SINK_ITERS)):
        grad = grad - states_ref[2 * sweep + 1] * jnp.sum(grad, axis=0, keepdims=True)
        grad = grad - states_ref[2 * sweep] * jnp.sum(grad, axis=1, keepdims=True)
    grad = grad.astype(bf16)
    gsort_ref[...] = dot_tn(means_ref[...], grad).astype(gsort_ref.dtype)
    gmeans[...] = dot_nt(grad, sort_ref[...]) * (1.0 / BLOCK)
    steps.swept()

    def weight_step(normed_ref, gkv_ref):
        k = pl.program_id(0)
        steps.weights(k)
        gkv = (gkv_ref[...].astype(f32) + collect_tokens(stage, matrix[...], k, TILE)).astype(bf16)
        gsum[pl.ds(pl.multiple_of(k * TILE, TILE), TILE), :] = gkv
        gproj[:, width:] += dot_tn(normed_ref[...], gkv)

    pltpu.emit_pipeline(
        weight_step,
        grid=(tiles,),
        in_specs=[rows_of(width), rows_of(2 * width)],
    )(normed_hbm, gkv_hbm)
    gpair_ref[...] = gproj[:, width:].astype(bf16).reshape(gpair_ref.shape)
    steps.end()


def back_scratch(seq, width):
    blocks = seq // BLOCK
    return [
            pltpu.VMEM((BLOCK, blocks, 2 * width), f32),
            pltpu.VMEM((GROUP, GROUP), bf16),
            pltpu.VMEM((2, TILE, 2 * width), bf16),
            pltpu.VMEM((8, 2 * width, blocks), bf16),
            pltpu.VMEM((width, 3 * width), f32),
            pltpu.VMEM((blocks, blocks), f32),
            pltpu.SemaphoreType.DMA((2,)),
            pltpu.SemaphoreType.DMA((8,)),
    ]


def back_shapes(seq, width):
    hbm = pl.BlockSpec(memory_space=pl.ANY)
    vmem = pl.BlockSpec(memory_space=pltpu.VMEM)
    blocks = seq // BLOCK
    shapes = (
        jax.ShapeDtypeStruct((seq, 2 * width), bf16),
        jax.ShapeDtypeStruct((width, 2 * width), bf16),
        jax.ShapeDtypeStruct((width, blocks), f32),
        jax.ShapeDtypeStruct((blocks, width), f32),
    )
    return shapes, [hbm, hbm, vmem, vmem, vmem, hbm, hbm, hbm], [vmem, vmem, vmem, vmem]


def back_plain(seq, width, ins, gout, gup, gdown):
    shapes, in_specs, out_specs = back_shapes(seq, width)
    gsum, gpair, gsort, gmeans, gquery = pl.pallas_call(
        back_plain_kernel,
        out_shape=shapes + (jax.ShapeDtypeStruct((width, width), bf16),),
        in_specs=in_specs,
        out_specs=out_specs + [pl.BlockSpec(memory_space=pltpu.VMEM)],
        scratch_shapes=back_scratch(seq, width),
        compiler_params=pltpu.CompilerParams(vmem_limit_bytes=VMEM_LIMIT),
        name="back",
    )(*ins)
    return gsum, gpair, gsort, gmeans, gquery, gout, gup, gdown


def split_shards(grad):
    return grad.reshape(SPLIT + (grad.shape[0] // 32, grad.shape[1]))


def back_near(seq, width, ins, gout, gup, gdown, gtwo, norms, proj, x):
    shapes, in_specs, unused = back_shapes(seq, width)
    hbm = pl.BlockSpec(memory_space=pl.ANY)
    vmem = pl.BlockSpec(memory_space=pltpu.VMEM)
    gout, gup, gdown = split_shards(gout), split_shards(gup), split_shards(gdown)
    blocks = seq // BLOCK
    query, pair, small = (width // 32, width), (width // 32, 2 * width), (32, LANES)
    scratch = back_scratch(seq, width) + [
        pltpu.VMEM((seq, 2 * width), bf16),
        pltpu.VMEM(SPLIT + pair, bf16),
        pltpu.VMEM((width, blocks), f32),
        pltpu.VMEM((blocks, width), f32),
        pltpu.VMEM(SPLIT + query, bf16),
        pltpu.VMEM((2, width), f32),
        pltpu.VMEM(SPLIT + small, bf16),
        pltpu.VMEM(small, f32),
    ]
    scratch += [pltpu.SemaphoreType.DMA((6 * COPIES,))] * 2
    for shape in (gup.shape[-2:], gdown.shape[-2:], gout.shape[-2:], query, pair, small):
        scratch += reduce_scratch(*shape)
    sums = [query, pair, gout.shape[-2:], gup.shape[-2:], gdown.shape[-2:]]
    sums += [(width // 32, blocks), (4, width // 32)]
    gx, *totals = pl.pallas_call(
        back_near_kernel,
        out_shape=(jax.ShapeDtypeStruct((seq, width), bf16),)
        + tuple(jax.ShapeDtypeStruct(shape, f32) for shape in sums),
        in_specs=in_specs + [vmem] * 6 + [hbm],
        out_specs=[hbm] + [vmem] * 7,
        scratch_shapes=scratch,
        compiler_params=pltpu.CompilerParams(
            collective_id=1, has_side_effects=True, vmem_limit_bytes=VMEM_LIMIT
        ),
        name="back",
    )(*ins, gout, gup, gdown, gtwo, norms, proj, x)
    return gx, totals


def input_tile(
    norms_ref, x_ref, gq_ref, gkv, means, proj_ref, gx_ref, gnorm_ref
):
    tile, width = x_ref.shape
    grad_normed = dot_nt(gq_ref[...], proj_ref[:, :width])
    grad_normed = grad_normed + dot_nt(gkv, proj_ref[:, width : 3 * width])
    grad_normed = grad_normed + jnp.broadcast_to(
        means[:, None, :], (tile // BLOCK, BLOCK, width)
    ).reshape(tile, width)
    xhat, inverse = center_scale(x_ref[...].astype(f32))
    gnorm_ref[0:1, :] += jnp.sum(grad_normed * xhat, axis=0, keepdims=True)
    gnorm_ref[1:2, :] += jnp.sum(grad_normed, axis=0, keepdims=True)
    gain = norms_ref[0:1, :].astype(f32)
    gx_ref[...] = layer_norm_back(grad_normed, gain, xhat, inverse).astype(bf16)


def inputs_kernel(
    norms_ref, x_ref, gq_ref, gsum_ref, gmeans_ref, proj_ref, gx_ref, gnorm_ref
):
    @pl.when(pl.program_id(0) == 0)
    def _():
        gnorm_ref[...] = jnp.zeros_like(gnorm_ref)

    input_tile(
        norms_ref, x_ref, gq_ref, gsum_ref[...], gmeans_ref[...], proj_ref, gx_ref, gnorm_ref
    )


def inputs_back(norms, x, gq, gsum, gmeans, proj):
    seq, width = x.shape

    def rows(columns):
        return pl.BlockSpec((TILE, columns), lambda i: (i, 0))

    def fixed(shape):
        return pl.BlockSpec(shape, lambda i: (0, 0), pipeline_mode=pl.Buffered(1))

    return pl.pallas_call(
        inputs_kernel,
        grid=(seq // TILE,),
        out_shape=(
            jax.ShapeDtypeStruct((seq, width), bf16),
            jax.ShapeDtypeStruct((2, width), f32),
        ),
        in_specs=[
            fixed(norms.shape), rows(width), rows(width), rows(2 * width),
            pl.BlockSpec((TILE // BLOCK, width), lambda i: (i, 0)), fixed(proj.shape),
        ],
        out_specs=[rows(width), fixed((2, width))],
        compiler_params=pltpu.CompilerParams(vmem_limit_bytes=VMEM_LIMIT),
        name="inputs",
    )(norms, x, gq, gsum, gmeans, proj)


def last_plain(gpair, gsort, gone, gtwo, gquery, gout, gup, gdown):
    grads = (gquery, gpair, gout, gup, gdown, gsort, jnp.concatenate([gone, gtwo], axis=0))
    return tuple(
        lax.psum_scatter(
            grad.astype(f32), AXES, scatter_dimension=1 if b == 6 else 0, tiled=True
        )
        for b, grad in enumerate(grads)
    )


def adamw(master, first, second, grad, rate, decay):
    first_new = beta_first * first + (1.0 - beta_first) * grad
    second_new = beta_second * second + (1.0 - beta_second) * grad * grad
    first_hat = first_new / (1.0 - beta_first**STEP)
    second_hat = second_new / (1.0 - beta_second**STEP)
    master_new = master - rate * (first_hat / (jnp.sqrt(second_hat) + adam_eps) + decay * master)
    return (master_new, first_new, second_new)


RATES = (
    (rate_matrix, weight_decay), (rate_matrix, weight_decay), (rate_matrix, weight_decay),
    (rate_other, weight_decay), (rate_other, 0.0),
)


def update_kernel(*refs):
    parts, sums, states, gx_out, results = refs[:2], refs[2:9], refs[9:24], refs[24], refs[25:]

    def add_step(hidden_grad, norm_grad, target):
        pl.when(pl.program_id(0) == 1)(functools.partial(update_shards, sums, states, results))
        target[...] = hidden_grad[...].astype(f32) + norm_grad[...].astype(f32)

    rows = pl.BlockSpec((2 * TILE, gx_out.shape[1]), lambda i: (i, 0))
    pltpu.emit_pipeline(
        add_step, grid=(gx_out.shape[0] // (2 * TILE),), in_specs=[rows] * 2, out_specs=[rows]
    )(*parts, gx_out)


def update_shards(sums, states, results):
    sums = [jnp.concatenate([ref[...] for ref in sums[:3]], axis=1)] + [ref[...] for ref in sums[3:]]
    for b, (rate, decay) in enumerate(RATES):
        state = [ref[...] for ref in states[3 * b : 3 * b + 3]]
        for ref, value in zip(
            results[3 * b : 3 * b + 3], adamw(*state, sums[b], rate, decay)
        ):
            ref[...] = value


def update(hidden_grad, gx, sums, states):
    vmem = pl.BlockSpec(memory_space=pltpu.VMEM)
    hbm = pl.BlockSpec(memory_space=pl.ANY)
    return pl.pallas_call(
        update_kernel,
        out_shape=tuple(jax.ShapeDtypeStruct(array.shape, f32) for array in (gx, *states)),
        in_specs=[hbm] * 2 + [vmem] * 22,
        out_specs=[hbm] + [vmem] * 15,
        compiler_params=pltpu.CompilerParams(vmem_limit_bytes=VMEM_LIMIT),
        name="update",
    )(hidden_grad, gx, *sums, *states)


def gather_plain(proj, up, down, sort, norm):
    def gathered(shard, axis):
        return lax.all_gather(shard.astype(bf16), AXES, axis=axis, tiled=True)

    return (*(gathered(shard, 0) for shard in (proj, up, down, sort)), gathered(norm, 1))


def body(near, layer_input, doc_lengths, out_cotangent, *states):
    x = layer_input[0]
    cot = out_cotangent[0]
    proj, up, down, sort, norms, normed, qkv, skv, tkv, means, kept = (
        front_near if near else front_plain
    )(doc_lengths, x, *states[::3])
    y, hidden_grad, gq, gkv, gskv, gup, gdown, gout, gnorm_two = middle(
        doc_lengths, norms, x, cot, qkv, skv, proj, up, down
    )
    ins = (gskv, tkv, kept, means, sort, normed, gq, gkv)
    if near:
        gx, sums = back_near(
            *x.shape, ins, gout, gup, gdown, gnorm_two, norms, proj, x
        )
    else:
        gsum, gpair, gsort, gmeans, *done = back_plain(*x.shape, ins, gout, gup, gdown)
        gx, gnorm_one = inputs_back(norms, x, gq, gsum, gmeans, proj)
        sums = last_plain(gpair, gsort, gnorm_one, gnorm_two, *done)
    gx, *updates = update(hidden_grad, gx, sums, states)
    return (y[None], gx[None], *updates)


def solution(mesh):
    rows3, rows2, columns = P(AXES, None, None), P(AXES, None), P(None, AXES)
    near = (mesh.shape["dp"], mesh.shape["fsdp"]) == (8, 4)
    return jax.shard_map(
        functools.partial(body, near),
        mesh=mesh,
        in_specs=(rows3, rows2, rows3) + (rows2,) * 12 + (columns,) * 3,
        out_specs=(rows3, rows3) + (rows2,) * 12 + (columns,) * 3,
        check_vma=False,
    )
```
